32 devices in a mesh: sel: 8 (over z, y), mdl: 4 (over x, core).
Axes of the slice: x: 2, y: 2, z: 4, core: 2. Of those that a mesh axis runs over, the one named last changes fastest.
Arguments:
- patches: bfloat16 [6144, 1408], P('sel', 'mdl'), may hold values from -6 to 6
- text: bfloat16 [1024, 1024], P('sel', 'mdl'), may hold values from -64 to 64
- ref_proj: bfloat16 [1408, 1024], P(None, 'mdl'), may hold values from -0.15625 to 0.15625
- w_up: bfloat16 [1408, 6144], P(None, 'mdl'), may hold values from -0.15625 to 0.15625
- w_down: bfloat16 [6144, 1408], P('mdl'), may hold values from -0.078125 to 0.078125
- kept_index: int32 [512], P('sel'), may hold values from 0 to 127, as said below
- dest: int32 [512], P('sel'), may hold values from 0 to 7, as said below
- cotan: bfloat16 [3072, 1408], P('sel', 'mdl'), may hold values from -6 to 6
Outputs:
- ref_loss: float32 [1024], P('sel')
- learnability: float32 [512], P('sel')
- grad_up: float32 [1408, 6144], P('sel', 'mdl')
The draws below stay inside these ranges and needn't reach their ends.
Inputs may be any that keep to these rules, and one draw needn't show every extreme that they name: `kept_index`: the 64 entries of one scorer shard are distinct. `dest`: on each scorer shard at most 16 kept entries name the same learner shard; one learner shard is named by exactly 16 kept entries of every scorer shard.
All inputs are finite; a program needn't handle non-finite values.
Results may differ from the reference program's by a relative error of at most 0.019.
Values may be sent and summed in bfloat16 or wider, within the bound.
No kernel may reach another device: no remote copies, remote signals or barrier semaphores. Data moves between devices by JAX's collectives and lax.ppermute only.
A program may use at most 128 MiB of HBM per device.

```python
import math
import jax
import jax.numpy as jnp
from jax import lax

D = 1408
FF = 6144
EMB = 1024
P_SIZE = 6
EX_DEV = 128
K_DEV = 64
EX = 1024
KEPT = 512


def draw_text(key, part):
    key_base, key_scale = jax.random.split(key, 2)
    base_vals = jnp.clip(jax.random.normal(key_base, (EX, EMB), jnp.float32), -6.0, 6.0)
    row_scale = jnp.exp(jax.random.uniform(key_scale, (EX, 1), jnp.float32, 0.0, math.log(10.0)))
    return jnp.clip(base_vals * row_scale, -64.0, 64.0).astype(jnp.bfloat16)


def pick_rows(group_key):
    return jax.random.permutation(group_key, EX_DEV)[:K_DEV]


def draw_kept_index(key, part):
    n_groups = EX // EX_DEV
    group_keys = jax.random.split(key, n_groups)
    return jax.vmap(pick_rows)(group_keys).reshape(KEPT).astype(jnp.int32)


def draw_dest(key, part):
    n_groups = KEPT // K_DEV
    key_shift, key_source, key_place, key_label = jax.random.split(key, 4)
    half_count = n_groups // 2
    shifts = jax.random.randint(key_shift, (half_count,), 0, K_DEV + 1).astype(jnp.int32)
    shifts = shifts.at[0].set(K_DEV)
    dest_loads = jnp.stack([K_DEV + shifts, K_DEV - shifts], axis=1).reshape(n_groups)
    bounds = jnp.cumsum(dest_loads).astype(jnp.int32)
    slot_ids = jnp.arange(KEPT, dtype=jnp.int32)
    sorted_dest = jnp.sum((bounds[None, :] <= slot_ids[:, None]).astype(jnp.int32), axis=1)
    slot_table = sorted_dest.reshape(K_DEV, n_groups).T
    source_order = jax.random.permutation(key_source, n_groups)
    slot_table = slot_table[source_order]
    slot_table = jax.random.permutation(key_place, slot_table, axis=1, independent=True)
    relabel = jax.random.permutation(key_label, n_groups).astype(jnp.int32)
    return relabel[slot_table].reshape(KEPT).astype(jnp.int32)


def with_spikes(result, rng, source, target, parts, factor):
    def block_of(position):
        return (jnp.arange(result.shape[position]) // (result.shape[position] // parts)).reshape((-1,) + (1,) * (result.ndim - 1 - position))

    near = jax.random.permutation(rng, parts)[block_of(target)]
    second = (block_of(target) + parts // 2) % parts
    return jnp.where((block_of(source) == near) | (block_of(source) == second), factor * result, result)


def levels(rng, shape, pieces, smallest, high):
    factor_of, own = 1.0, jax.random.fold_in(rng, 6)
    for dim, parts in pieces:
        draws = jnp.exp(jax.random.uniform(jax.random.fold_in(own, dim), (parts,), jnp.float32, smallest / len(pieces), high / len(pieces)))
        factor_of = factor_of * jnp.repeat(draws, shape[dim] // parts).reshape([-1 if axis == dim else 1 for axis in range(len(shape))])
    return factor_of


def scatter_about(own_key, shape, width, limit, pieces=(), kind=jnp.bfloat16):
    values = width * jax.random.normal(own_key, shape, jnp.float32)
    if pieces:
        values = values * levels(own_key, shape, pieces, -0.22, 0.18)
    return jnp.clip(values, -limit, limit).astype(kind)


def gaussian_with(stream_key, dims, deviation, most, pieces, heavy, kind=jnp.bfloat16):
    values = deviation * jax.random.normal(stream_key, dims, jnp.float32)
    if pieces:
        values = values * levels(stream_key, dims, pieces, -0.22, 0.18)
    return jnp.clip(with_spikes(values, jax.random.fold_in(stream_key, 3), *heavy), -most, most).astype(kind)


def setup_inputs(seed: int = 0) -> dict:
    keys = jax.random.split(jax.random.key(seed), 9)
    patches = scatter_about(keys[0], (EX * P_SIZE, D), 1.0, 6.0, ((0, 8), (1, 4)))
    text = draw_text(jax.random.fold_in(keys[8], 71), 0)
    ref_proj = scatter_about(keys[2], (D, EMB), D ** -0.5, 0.15625, ((1, 4),))
    w_up = scatter_about(keys[3], (D, FF), D ** -0.5, 0.15625, ((1, 4),))
    w_down = scatter_about(keys[4], (FF, D), FF ** -0.5, 0.078125, ((0, 4),))
    kept_index = draw_kept_index(jax.random.fold_in(keys[8], 71), 0)
    dest = draw_dest(jax.random.fold_in(keys[8], 71), 0)
    cotan = gaussian_with(keys[7], (KEPT * P_SIZE, D), 1.0, 6.0, ((0, 8), (1, 4)), (0, 1, 8, 2.0))
    return {"patches": patches, "text": text, "ref_proj": ref_proj, "w_up": w_up, "w_down": w_down, "kept_index": kept_index, "dest": dest, "cotan": cotan}


logit_scale = 64.0
eps = 1e-06

def gelu_parts(pre_act):
    cumul = 0.5 * (1.0 + lax.erf(pre_act * 0.7071067811865476))
    density = jnp.exp(-0.5 * pre_act * pre_act) * 0.3989422804014327
    return (pre_act * cumul, cumul + pre_act * density)

def unit_rows(values):
    norm_sq = lax.optimization_barrier(jnp.sum(values * values, axis=1))
    return (values * lax.rsqrt(norm_sq + eps)[:, None]).astype(jnp.bfloat16)

def reference(patches, text, ref_proj, w_up, w_down, kept_index, dest, cotan):
    n_sel = EX // EX_DEV
    blocks = patches.reshape(EX, P_SIZE, D)
    pooled = lax.optimization_barrier(jnp.mean(blocks, axis=1, dtype=jnp.float32)).astype(jnp.bfloat16)
    img_hat = unit_rows(jnp.dot(pooled, ref_proj, preferred_element_type=jnp.float32))
    text_hat = unit_rows(text.astype(jnp.float32))

    def loss_block(args_pair):
        rows_hat, own_cols = args_pair
        scores = logit_scale * jnp.dot(rows_hat, text_hat.T, preferred_element_type=jnp.float32)
        log_total = jnp.log(lax.optimization_barrier(jnp.sum(jnp.exp(scores), axis=1)))
        own_score = jnp.take_along_axis(scores, own_cols[:, None], axis=1)[:, 0]
        return log_total - own_score
    ref_loss = lax.map(loss_block, (img_hat.reshape(n_sel, EX_DEV, EMB), jnp.arange(EX, dtype=jnp.int32).reshape(n_sel, EX_DEV))).reshape(EX)
    kept_global = jnp.arange(KEPT, dtype=jnp.int32) // K_DEV * EX_DEV + kept_index
    dest_counts = lax.optimization_barrier(jnp.sum((dest[:, None] == jnp.arange(n_sel, dtype=jnp.int32)[None, :]).astype(jnp.float32), axis=0))
    row_weight = 1.0 / dest_counts[dest]
    kept_tok = blocks[kept_global].reshape(n_sel, K_DEV, P_SIZE, D)
    kept_cot = cotan.reshape(n_sel, K_DEV, P_SIZE, D)

    def learner_step(total_up, inputs):
        block_tok, block_cot, block_weight = inputs
        tok_rows = block_tok.reshape(K_DEV * P_SIZE, D)
        weighted = (block_cot.astype(jnp.float32) * block_weight[:, None, None]).astype(jnp.bfloat16).reshape(K_DEV * P_SIZE, D)
        pre_act = jnp.dot(tok_rows, w_up, preferred_element_type=jnp.float32)
        activated, gelu_slope = gelu_parts(pre_act)
        hidden = activated.astype(jnp.bfloat16)
        mixed_part = jnp.dot(hidden, w_down, preferred_element_type=jnp.float32)
        outputs = tok_rows.astype(jnp.float32) + mixed_part
        pooled_rows = lax.optimization_barrier(jnp.mean(outputs.reshape(K_DEV, P_SIZE, D), axis=1)).astype(jnp.bfloat16)
        learn_hat = unit_rows(jnp.dot(pooled_rows, ref_proj, preferred_element_type=jnp.float32))
        grad_act = jnp.dot(weighted, w_down.T, preferred_element_type=jnp.float32)
        grad_pre = (grad_act * gelu_slope).astype(jnp.bfloat16)
        grad_up = total_up + jnp.dot(tok_rows.T, grad_pre, preferred_element_type=jnp.float32)
        return (grad_up, learn_hat)
    zeros_grad = jnp.zeros((D, FF), jnp.float32)
    grad_up, learn_hat = lax.scan(learner_step, zeros_grad, (kept_tok, kept_cot, row_weight.reshape(n_sel, K_DEV)))
    learner_loss = lax.map(loss_block, (learn_hat, kept_global.reshape(n_sel, K_DEV))).reshape(KEPT)
    learnability = learner_loss - ref_loss[kept_global]
    return (ref_loss, learnability, grad_up)
```

```python
import jax
import jax.numpy as jnp
from jax import lax
from jax.sharding import PartitionSpec as P

logit_scale = 64.0
eps = 1e-06
f32 = jnp.float32
bf16 = jnp.bfloat16


def gelu_parts(pre_act):
    cumul = 0.5 * (1.0 + lax.erf(pre_act * 0.7071067811865476))
    density = jnp.exp(-0.5 * pre_act * pre_act) * 0.3989422804014327
    return (pre_act * cumul, cumul + pre_act * density)


def swap(value, axis, bit):
    size = lax.axis_size(axis)
    return lax.ppermute(value, axis, [(i, i ^ bit) for i in range(size)])


def rotate_pairs(value, step):
    size = lax.axis_size("sel")
    return lax.ppermute(value, "sel", [(i, (i + 2 * step) % size) for i in range(size)])


def mdl_pieces(value):
    n = lax.axis_size("mdl")
    out = [value] + [None] * (n - 1)
    top = n // 2
    if n == 1:
        return out
    out[top] = swap(value, "mdl", top)
    low = top // 2
    have = [0, top]
    while low:
        for j in list(have):
            out[j | low] = swap(out[j], "mdl", low)
            have.append(j | low)
        low //= 2
    return out


def in_order(pieces, axis):
    me = lax.axis_index("mdl")
    bit = 1
    while bit < lax.axis_size("mdl"):
        set_bit = (me & bit) != 0
        merged = []
        for j in range(0, len(pieces), 2):
            first, second = pieces[j], pieces[j + 1]
            merged.append(
                jnp.where(
                    set_bit,
                    jnp.concatenate([second, first], axis),
                    jnp.concatenate([first, second], axis),
                )
            )
        pieces = merged
        bit *= 2
    return pieces[0]


def mdl_sum(value):
    bit = 1
    while bit < lax.axis_size("mdl"):
        value = value + swap(value, "mdl", bit)
        bit *= 2
    return value


def unit_rows(values):
    norm_sq = jnp.sum(values * values, axis=1)
    return (values * lax.rsqrt(norm_sq + eps)[:, None]).astype(bf16)


def exp_total(rows_full, texts):
    scores = lax.dot_general(
        rows_full, texts, (((1,), (1,)), ((), ())), preferred_element_type=f32
    )
    return jnp.sum(jnp.exp(logit_scale * scores), axis=1)


def own_product(rows, texts):
    return jnp.sum(rows.astype(f32) * texts.astype(f32), axis=1)


def per_device(patches, text, ref_proj, w_up, w_down, kept_index, dest, cotan):
    n_sel = lax.axis_size("sel")
    n_mdl = lax.axis_size("mdl")
    ex_dev = text.shape[0]
    d_part = patches.shape[1]
    n_patch = patches.shape[0] // ex_dev
    k_dev = kept_index.shape[0]
    n_rows = k_dev * n_patch
    ff_dev = w_up.shape[1]
    n_high = n_sel // 2
    rotations = n_high <= 4
    sel_me, mdl_me = lax.axis_index("sel"), lax.axis_index("mdl")
    pair_me, high_me = sel_me % 2, sel_me // 2

    patches_t = patches.T
    row_of = (kept_index[:, None] * n_patch + jnp.arange(n_patch)[None, :]).reshape(-1)
    pick = (jnp.arange(ex_dev * n_patch)[:, None] == row_of[None, :]).astype(bf16)
    tok_t = jnp.dot(patches_t, pick, preferred_element_type=f32).astype(bf16)
    cot_t = cotan.T
    blk = d_part * n_mdl // n_sel
    halves = tok_t.reshape(d_part // (2 * blk), 2, blk, n_rows)
    send_half = lax.dynamic_index_in_dim(halves, 1 - pair_me, 1, keepdims=False)
    recv_half = swap(send_half.reshape(d_part // 2, n_rows), "sel", 1)

    tok_full = in_order(mdl_pieces(tok_t), 0)
    cot_full = in_order(mdl_pieces(cot_t), 0)
    recv_half_full = in_order(mdl_pieces(recv_half), 0)
    n_blk = d_part * n_mdl // (2 * blk)
    own_half_full = lax.dynamic_index_in_dim(
        tok_full.reshape(n_blk, 2, blk, n_rows), pair_me, 1, keepdims=False
    ).reshape(n_blk * blk, n_rows)
    tok_pair = jnp.concatenate([own_half_full, recv_half_full], axis=1)

    counts = jnp.sum((dest[:, None] == jnp.arange(n_sel)[None, :]).astype(f32), axis=0)
    if rotations:
        pair_counts = counts + swap(counts, "sel", 1)
        counts = pair_counts
        for step in range(1, n_high):
            counts = counts + rotate_pairs(pair_counts, step)
    else:
        counts = lax.psum(counts, "sel")
    row_weight = 1.0 / jnp.repeat(counts[dest], n_patch)

    text_full = in_order(mdl_pieces(text), 1).astype(f32)
    text_hat = unit_rows(text_full)
    share = ex_dev // n_mdl
    text_share = lax.dynamic_slice_in_dim(text_hat, mdl_me * share, share, 0)
    if rotations:
        pair_share = jnp.concatenate([text_share, swap(text_share, "sel", 1)], axis=0)
        text_split = jnp.concatenate(
            [pair_share] + [rotate_pairs(pair_share, s) for s in range(1, n_high)], axis=0
        )
    else:
        text_split = lax.all_gather(text_share, "sel", axis=0, tiled=True)

    pooled_t = (
        jnp.sum(patches_t.reshape(d_part, ex_dev, n_patch).astype(f32), axis=2) * (1.0 / n_patch)
    ).astype(bf16)
    pooled_full = in_order(mdl_pieces(pooled_t), 0)
    img_emb = lax.dot_general(
        pooled_full, ref_proj, (((0,), (0,)), ((), ())), preferred_element_type=f32
    )
    img_hat = unit_rows(in_order(mdl_pieces(img_emb), 1))
    ref_own = own_product(img_hat, text_hat)
    ref_part = exp_total(img_hat, text_split)

    pre_act = lax.dot_general(
        tok_full, w_up, (((0,), (0,)), ((), ())), preferred_element_type=f32
    )
    activated, gelu_slope = gelu_parts(pre_act)
    hidden = activated.astype(bf16)
    mixed = jnp.dot(hidden, w_down, preferred_element_type=f32)
    mixed_pool = mdl_sum(jnp.sum(mixed.reshape(k_dev, n_patch, -1), axis=1))
    tok_pool = jnp.sum(tok_full.reshape(-1, k_dev, n_patch).astype(f32), axis=2).T
    learn_pool = ((mixed_pool + tok_pool) * (1.0 / n_patch)).astype(bf16)
    learn_emb = jnp.dot(learn_pool, ref_proj, preferred_element_type=f32)
    learn_hat = unit_rows(in_order(mdl_pieces(learn_emb), 1))
    kept_text = text_hat[kept_index]
    learn_own = own_product(learn_hat, kept_text)
    learn_part = exp_total(learn_hat, text_split)
    totals = mdl_sum(jnp.concatenate([ref_part, learn_part]))
    ref_loss = jnp.log(totals[:ex_dev]) - logit_scale * ref_own
    learner_loss = jnp.log(totals[ex_dev:]) - logit_scale * learn_own
    learnability = learner_loss - ref_loss[kept_index]

    n_chunks = 4
    width = ff_dev // n_chunks
    outs = []
    for c in range(n_chunks):
        cols = slice(c * width, (c + 1) * width)
        grad_act = lax.dot_general(
            cot_full, w_down[cols], (((0,), (1,)), ((), ())), preferred_element_type=f32
        )
        grad_pre = (grad_act * row_weight[:, None] * gelu_slope[:, cols]).astype(bf16)
        pair_pre = jnp.concatenate([grad_pre, swap(grad_pre, "sel", 1)], axis=0)
        part = jnp.dot(tok_pair, pair_pre, preferred_element_type=f32)
        part = part.reshape(n_high, blk, width)
        if rotations:
            total = lax.dynamic_index_in_dim(part, high_me, 0, keepdims=False)
            for step in range(1, n_high):
                block = lax.dynamic_index_in_dim(
                    part, (high_me + step) % n_high, 0, keepdims=False
                )
                total = total + rotate_pairs(block.astype(bf16), step).astype(f32)
        else:
            total = lax.psum_scatter(
                part,
                "sel",
                scatter_dimension=0,
                axis_index_groups=[list(range(p, n_sel, 2)) for p in range(2)],
                tiled=False,
            )
        outs.append(total)
    grad_up = jnp.concatenate(outs, axis=1)
    return (ref_loss, learnability, grad_up)


def solution(mesh):
    in_specs = (
        P("sel", "mdl"),
        P("sel", "mdl"),
        P(None, "mdl"),
        P(None, "mdl"),
        P("mdl", None),
        P("sel"),
        P("sel"),
        P("sel", "mdl"),
    )
    out_specs = (P("sel"), P("sel"), P("sel", "mdl"))
    return jax.shard_map(
        per_device, mesh=mesh, in_specs=in_specs, out_specs=out_specs, check_vma=False
    )
```

```python
import functools

import jax
import jax.numpy as jnp
from jax import lax
from jax.experimental import pallas as pl
from jax.experimental.pallas import tpu as pltpu
from jax.sharding import PartitionSpec as P

logit_scale = 64.0
eps = 1e-06
f32 = jnp.float32
bf16 = jnp.bfloat16


def gelu_parts(pre_act):
    cumul = 0.5 * (1.0 + lax.erf(pre_act * 0.7071067811865476))
    density = jnp.exp(-0.5 * pre_act * pre_act) * 0.3989422804014327
    return (pre_act * cumul, cumul + pre_act * density)


def swap(value, axis, bit):
    size = lax.axis_size(axis)
    return lax.ppermute(value, axis, [(i, i ^ bit) for i in range(size)])


def rotate_pairs(value, step):
    size = lax.axis_size("sel")
    return lax.ppermute(value, "sel", [(i, (i + 2 * step) % size) for i in range(size)])


def mdl_pieces(value):
    n = lax.axis_size("mdl")
    out = [value] + [None] * (n - 1)
    top = n // 2
    if n == 1:
        return out
    out[top] = swap(value, "mdl", top)
    low = top // 2
    have = [0, top]
    while low:
        for j in list(have):
            out[j | low] = swap(out[j], "mdl", low)
            have.append(j | low)
        low //= 2
    return out


def in_order(pieces, axis):
    me = lax.axis_index("mdl")
    bit = 1
    while bit < lax.axis_size("mdl"):
        set_bit = (me & bit) != 0
        merged = []
        for j in range(0, len(pieces), 2):
            first, second = pieces[j], pieces[j + 1]
            merged.append(
                jnp.where(
                    set_bit,
                    jnp.concatenate([second, first], axis),
                    jnp.concatenate([first, second], axis),
                )
            )
        pieces = merged
        bit *= 2
    return pieces[0]


def mdl_sum(value):
    bit = 1
    while bit < lax.axis_size("mdl"):
        value = value + swap(value, "mdl", bit)
        bit *= 2
    return value


def unit_rows(values):
    norm_sq = jnp.sum(values * values, axis=1)
    return (values * lax.rsqrt(norm_sq + eps)[:, None]).astype(bf16)


def exp_total(rows_full, texts):
    scores = lax.dot_general(
        rows_full, texts, (((1,), (1,)), ((), ())), preferred_element_type=f32
    )
    return jnp.sum(jnp.exp(logit_scale * scores), axis=1)


def own_product(rows, texts):
    return jnp.sum(rows.astype(f32) * texts.astype(f32), axis=1)


def per_device(patches, text, ref_proj, w_up, w_down, kept_index, dest, cotan):
    n_sel = lax.axis_size("sel")
    n_mdl = lax.axis_size("mdl")
    ex_dev = text.shape[0]
    d_part = patches.shape[1]
    n_patch = patches.shape[0] // ex_dev
    k_dev = kept_index.shape[0]
    n_rows = k_dev * n_patch
    ff_dev = w_up.shape[1]
    n_high = n_sel // 2
    rotations = n_high <= 4
    sel_me, mdl_me = lax.axis_index("sel"), lax.axis_index("mdl")
    pair_me, high_me = sel_me % 2, sel_me // 2

    patches_t = patches.T
    row_of = (kept_index[:, None] * n_patch + jnp.arange(n_patch)[None, :]).reshape(-1)
    pick = (jnp.arange(ex_dev * n_patch)[:, None] == row_of[None, :]).astype(bf16)
    tok_t = jnp.dot(patches_t, pick, preferred_element_type=f32).astype(bf16)
    cot_t = cotan.T
    blk = d_part * n_mdl // n_sel
    halves = tok_t.reshape(d_part // (2 * blk), 2, blk, n_rows)
    send_half = lax.dynamic_index_in_dim(halves, 1 - pair_me, 1, keepdims=False)
    recv_half = swap(send_half.reshape(d_part // 2, n_rows), "sel", 1)

    tok_full = in_order(mdl_pieces(tok_t), 0)
    cot_full = in_order(mdl_pieces(cot_t), 0)
    recv_half_full = in_order(mdl_pieces(recv_half), 0)
    n_blk = d_part * n_mdl // (2 * blk)
    own_half_full = lax.dynamic_index_in_dim(
        tok_full.reshape(n_blk, 2, blk, n_rows), pair_me, 1, keepdims=False
    ).reshape(n_blk * blk, n_rows)
    tok_pair = jnp.concatenate([own_half_full, recv_half_full], axis=1)

    counts = jnp.sum((dest[:, None] == jnp.arange(n_sel)[None, :]).astype(f32), axis=0)
    if rotations:
        pair_counts = counts + swap(counts, "sel", 1)
        counts = pair_counts
        for step in range(1, n_high):
            counts = counts + rotate_pairs(pair_counts, step)
    else:
        counts = lax.psum(counts, "sel")
    row_weight = 1.0 / jnp.repeat(counts[dest], n_patch)

    text_full = in_order(mdl_pieces(text), 1).astype(f32)
    text_hat = unit_rows(text_full)
    share = ex_dev // n_mdl
    text_share = lax.dynamic_slice_in_dim(text_hat, mdl_me * share, share, 0)
    if rotations:
        pair_share = jnp.concatenate([text_share, swap(text_share, "sel", 1)], axis=0)
        text_split = jnp.concatenate(
            [pair_share] + [rotate_pairs(pair_share, s) for s in range(1, n_high)], axis=0
        )
    else:
        text_split = lax.all_gather(text_share, "sel", axis=0, tiled=True)

    pooled_t = (
        jnp.sum(patches_t.reshape(d_part, ex_dev, n_patch).astype(f32), axis=2) * (1.0 / n_patch)
    ).astype(bf16)
    pooled_full = in_order(mdl_pieces(pooled_t), 0)
    img_emb = lax.dot_general(
        pooled_full, ref_proj, (((0,), (0,)), ((), ())), preferred_element_type=f32
    )
    img_hat = unit_rows(in_order(mdl_pieces(img_emb), 1))
    ref_own = own_product(img_hat, text_hat)
    ref_part = exp_total(img_hat, text_split)

    pre_act = lax.dot_general(
        tok_full, w_up, (((0,), (0,)), ((), ())), preferred_element_type=f32
    )
    activated, gelu_slope = gelu_parts(pre_act)
    hidden = activated.astype(bf16)
    mixed = jnp.dot(hidden, w_down, preferred_element_type=f32)
    mixed_pool = mdl_sum(jnp.sum(mixed.reshape(k_dev, n_patch, -1), axis=1))
    tok_pool = jnp.sum(tok_full.reshape(-1, k_dev, n_patch).astype(f32), axis=2).T
    learn_pool = ((mixed_pool + tok_pool) * (1.0 / n_patch)).astype(bf16)
    learn_emb = jnp.dot(learn_pool, ref_proj, preferred_element_type=f32)
    learn_hat = unit_rows(in_order(mdl_pieces(learn_emb), 1))
    kept_text = text_hat[kept_index]
    learn_own = own_product(learn_hat, kept_text)
    learn_part = exp_total(learn_hat, text_split)
    totals = mdl_sum(jnp.concatenate([ref_part, learn_part]))
    ref_loss = jnp.log(totals[:ex_dev]) - logit_scale * ref_own
    learner_loss = jnp.log(totals[ex_dev:]) - logit_scale * learn_own
    learnability = learner_loss - ref_loss[kept_index]

    n_chunks = 4
    width = ff_dev // n_chunks
    outs = []
    for c in range(n_chunks):
        cols = slice(c * width, (c + 1) * width)
        grad_act = lax.dot_general(
            cot_full, w_down[cols], (((0,), (1,)), ((), ())), preferred_element_type=f32
        )
        grad_pre = (grad_act * row_weight[:, None] * gelu_slope[:, cols]).astype(bf16)
        pair_pre = jnp.concatenate([grad_pre, swap(grad_pre, "sel", 1)], axis=0)
        part = jnp.dot(tok_pair, pair_pre, preferred_element_type=f32)
        part = part.reshape(n_high, blk, width)
        if rotations:
            total = lax.dynamic_index_in_dim(part, high_me, 0, keepdims=False)
            for step in range(1, n_high):
                block = lax.dynamic_index_in_dim(
                    part, (high_me + step) % n_high, 0, keepdims=False
                )
                total = total + rotate_pairs(block.astype(bf16), step).astype(f32)
        else:
            total = lax.psum_scatter(
                part,
                "sel",
                scatter_dimension=0,
                axis_index_groups=[list(range(p, n_sel, 2)) for p in range(2)],
                tiled=False,
            )
        outs.append(total)
    grad_up = jnp.concatenate(outs, axis=1)
    return (ref_loss, learnability, grad_up)


def dot_f32(a, b):
    return jnp.dot(a, b, preferred_element_type=f32)


def dot_rows(a, b):
    return lax.dot_general(a, b, (((1,), (1,)), ((), ())), preferred_element_type=f32)


def dot_cols(a, b):
    return lax.dot_general(a, b, (((0,), (0,)), ((), ())), preferred_element_type=f32)


def group_mask(n_items, n_patch):
    shape = (n_items, n_items * n_patch)
    row = lax.broadcasted_iota(jnp.int32, shape, 1)
    first = n_patch * lax.broadcasted_iota(jnp.int32, shape, 0)
    return (row >= first) & (row < first + n_patch), row - first


def as_row(column):
    n = column.shape[0]
    return jnp.broadcast_to(column, (n, n)).T[0:1]


def place(index, length):
    return pl.ds(pl.multiple_of(index * length, length), length)


def call(body, out_shape, cost, grid=(), **kwargs):
    flops, moved = cost
    return pl.pallas_call(
        body,
        out_shape=out_shape,
        grid=grid,
        cost_estimate=pl.CostEstimate(flops=flops, bytes_accessed=moved, transcendentals=0),
        compiler_params=pltpu.CompilerParams(vmem_limit_bytes=40 * 2**20),
        **kwargs,
    )


def struct(shape, dtype):
    return jax.ShapeDtypeStruct(shape, dtype)


def pick_body(n_patch, patches, kept, dest, tok, half, pool, counts):
    d_part, n_all = patches.shape
    ex_dev = n_all // n_patch
    k_dev = kept.shape[1]
    member, offset = group_mask(k_dev, n_patch)
    expand = member.astype(bf16)
    index = jnp.broadcast_to(kept[...].astype(f32), (8, k_dev)).astype(bf16)
    base = dot_f32(index, expand)[0:1].astype(jnp.int32)
    row = base * n_patch + jnp.sum(jnp.where(member, offset, 0), axis=0, keepdims=True)
    pick = (lax.broadcasted_iota(jnp.int32, (n_all, row.shape[1]), 0) == row).astype(bf16)
    values = patches[...]
    tok[...] = dot_f32(values, pick).astype(bf16)
    other = 1 - lax.rem(lax.axis_index("sel"), 2)
    half[...] = tok[place(other, d_part // 2), :]
    groups, _ = group_mask(ex_dev, n_patch)
    pool[...] = (dot_rows(values, groups.astype(bf16)) * (1.0 / n_patch)).astype(bf16)
    shards = lax.broadcasted_iota(jnp.int32, (128, k_dev), 0) == dest[...]
    counts[...] = dot_rows(jnp.ones((8, k_dev), bf16), shards.astype(bf16))


def text_body(t0, t1, t2, t3, hat, share, whole):
    me = lax.axis_index("mdl")
    width = t0.shape[1]
    for j, piece in enumerate((t0, t1, t2, t3)):
        whole[:, place(me ^ j, width)] = piece[...].astype(f32)
    values = whole[...]
    norm_sq = jnp.sum(values * values, axis=1, keepdims=True)
    hat[...] = (values * lax.rsqrt(norm_sq + eps)).astype(bf16)
    share[...] = hat[place(me, share.shape[0]), :]


def forward_body(n_patch, n_mdl, t0, t1, t2, t3, w_up, w_down, slope, mixed, tok_full, tok):
    d_part, n_rows = t0.shape
    k_dev = n_rows // n_patch
    member, _ = group_mask(k_dev, n_patch)
    groups = member.astype(bf16)

    @pl.when(pl.program_id(0) == 0)
    def _():
        me = lax.axis_index("mdl")
        for j, piece in enumerate((t0, t1, t2, t3)):
            tok_full[place(me ^ j, d_part), :] = piece[...]
        tok[...] = tok_full[...].T
        mixed[...] = dot_f32(groups, tok[...]) * (1.0 / n_mdl)

    pre_act = dot_f32(tok[...], w_up[...])
    activated, gelu_slope = gelu_parts(pre_act)
    slope[...] = gelu_slope
    pooled = dot_f32(groups, activated.astype(bf16))
    high = pooled.astype(bf16)
    low = (pooled - high.astype(f32)).astype(bf16)
    both = dot_f32(jnp.concatenate([high, low], axis=0), w_down[...])
    mixed[...] += both[:k_dev] + both[k_dev:]


def weigh_body(n_patch, c0, c1, c2, c3, n0, n1, n2, n3, dest, w_down, slope, weighted, pre, cot):
    d_part, n_rows = c0.shape
    k_dev = n_rows // n_patch
    member, _ = group_mask(k_dev, n_patch)
    counts = (n0[...] + n1[...]) + (n2[...] + n3[...])
    shards = lax.broadcasted_iota(jnp.int32, (128, k_dev), 0) == dest[...]
    named = dot_f32(counts.astype(bf16), shards.astype(bf16))
    weight = 1.0 / dot_f32(named.astype(bf16), member.astype(bf16))[0:1]
    me = lax.axis_index("mdl")
    for j, piece in enumerate((c0, c1, c2, c3)):
        cot[place(me ^ j, d_part), :] = (piece[...].astype(f32) * weight).astype(bf16)
    weighted[...] = cot[...].T
    pre[...] = (dot_rows(weighted[...], w_down[...]) * slope[...]).astype(bf16)


def backward_body(weighted, w_down, slope, pre):
    pre[...] = (dot_rows(weighted[...], w_down[...]) * slope[...]).astype(bf16)


def send_blocks(part, own, sends):
    blk = own.shape[0]
    own[...] = part[:blk]
    for r, block in enumerate(sends):
        block[...] = part[(r + 1) * blk : (r + 2) * blk].astype(bf16)


def first_grad_body(n_high, tok_full, h0, h1, h2, h3, pre, pre_pair, pair, own, *sends):
    n_rows = tok_full.shape[1]
    blk = own.shape[0]
    me = lax.axis_index("mdl")
    sel = lax.axis_index("sel")
    parity, high = lax.rem(sel, 2), lax.div(sel, 2)
    for j, piece in enumerate((h0, h1, h2, h3)):
        block = me ^ j
        rows = place(lax.rem(block + n_high - high, n_high), blk)
        pair[rows, 0:n_rows] = tok_full[place(2 * block + parity, blk), :]
        pair[rows, n_rows:] = piece[:, 0:n_rows]
    part = dot_f32(pair[:, 0:n_rows], pre[...]) + dot_f32(pair[:, n_rows:], pre_pair[...])
    send_blocks(part, own, sends)


def grad_body(pair, pre, pre_pair, own, *sends):
    n_rows = pre.shape[0]
    part = dot_f32(pair[:, 0:n_rows], pre[...]) + dot_f32(pair[:, n_rows:], pre_pair[...])
    send_blocks(part, own, sends)


def image_body(h0, h1, h2, h3, ref_proj, emb, pooled):
    me = lax.axis_index("mdl")
    n_rows = h0.shape[0]
    n_ex = pooled.shape[1]
    first = h0.shape[1] - 2 * n_ex
    for j, piece in enumerate((h0, h1, h2, h3)):
        for part in range(2):
            pooled[place((me ^ j) * 2 + part, n_rows), :] = piece[
                :, first + part * n_ex : first + (part + 1) * n_ex
            ]
    emb[...] = dot_cols(pooled[...], ref_proj[...])


def normed(pieces, whole):
    me = lax.axis_index("mdl")
    width = pieces[0].shape[1]
    for j, piece in enumerate(pieces):
        whole[:, place(me ^ j, width)] = piece[...]
    values = whole[...]
    norm_sq = jnp.sum(values * values, axis=1, keepdims=True)
    return (values * lax.rsqrt(norm_sq + eps)).astype(bf16)


def share_totals(hat, shares):
    total = None
    for share in shares:
        scores = dot_rows(share[...], hat)
        part = jnp.sum(jnp.exp(logit_scale * scores), axis=0, keepdims=True)
        total = part if total is None else total + part
    return total


def own_score(hat, texts):
    return jnp.sum(hat.astype(f32) * texts.astype(f32), axis=1, keepdims=True)


def image_loss_body(e0, e1, e2, e3, text_hat, s0, s1, s2, s3, s4, own, total, whole):
    hat = normed((e0, e1, e2, e3), whole)
    own[...] = as_row(own_score(hat, text_hat[...]))
    total[...] = share_totals(hat, (s0, s1, s2, s3, s4))


def learn_head_body(n_patch, a, b, ref_proj, emb):
    learn_pool = ((a[...] + b[...]) * (1.0 / n_patch)).astype(bf16)
    emb[...] = dot_f32(learn_pool, ref_proj[...])


def learn_loss_body(
    e0, e1, e2, e3, text_hat, kept, s0, s1, s2, s3, s4, ref_total, own, totals, whole
):
    hat = normed((e0, e1, e2, e3), whole)
    k_dev, ex_dev = kept.shape[1], text_hat.shape[0]
    pick = (lax.broadcasted_iota(jnp.int32, (ex_dev, k_dev), 0) == kept[...]).astype(bf16)
    kept_text = dot_cols(pick, text_hat[...])
    own[...] = as_row(own_score(hat, kept_text))
    totals[...] = jnp.zeros_like(totals)
    totals[:, 0:ex_dev] = ref_total[...]
    totals[:, ex_dev : ex_dev + k_dev] = share_totals(hat, (s0, s1, s2, s3, s4))


def losses_body(a, b, ref_own, own, kept, ref_loss, learnability):
    totals = a[...] + b[...]
    k_dev, ex_dev = kept.shape[1], ref_own.shape[1]
    losses = jnp.log(totals[:, 0:ex_dev]) - logit_scale * ref_own[...]
    ref_loss[...] = losses
    learner = jnp.log(totals[:, ex_dev : ex_dev + k_dev]) - logit_scale * own[...]
    column = as_row_t(losses)
    pick = lax.broadcasted_iota(jnp.int32, (ex_dev, k_dev), 0) == kept[...]
    picked = jnp.sum(jnp.where(pick, column, 0.0), axis=0, keepdims=True)
    learnability[...] = learner - picked


def as_row_t(row):
    n = row.shape[1]
    return jnp.broadcast_to(row, (n, n)).T[:, 0:1]


def quarter_sel(patches, text, ref_proj, w_up, w_down, kept_index, dest, cotan):
    n_mdl, n_sel = lax.axis_size("mdl"), lax.axis_size("sel")
    n_high = n_sel // 2
    ex_dev, emb_part = text.shape
    d_part = patches.shape[1]
    d_full = d_part * n_mdl
    n_patch = patches.shape[0] // ex_dev
    k_dev = kept_index.shape[0]
    n_rows = k_dev * n_patch
    ff_dev = w_up.shape[1]
    blk = d_full // n_sel
    kept_row = kept_index.reshape(1, k_dev)
    dest_row = dest.reshape(1, k_dev)
    cot_t = cotan.T

    tok, half, pool, counts = call(
        functools.partial(pick_body, n_patch),
        (
            struct((d_part, n_rows), bf16),
            struct((d_part // 2, n_rows), bf16),
            struct((d_part, ex_dev), bf16),
            struct((8, 128), f32),
        ),
        (2 * d_part * ex_dev * n_patch * n_rows, 2 * 2**20),
    )(patches.T, kept_row, dest_row)

    tok_pieces = mdl_pieces(tok)
    half_pair = swap(half, "sel", 1)
    pair_counts = counts + swap(counts, "sel", 1)
    all_counts = [pair_counts] + [rotate_pairs(pair_counts, s) for s in range(1, n_high)]
    cot_pieces = mdl_pieces(cot_t)
    text_pieces = mdl_pieces(text)

    text_hat, text_share = call(
        text_body,
        (struct((ex_dev, emb_part * n_mdl), bf16), struct((ex_dev // n_mdl, emb_part * n_mdl), bf16)),
        (2**20, 2**20),
        scratch_shapes=[pltpu.VMEM((ex_dev, emb_part * n_mdl), f32)],
    )(*text_pieces)
    share_pair = swap(text_share, "sel", 1)
    two_shares = jnp.concatenate([text_share, share_pair], axis=0)
    shares = [text_share, share_pair] + [rotate_pairs(two_shares, s) for s in range(1, n_high)]

    extras = jnp.concatenate(
        [half_pair, pool[: d_part // 2], pool[d_part // 2 :]], axis=1
    )
    extra_pieces = mdl_pieces(extras)

    width = 512
    whole = lambda shape: pl.BlockSpec(shape, lambda i: (0,) * len(shape))
    slope, mixed, tok_full = call(
        functools.partial(forward_body, n_patch, n_mdl),
        (
            struct((n_rows, ff_dev), f32),
            struct((k_dev, d_full), f32),
            struct((d_full, n_rows), bf16),
        ),
        (4 * n_rows * d_full * ff_dev, 12 * 2**20),
        grid=(ff_dev // width,),
        in_specs=[whole((d_part, n_rows))] * 4
        + [
            pl.BlockSpec((d_full, width), lambda i: (0, i)),
            pl.BlockSpec((width, d_full), lambda i: (i, 0)),
        ],
        out_specs=[
            pl.BlockSpec((n_rows, width), lambda i: (0, i)),
            whole((k_dev, d_full)),
            whole((d_full, n_rows)),
        ],
        scratch_shapes=[pltpu.VMEM((n_rows, d_full), bf16)],
    )(*tok_pieces, w_up, w_down)

    widths = (256, 256, 512, 512)
    starts = [sum(widths[:c]) for c in range(len(widths))]

    def chunk_specs(c):
        first, size = starts[c] // widths[c], widths[c]
        return [
            pl.BlockSpec((size, d_full), lambda i: (first, 0)),
            pl.BlockSpec((n_rows, size), lambda i: (0, first)),
        ]

    pres = []
    for c, size in enumerate(widths):
        cost = (2 * n_rows * d_full * size, (d_full * (size + n_rows) * 2 + n_rows * size * 6))
        pre_struct = struct((n_rows, size), bf16)
        if c == 0:
            weighted, pre = call(
                functools.partial(weigh_body, n_patch),
                (struct((n_rows, d_full), bf16), pre_struct),
                cost,
                grid=(1,),
                in_specs=[whole((d_part, n_rows))] * 4
                + [whole((8, 128))] * 4
                + [whole((1, k_dev))]
                + chunk_specs(c),
                out_specs=[whole((n_rows, d_full)), whole((n_rows, size))],
                scratch_shapes=[pltpu.VMEM((d_full, n_rows), bf16)],
            )(*cot_pieces, *all_counts, dest_row, w_down, slope)
        else:
            pre = call(
                backward_body,
                pre_struct,
                cost,
                grid=(1,),
                in_specs=[whole((n_rows, d_full))] + chunk_specs(c),
                out_specs=whole((n_rows, size)),
            )(weighted, w_down, slope)
        pres.append(pre)
    pair_pres = [swap(pre, "sel", 1) for pre in pres]

    outs = []
    for c, size in enumerate(widths):
        cost = (4 * n_rows * blk * n_high * size, 4 * 2**20)
        blocks = (struct((blk, size), f32),) + (struct((blk, size), bf16),) * (n_high - 1)
        if c == 0:
            pair, *blocks = call(
                functools.partial(first_grad_body, n_high),
                (struct((blk * n_high, 2 * n_rows), bf16),) + blocks,
                cost,
            )(tok_full, *extra_pieces, pres[c], pair_pres[c])
        else:
            blocks = call(grad_body, blocks, cost)(pair, pres[c], pair_pres[c])
        total = blocks[0]
        for r in range(1, n_high):
            total = total + rotate_pairs(blocks[r], r).astype(f32)
        outs.append(total)
    grad_up = jnp.concatenate(outs, axis=1)

    emb_cost = (2 * ex_dev * d_full * emb_part, 2**20)
    img_emb = call(
        image_body,
        struct((ex_dev, emb_part), f32),
        emb_cost,
        scratch_shapes=[pltpu.VMEM((d_full, ex_dev), bf16)],
    )(*extra_pieces, ref_proj)
    emb_full = emb_part * n_mdl
    loss_cost = (2 * ex_dev * emb_full * ex_dev * n_sel // n_mdl, 2 * 2**20)
    ref_own, ref_total = call(
        image_loss_body,
        (struct((1, ex_dev), f32), struct((1, ex_dev), f32)),
        loss_cost,
        scratch_shapes=[pltpu.VMEM((ex_dev, emb_full), f32)],
    )(*mdl_pieces(img_emb), text_hat, *shares)

    mixed = mixed + swap(mixed, "mdl", 1)
    learn_emb = call(
        functools.partial(learn_head_body, n_patch),
        struct((k_dev, emb_part), f32),
        (2 * k_dev * d_full * emb_part, 2**20),
    )(mixed, swap(mixed, "mdl", 2), ref_proj)
    learn_own, totals = call(
        learn_loss_body,
        (struct((1, k_dev), f32), struct((1, 2 * ex_dev), f32)),
        loss_cost,
        scratch_shapes=[pltpu.VMEM((k_dev, emb_full), f32)],
    )(*mdl_pieces(learn_emb), text_hat, kept_row, *shares, ref_total)
    totals = totals + swap(totals, "mdl", 1)
    ref_loss, learnability = call(
        losses_body,
        (struct((1, ex_dev), f32), struct((1, k_dev), f32)),
        (2**16, 2**16),
    )(totals, swap(totals, "mdl", 2), ref_own, learn_own, kept_row)
    return (ref_loss.reshape(ex_dev), learnability.reshape(k_dev), grad_up)


def solution(mesh):
    in_specs = (
        P("sel", "mdl"),
        P("sel", "mdl"),
        P(None, "mdl"),
        P(None, "mdl"),
        P("mdl", None),
        P("sel"),
        P("sel"),
        P("sel", "mdl"),
    )
    out_specs = (P("sel"), P("sel"), P("sel", "mdl"))
    body = quarter_sel if (mesh.shape["sel"], mesh.shape["mdl"]) == (8, 4) else per_device
    return jax.shard_map(
        body, mesh=mesh, in_specs=in_specs, out_specs=out_specs, check_vma=False
    )
```

```python
import functools

import jax
import jax.numpy as jnp
from jax import lax
from jax.experimental import pallas as pl
from jax.experimental.pallas import tpu as pltpu
from jax.sharding import PartitionSpec as P

logit_scale = 64.0
eps = 1e-06
f32 = jnp.float32
bf16 = jnp.bfloat16


def gelu_parts(pre_act):
    cumul = 0.5 * (1.0 + lax.erf(pre_act * 0.7071067811865476))
    density = jnp.exp(-0.5 * pre_act * pre_act) * 0.3989422804014327
    return (pre_act * cumul, cumul + pre_act * density)


def swap(value, axis, bit):
    size = lax.axis_size(axis)
    return lax.ppermute(value, axis, [(i, i ^ bit) for i in range(size)])


def rotate_pairs(value, step):
    size = lax.axis_size("sel")
    return lax.ppermute(value, "sel", [(i, (i + 2 * step) % size) for i in range(size)])


def mdl_pieces(value):
    n = lax.axis_size("mdl")
    out = [value] + [None] * (n - 1)
    top = n // 2
    if n == 1:
        return out
    out[top] = swap(value, "mdl", top)
    low = top // 2
    have = [0, top]
    while low:
        for j in list(have):
            out[j | low] = swap(out[j], "mdl", low)
            have.append(j | low)
        low //= 2
    return out


def in_order(pieces, axis):
    me = lax.axis_index("mdl")
    bit = 1
    while bit < lax.axis_size("mdl"):
        set_bit = (me & bit) != 0
        merged = []
        for j in range(0, len(pieces), 2):
            first, second = pieces[j], pieces[j + 1]
            merged.append(
                jnp.where(
                    set_bit,
                    jnp.concatenate([second, first], axis),
                    jnp.concatenate([first, second], axis),
                )
            )
        pieces = merged
        bit *= 2
    return pieces[0]


def mdl_sum(value):
    bit = 1
    while bit < lax.axis_size("mdl"):
        value = value + swap(value, "mdl", bit)
        bit *= 2
    return value


def unit_rows(values):
    norm_sq = jnp.sum(values * values, axis=1)
    return (values * lax.rsqrt(norm_sq + eps)[:, None]).astype(bf16)


def exp_total(rows_full, texts):
    scores = lax.dot_general(
        rows_full, texts, (((1,), (1,)), ((), ())), preferred_element_type=f32
    )
    return jnp.sum(jnp.exp(logit_scale * scores), axis=1)


def own_product(rows, texts):
    return jnp.sum(rows.astype(f32) * texts.astype(f32), axis=1)


def per_device(patches, text, ref_proj, w_up, w_down, kept_index, dest, cotan):
    n_sel = lax.axis_size("sel")
    n_mdl = lax.axis_size("mdl")
    ex_dev = text.shape[0]
    d_part = patches.shape[1]
    n_patch = patches.shape[0] // ex_dev
    k_dev = kept_index.shape[0]
    n_rows = k_dev * n_patch
    ff_dev = w_up.shape[1]
    n_high = n_sel // 2
    rotations = n_high <= 4
    sel_me, mdl_me = lax.axis_index("sel"), lax.axis_index("mdl")
    pair_me, high_me = sel_me % 2, sel_me // 2

    patches_t = patches.T
    row_of = (kept_index[:, None] * n_patch + jnp.arange(n_patch)[None, :]).reshape(-1)
    pick = (jnp.arange(ex_dev * n_patch)[:, None] == row_of[None, :]).astype(bf16)
    tok_t = jnp.dot(patches_t, pick, preferred_element_type=f32).astype(bf16)
    cot_t = cotan.T
    blk = d_part * n_mdl // n_sel
    halves = tok_t.reshape(d_part // (2 * blk), 2, blk, n_rows)
    send_half = lax.dynamic_index_in_dim(halves, 1 - pair_me, 1, keepdims=False)
    recv_half = swap(send_half.reshape(d_part // 2, n_rows), "sel", 1)

    tok_full = in_order(mdl_pieces(tok_t), 0)
    cot_full = in_order(mdl_pieces(cot_t), 0)
    recv_half_full = in_order(mdl_pieces(recv_half), 0)
    n_blk = d_part * n_mdl // (2 * blk)
    own_half_full = lax.dynamic_index_in_dim(
        tok_full.reshape(n_blk, 2, blk, n_rows), pair_me, 1, keepdims=False
    ).reshape(n_blk * blk, n_rows)
    tok_pair = jnp.concatenate([own_half_full, recv_half_full], axis=1)

    counts = jnp.sum((dest[:, None] == jnp.arange(n_sel)[None, :]).astype(f32), axis=0)
    if rotations:
        pair_counts = counts + swap(counts, "sel", 1)
        counts = pair_counts
        for step in range(1, n_high):
            counts = counts + rotate_pairs(pair_counts, step)
    else:
        counts = lax.psum(counts, "sel")
    row_weight = 1.0 / jnp.repeat(counts[dest], n_patch)

    text_full = in_order(mdl_pieces(text), 1).astype(f32)
    text_hat = unit_rows(text_full)
    share = ex_dev // n_mdl
    text_share = lax.dynamic_slice_in_dim(text_hat, mdl_me * share, share, 0)
    if rotations:
        pair_share = jnp.concatenate([text_share, swap(text_share, "sel", 1)], axis=0)
        text_split = jnp.concatenate(
            [pair_share] + [rotate_pairs(pair_share, s) for s in range(1, n_high)], axis=0
        )
    else:
        text_split = lax.all_gather(text_share, "sel", axis=0, tiled=True)

    pooled_t = (
        jnp.sum(patches_t.reshape(d_part, ex_dev, n_patch).astype(f32), axis=2) * (1.0 / n_patch)
    ).astype(bf16)
    pooled_full = in_order(mdl_pieces(pooled_t), 0)
    img_emb = lax.dot_general(
        pooled_full, ref_proj, (((0,), (0,)), ((), ())), preferred_element_type=f32
    )
    img_hat = unit_rows(in_order(mdl_pieces(img_emb), 1))
    ref_own = own_product(img_hat, text_hat)
    ref_part = exp_total(img_hat, text_split)

    pre_act = lax.dot_general(
        tok_full, w_up, (((0,), (0,)), ((), ())), preferred_element_type=f32
    )
    activated, gelu_slope = gelu_parts(pre_act)
    hidden = activated.astype(bf16)
    mixed = jnp.dot(hidden, w_down, preferred_element_type=f32)
    mixed_pool = mdl_sum(jnp.sum(mixed.reshape(k_dev, n_patch, -1), axis=1))
    tok_pool = jnp.sum(tok_full.reshape(-1, k_dev, n_patch).astype(f32), axis=2).T
    learn_pool = ((mixed_pool + tok_pool) * (1.0 / n_patch)).astype(bf16)
    learn_emb = jnp.dot(learn_pool, ref_proj, preferred_element_type=f32)
    learn_hat = unit_rows(in_order(mdl_pieces(learn_emb), 1))
    kept_text = text_hat[kept_index]
    learn_own = own_product(learn_hat, kept_text)
    learn_part = exp_total(learn_hat, text_split)
    totals = mdl_sum(jnp.concatenate([ref_part, learn_part]))
    ref_loss = jnp.log(totals[:ex_dev]) - logit_scale * ref_own
    learner_loss = jnp.log(totals[ex_dev:]) - logit_scale * learn_own
    learnability = learner_loss - ref_loss[kept_index]

    n_chunks = 4
    width = ff_dev // n_chunks
    outs = []
    for c in range(n_chunks):
        cols = slice(c * width, (c + 1) * width)
        grad_act = lax.dot_general(
            cot_full, w_down[cols], (((0,), (1,)), ((), ())), preferred_element_type=f32
        )
        grad_pre = (grad_act * row_weight[:, None] * gelu_slope[:, cols]).astype(bf16)
        pair_pre = jnp.concatenate([grad_pre, swap(grad_pre, "sel", 1)], axis=0)
        part = jnp.dot(tok_pair, pair_pre, preferred_element_type=f32)
        part = part.reshape(n_high, blk, width)
        if rotations:
            total = lax.dynamic_index_in_dim(part, high_me, 0, keepdims=False)
            for step in range(1, n_high):
                block = lax.dynamic_index_in_dim(
                    part, (high_me + step) % n_high, 0, keepdims=False
                )
                total = total + rotate_pairs(block.astype(bf16), step).astype(f32)
        else:
            total = lax.psum_scatter(
                part,
                "sel",
                scatter_dimension=0,
                axis_index_groups=[list(range(p, n_sel, 2)) for p in range(2)],
                tiled=False,
            )
        outs.append(total)
    grad_up = jnp.concatenate(outs, axis=1)
    return (ref_loss, learnability, grad_up)


def dot_f32(a, b):
    return jnp.dot(a, b, preferred_element_type=f32)


def dot_rows(a, b):
    return lax.dot_general(a, b, (((1,), (1,)), ((), ())), preferred_element_type=f32)


def dot_cols(a, b):
    return lax.dot_general(a, b, (((0,), (0,)), ((), ())), preferred_element_type=f32)


def group_mask(n_items, n_patch):
    shape = (n_items, n_items * n_patch)
    row = lax.broadcasted_iota(jnp.int32, shape, 1)
    first = n_patch * lax.broadcasted_iota(jnp.int32, shape, 0)
    return (row >= first) & (row < first + n_patch), row - first


def as_row(column):
    n = column.shape[0]
    return jnp.broadcast_to(column, (n, n)).T[0:1]


def place(index, length):
    return pl.ds(pl.multiple_of(index * length, length), length)


def call(body, out_shape, cost, grid=(), vmem=40 * 2**20, **kwargs):
    flops, moved = cost
    return pl.pallas_call(
        body,
        out_shape=out_shape,
        grid=grid,
        cost_estimate=pl.CostEstimate(flops=1, bytes_accessed=1, transcendentals=0),
        compiler_params=pltpu.CompilerParams(vmem_limit_bytes=vmem),
        **kwargs,
    )


def struct(shape, dtype):
    return jax.ShapeDtypeStruct(shape, dtype)


def pick_body(
    n_patch, patches_hbm, cot_hbm, kept, dest, text_hbm, both, half, pool, texts, patches, sems
):
    d_part, n_all = patches.shape
    ex_dev = n_all // n_patch
    copies = [
        pltpu.make_async_copy(patches_hbm, patches, sems.at[0]),
        pltpu.make_async_copy(cot_hbm, both.at[pl.ds(d_part, d_part), :], sems.at[1]),
        pltpu.make_async_copy(text_hbm, texts.at[pl.ds(0, ex_dev), :], sems.at[2]),
    ]
    for copy in copies:
        copy.start()
    k_dev = kept.shape[1]
    member, offset = group_mask(k_dev, n_patch)
    expand = member.astype(bf16)
    index = jnp.broadcast_to(kept[...].astype(f32), (8, k_dev)).astype(bf16)
    base = dot_f32(index, expand)[0:1].astype(jnp.int32)
    row = base * n_patch + jnp.sum(jnp.where(member, offset, 0), axis=0, keepdims=True)
    pick = (lax.broadcasted_iota(jnp.int32, (n_all, row.shape[1]), 0) == row).astype(bf16)
    for copy in copies:
        copy.wait()
    values = patches[...]
    both[0:d_part, :] = dot_f32(values, pick).astype(bf16)
    other = 1 - lax.rem(lax.axis_index("sel"), 2)
    half[...] = both[place(other, d_part // 2), :]
    texts[ex_dev:, :] = jnp.zeros((16, texts.shape[1]), bf16)
    texts[ex_dev:, 0:k_dev] = jnp.broadcast_to(dest[...].astype(f32), (16, k_dev)).astype(bf16)
    groups, _ = group_mask(ex_dev, n_patch)
    pool[...] = (dot_rows(values, groups.astype(bf16)) * (1.0 / n_patch)).astype(bf16)


def extras_body(half, pool, t0, t1, t2, t3, extras, texts):
    n_half, n_rows = half.shape
    n_ex = pool.shape[1]
    extras[:, 0:n_rows] = half[...]
    extras[:, n_rows : n_rows + n_ex] = pool[0:n_half, :]
    extras[:, n_rows + n_ex :] = pool[n_half:, :]
    n_text = t0.shape[0]
    for r, piece in enumerate((t0, t1, t2, t3)):
        texts[r * n_text : (r + 1) * n_text, :] = piece[...]


def text_body(k_dev, n_patch, mine, theirs, whole, send, weights):
    n_high = 4
    n_text = mine.shape[0] // n_high
    ex_dev = n_text - 16
    me = lax.axis_index("mdl")
    sel = lax.axis_index("sel")
    parity, high = lax.rem(sel, 2), lax.div(sel, 2)
    shard = lax.broadcasted_iota(jnp.int32, (128, k_dev), 0).astype(f32)
    ones = jnp.ones((8, k_dev), bf16)
    counts = jnp.zeros((8, 128), f32)
    named = []
    for which, place_in_pair in ((mine, parity), (theirs, 1 - parity)):
        for r in range(n_high):
            source = lax.rem(high + n_high - r, n_high)
            rows = place(source * 2 + place_in_pair, ex_dev)
            whole[rows, :] = which[r * n_text : r * n_text + ex_dev, :]
            dest = which[r * n_text + ex_dev : (r + 1) * n_text, 0:k_dev].astype(f32)[0:1]
            is_dest = (shard == dest).astype(bf16)
            counts = counts + dot_rows(ones, is_dest)
            if r == 0:
                named.append(is_dest)
    member = group_mask(k_dev, n_patch)[0].astype(bf16)
    n_rows = k_dev * n_patch
    for i, is_dest in enumerate(named):
        count = dot_f32(counts.astype(bf16), is_dest).astype(bf16)
        weights[:, i * n_rows : (i + 1) * n_rows] = 1.0 / dot_f32(count, member)
    for i in range(2):
        send[i * 2 * ex_dev : (i + 1) * 2 * ex_dev, :] = whole[place(me ^ (2 + i), 2 * ex_dev), :]


def text_relay_body(whole, received, send):
    n_share = received.shape[0] // 2
    send[0:n_share, :] = whole[place(lax.axis_index("mdl") ^ 1, n_share), :]
    send[n_share:, :] = received[n_share:, :]


def share_body(whole, from_x, from_core, share, values):
    n_share, width = share.shape[0], whole.shape[1]
    me = lax.axis_index("mdl")
    pieces = (
        whole[place(me, n_share), :],
        from_core[0:n_share, :],
        from_x[0:n_share, :],
        from_core[n_share:, :],
    )
    for j, piece in enumerate(pieces):
        values[:, place(me ^ j, width)] = piece.astype(f32)
    rows = values[...]
    norm_sq = jnp.sum(rows * rows, axis=1, keepdims=True)
    share[...] = (rows * lax.rsqrt(norm_sq + eps)).astype(bf16)


def stage_body(up, down, up_held, down_held, sems):
    copies = [
        pltpu.make_async_copy(up, up_held, sems.at[0]),
        pltpu.make_async_copy(down, down_held, sems.at[1]),
    ]
    for copy in copies:
        copy.start()
    for copy in copies:
        copy.wait()


def chunk_work(n_patch, tok, cot, w_up, w_down, pre, mixed):
    k_dev = tok.shape[0] // n_patch
    groups = group_mask(k_dev, n_patch)[0].astype(bf16)
    pre_act = dot_f32(tok[...], w_up[...])
    activated, gelu_slope = gelu_parts(pre_act)
    pre[...] = (dot_rows(cot[...], w_down[...]) * gelu_slope).astype(bf16)
    pooled = dot_f32(groups, activated.astype(bf16))
    high = pooled.astype(bf16)
    low = (pooled - high.astype(f32)).astype(bf16)
    both = dot_f32(jnp.concatenate([high, low], axis=0), w_down[...])
    return mixed + (both[:k_dev] + both[k_dev:])


def first_chunk_body(
    n_patch, n_mdl, b0, b1, b2, b3, w_up, w_down, pre, mixed, tok_full, tok, cot, cot_full
):
    d_part, n_rows = b0.shape[0] // 2, b0.shape[1]
    groups = group_mask(n_rows // n_patch, n_patch)[0].astype(bf16)
    me = lax.axis_index("mdl")
    for j, piece in enumerate((b0, b1, b2, b3)):
        tok_full[place(me ^ j, d_part), :] = piece[0:d_part, :]
        cot_full[place(me ^ j, d_part), :] = piece[d_part:, :]
    tok[...] = tok_full[...].T
    cot[...] = cot_full[...].T
    start = dot_f32(groups, tok[...]) * (1.0 / n_mdl)
    mixed[...] = chunk_work(n_patch, tok, cot, w_up, w_down, pre, start)


def next_chunk_body(n_patch, tok, cot, w_up, w_down, mixed_in, pre, mixed):
    mixed[...] = chunk_work(n_patch, tok, cot, w_up, w_down, pre, mixed_in[...])


def split_part(part, keep, send):
    n_keep = keep.shape[0]
    keep[...] = part[:n_keep]
    send[...] = part[n_keep:].astype(bf16)


def first_grad_body(tok_full, h0, h1, h2, h3, weights, pre, pre_pair, pair, keep, send):
    n_rows = tok_full.shape[1]
    blk = h0.shape[0]
    me = lax.axis_index("mdl")
    sel = lax.axis_index("sel")
    parity, high = lax.rem(sel, 2), lax.div(sel, 2)
    for j, piece in enumerate((h0, h1, h2, h3)):
        block = me ^ j
        apart = block ^ high
        rows = place(2 * lax.rem(apart, 2) + lax.div(apart, 2), blk)
        own_tok = tok_full[place(2 * block + parity, blk), :].astype(f32)
        pair[rows, 0:n_rows] = (own_tok * weights[0:1, 0:n_rows]).astype(bf16)
        pair_tok = piece[:, 0:n_rows].astype(f32)
        pair[rows, n_rows:] = (pair_tok * weights[0:1, n_rows:]).astype(bf16)
    grad_body(pair, pre, pre_pair, keep, send)


def grad_body(pair, pre, pre_pair, keep, send):
    n_rows = pre.shape[0]
    part = dot_f32(pair[:, 0:n_rows], pre[...]) + dot_f32(pair[:, n_rows:], pre_pair[...])
    split_part(part, keep, send)


def add_body(held, received, keep, send):
    split_part(held[...] + received[...].astype(f32), keep, send)


def mix_body(a, b, total):
    total[...] = (a[...] + b[...]).astype(total.dtype)


def heads_body(n_patch, h0, h1, h2, h3, a, b, ref_proj, emb, pooled):
    me = lax.axis_index("mdl")
    n_rows = h0.shape[0]
    n_ex = pooled.shape[1]
    first = h0.shape[1] - 2 * n_ex
    for j, piece in enumerate((h0, h1, h2, h3)):
        for part in range(2):
            pooled[place((me ^ j) * 2 + part, n_rows), :] = piece[
                :, first + part * n_ex : first + (part + 1) * n_ex
            ]
    learn_pool = ((a[...].astype(f32) + b[...].astype(f32)) * (1.0 / n_patch)).astype(bf16)
    emb[0:n_ex, :] = dot_cols(pooled[...], ref_proj[...])
    emb[n_ex:, :] = dot_f32(learn_pool, ref_proj[...])


def own_score(hat, texts):
    return jnp.sum(hat.astype(f32) * texts.astype(f32), axis=1, keepdims=True)


def scores_body(e0, e1, e2, e3, share, kept, out, whole):
    me = lax.axis_index("mdl")
    sel = lax.axis_index("sel")
    width = e0.shape[1]
    for j, piece in enumerate((e0, e1, e2, e3)):
        whole[:, place(me ^ j, width)] = piece[...]
    values = whole[...]
    norm_sq = jnp.sum(values * values, axis=1, keepdims=True)
    hat = (values * lax.rsqrt(norm_sq + eps)).astype(bf16)
    k_dev = kept.shape[1]
    n_all = hat.shape[0]
    ex_dev = n_all - k_dev
    scores = dot_rows(share[...], hat)
    out[:, 0:n_all] = jnp.sum(jnp.exp(logit_scale * scores), axis=0, keepdims=True)
    own_text = share[place(lax.rem(sel, 2), ex_dev), :]
    holds = me == lax.div(sel, 2)
    pick = (lax.broadcasted_iota(jnp.int32, (ex_dev, k_dev), 0) == kept[...]).astype(bf16)
    kept_text = dot_cols(pick, own_text)
    learn_own = as_row(own_score(hat[ex_dev:], kept_text))
    image_own = as_row(own_score(hat[:ex_dev], own_text))
    out[:, n_all : n_all + k_dev] = jnp.where(holds, learn_own, 0.0)
    out[:, n_all + k_dev :] = jnp.where(holds, image_own, 0.0)


def losses_body(a, b, kept, ref_loss, learnability):
    sums = a[...] + b[...]
    k_dev, ex_dev = kept.shape[1], ref_loss.shape[1]
    n_all = ex_dev + k_dev
    losses = jnp.log(sums[:, 0:ex_dev]) - logit_scale * sums[:, n_all + k_dev :]
    ref_loss[...] = losses
    learner = jnp.log(sums[:, ex_dev:n_all]) - logit_scale * sums[:, n_all : n_all + k_dev]
    pick = lax.broadcasted_iota(jnp.int32, (ex_dev, k_dev), 0) == kept[...]
    picked = jnp.sum(jnp.where(pick, as_row_t(losses), 0.0), axis=0, keepdims=True)
    learnability[...] = learner - picked


def as_row_t(row):
    n = row.shape[1]
    return jnp.broadcast_to(row, (n, n)).T[:, 0:1]


def after(value, *others):
    return lax.optimization_barrier((value,) + others)[0] if others else value


class Order:
    def __init__(self):
        self.last = ()

    def wait(self, *values):
        self.last = self.last + values

    def call(self, body, out_shape, cost, *operands, **kwargs):
        operands = list(operands)
        operands[0] = lax.optimization_barrier((operands[0],) + self.last)[0]
        result = call(body, out_shape, cost, **kwargs)(*operands)
        self.last = (result[-1] if isinstance(result, (tuple, list)) else result,)
        return result


def quarter_sel(patches, text, ref_proj, w_up, w_down, kept_index, dest, cotan):
    n_mdl, n_sel = lax.axis_size("mdl"), lax.axis_size("sel")
    n_high = n_sel // 2
    ex_dev, emb_part = text.shape
    emb_full = emb_part * n_mdl
    d_part = patches.shape[1]
    d_full = d_part * n_mdl
    n_patch = patches.shape[0] // ex_dev
    k_dev = kept_index.shape[0]
    n_rows = k_dev * n_patch
    ff_dev = w_up.shape[1]
    blk = d_full // n_sel
    n_share = ex_dev * n_sel // n_mdl
    n_emb = ex_dev + k_dev
    kept_row = kept_index.reshape(1, k_dev)
    dest_row = dest.reshape(1, k_dev)
    order = Order()
    whole = lambda shape: pl.BlockSpec(shape, lambda i: (0,) * len(shape))
    widths = (384, 384, 384, 384)
    starts = [sum(widths[:c]) for c in range(len(widths))]
    row_struct = struct((n_rows, d_full), bf16)
    row_spec = whole((n_rows, d_full))
    mixed_struct = struct((k_dev, d_full), f32)
    mixed_spec = whole((k_dev, d_full))
    small = (2**20, 2**20)

    both, half, pool, texts = order.call(
        functools.partial(pick_body, n_patch),
        (
            struct((2 * d_part, n_rows), bf16),
            struct((d_part // 2, n_rows), bf16),
            struct((d_part, ex_dev), bf16),
            struct((ex_dev + 16, emb_part), bf16),
        ),
        small,
        patches.T,
        cotan.T,
        kept_row,
        dest_row,
        text,
        in_specs=[
            pl.BlockSpec(memory_space=space)
            for space in (pltpu.HBM, pltpu.HBM, pltpu.VMEM, pltpu.VMEM, pltpu.HBM)
        ],
        scratch_shapes=[
            pltpu.VMEM((d_part, ex_dev * n_patch), bf16),
            pltpu.SemaphoreType.DMA((3,)),
        ],
    )
    both_x = swap(both, "mdl", 2)
    both_core = swap(both, "mdl", 1)
    text_pieces = [texts] + [rotate_pairs(texts, s) for s in range(1, n_high)]
    half = lax.optimization_barrier((half, both_core))[0]
    half_pair = swap(half, "sel", 1)
    held_up, held_down = order.call(
        stage_body,
        (struct(w_up.shape, bf16), struct(w_down.shape, bf16)),
        small,
        w_up,
        w_down,
        in_specs=[pl.BlockSpec(memory_space=pltpu.HBM)] * 2,
        scratch_shapes=[pltpu.SemaphoreType.DMA((2,))],
    )
    extras, my_texts = order.call(
        extras_body,
        (
            struct((d_part // 2, n_rows + 2 * ex_dev), bf16),
            struct((n_high * (ex_dev + 16), emb_part), bf16),
        ),
        small,
        half_pair,
        pool,
        *text_pieces,
    )
    both_x = lax.optimization_barrier((both_x, extras))[0]
    both_diag = swap(both_x, "mdl", 1)
    pair_texts = swap(my_texts, "sel", 1)
    extra_pieces = mdl_pieces(extras)
    order.wait(extra_pieces[1])

    def weight_specs(c):
        first, size = starts[c] // widths[c], widths[c]
        if starts[c] % size == 0:
            return [
                pl.BlockSpec((d_full, size), lambda i: (0, first)),
                pl.BlockSpec((size, d_full), lambda i: (first, 0)),
            ]
        start = starts[c]
        return [
            pl.BlockSpec((pl.Element(d_full), pl.Element(size)), lambda i: (0, start)),
            pl.BlockSpec((pl.Element(size), pl.Element(d_full)), lambda i: (start, 0)),
        ]

    pres = [None] * len(widths)
    pair_pres = list(pres)

    def chunk(c, state):
        size = widths[c]
        tok, cot, mixed = state
        cost = (4 * n_rows * d_full * size, 8 * d_full * size)
        pre_struct = struct((n_rows, size), bf16)
        if c == 0:
            pre, mixed, tok_full, tok, cot = order.call(
                functools.partial(first_chunk_body, n_patch, n_mdl),
                (pre_struct, mixed_struct, struct((d_full, n_rows), bf16), row_struct, row_struct),
                cost,
                both,
                both_core,
                both_x,
                both_diag,
                held_up,
                held_down,
                grid=(1,),
                in_specs=[whole((2 * d_part, n_rows))] * 4 + weight_specs(c),
                out_specs=[
                    whole((n_rows, size)),
                    mixed_spec,
                    whole((d_full, n_rows)),
                    row_spec,
                    row_spec,
                ],
                scratch_shapes=[pltpu.VMEM((d_full, n_rows), bf16)],
            )
        else:
            tok_full = None
            pre, mixed = order.call(
                functools.partial(next_chunk_body, n_patch),
                (pre_struct, mixed_struct),
                cost,
                tok,
                cot,
                held_up,
                held_down,
                mixed,
                grid=(1,),
                in_specs=[row_spec, row_spec] + weight_specs(c) + [mixed_spec],
                out_specs=[whole((n_rows, size)), mixed_spec],
            )
        pres[c] = pre
        if c < 2:
            pair_pres[c] = swap(pre, "sel", 1)
        return (tok, cot, mixed), tok_full

    state, tok_full = chunk(0, (None, None, None))
    state, _ = chunk(1, state)

    all_texts, text_send, weights = order.call(
        functools.partial(text_body, k_dev, n_patch),
        (
            struct((ex_dev * n_sel, emb_part), bf16),
            struct((2 * n_share, emb_part), bf16),
            struct((8, 2 * n_rows), f32),
        ),
        small,
        my_texts,
        pair_texts,
    )
    state, _ = chunk(2, state)
    order.wait(extra_pieces[2])
    state, _ = chunk(3, state)

    parts = [None] * len(widths)

    def first_half(c, pair):
        size = widths[c]
        cost = (4 * n_rows * blk * n_high * size, 4 * 2**20)
        halves = (struct((2 * blk, size), f32), struct((2 * blk, size), bf16))
        if c == 0:
            pair, keep, send = order.call(
                first_grad_body,
                (struct((blk * n_high, 2 * n_rows), bf16),) + halves,
                cost,
                tok_full,
                *extra_pieces,
                weights,
                pres[c],
                pair_pres[c],
            )
        else:
            keep, send = order.call(grad_body, halves, cost, pair, pres[c], pair_pres[c])
        parts[c] = [keep, swap(send, "sel", 2)]
        return pair

    def second_half(c):
        if c > 1:
            order.wait(parts[c - 2][1])
        keep, send = order.call(
            add_body,
            (struct((blk, widths[c]), f32), struct((blk, widths[c]), bf16)),
            (2**16, 2**20),
            *parts[c],
        )
        parts[c] = [keep, swap(send, "sel", 4)]

    pair = first_half(0, None)
    mixed = state[2]
    mixed_core = swap(mixed, "mdl", 1)
    first_half(1, pair)
    pair_pres[2] = swap(after(pres[2], parts[1][0]), "sel", 1)
    text_x = swap(after(text_send, parts[1][0]), "mdl", 2)
    mixed = order.call(mix_body, struct((k_dev, d_full), bf16), small, mixed, mixed_core)
    mixed_x = swap(mixed, "mdl", 2)
    second_half(0)
    pair_pres[3] = swap(after(pres[3], parts[0][0]), "sel", 1)
    relay = order.call(
        text_relay_body, struct((2 * n_share, emb_part), bf16), small, all_texts, text_x
    )
    text_core = swap(relay, "mdl", 1)
    emb = order.call(
        functools.partial(heads_body, n_patch),
        struct((n_emb, emb_part), f32),
        small,
        *extra_pieces,
        mixed,
        mixed_x,
        ref_proj,
        scratch_shapes=[pltpu.VMEM((d_full, ex_dev), bf16)],
    )
    emb_pieces = mdl_pieces(emb)
    first_half(2, pair)
    second_half(1)
    share = order.call(
        share_body,
        struct((n_share, emb_full), bf16),
        small,
        all_texts,
        text_x,
        text_core,
        scratch_shapes=[pltpu.VMEM((n_share, emb_full), f32)],
    )
    first_half(3, pair)
    sums = order.call(
        scores_body,
        struct((1, 2 * n_emb), f32),
        small,
        *emb_pieces,
        share,
        kept_row,
        scratch_shapes=[pltpu.VMEM((n_emb, emb_full), f32)],
    )
    sums_core = swap(sums, "mdl", 1)
    second_half(2)
    sums = order.call(mix_body, struct((1, 2 * n_emb), f32), small, sums, sums_core)
    sums_x = swap(sums, "mdl", 2)
    second_half(3)
    ref_loss, learnability = order.call(
        losses_body,
        (struct((1, ex_dev), f32), struct((1, k_dev), f32)),
        small,
        sums,
        sums_x,
        kept_row,
    )
    parts[-1][0], ref_loss, learnability = lax.optimization_barrier(
        (parts[-1][0], ref_loss, learnability)
    )
    grad_up = jnp.concatenate([own + other.astype(f32) for own, other in parts], axis=1)
    return (ref_loss.reshape(ex_dev), learnability.reshape(k_dev), grad_up)


def solution(mesh):
    in_specs = (
        P("sel", "mdl"),
        P("sel", "mdl"),
        P(None, "mdl"),
        P(None, "mdl"),
        P("mdl", None),
        P("sel"),
        P("sel"),
        P("sel", "mdl"),
    )
    out_specs = (P("sel"), P("sel"), P("sel", "mdl"))
    body = quarter_sel if (mesh.shape["sel"], mesh.shape["mdl"]) == (8, 4) else per_device
    return jax.shard_map(
        body, mesh=mesh, in_specs=in_specs, out_specs=out_specs, check_vma=False
    )
```

```python
import functools

import jax
import jax.numpy as jnp
from jax import lax
from jax.experimental import pallas as pl
from jax.experimental.pallas import tpu as pltpu
from jax.sharding import PartitionSpec as P

logit_scale = 64.0
eps = 1e-06
f32 = jnp.float32
bf16 = jnp.bfloat16


def gelu_parts(pre_act):
    cumul = 0.5 * (1.0 + lax.erf(pre_act * 0.7071067811865476))
    density = jnp.exp(-0.5 * pre_act * pre_act) * 0.3989422804014327
    return (pre_act * cumul, cumul + pre_act * density)


def swap(value, axis, bit):
    size = lax.axis_size(axis)
    return lax.ppermute(value, axis, [(i, i ^ bit) for i in range(size)])


def rotate_pairs(value, step):
    size = lax.axis_size("sel")
    return lax.ppermute(value, "sel", [(i, (i + 2 * step) % size) for i in range(size)])


def mdl_pieces(value):
    n = lax.axis_size("mdl")
    out = [value] + [None] * (n - 1)
    top = n // 2
    if n == 1:
        return out
    out[top] = swap(value, "mdl", top)
    low = top // 2
    have = [0, top]
    while low:
        for j in list(have):
            out[j | low] = swap(out[j], "mdl", low)
            have.append(j | low)
        low //= 2
    return out


def in_order(pieces, axis):
    me = lax.axis_index("mdl")
    bit = 1
    while bit < lax.axis_size("mdl"):
        set_bit = (me & bit) != 0
        merged = []
        for j in range(0, len(pieces), 2):
            first, second = pieces[j], pieces[j + 1]
            merged.append(
                jnp.where(
                    set_bit,
                    jnp.concatenate([second, first], axis),
                    jnp.concatenate([first, second], axis),
                )
            )
        pieces = merged
        bit *= 2
    return pieces[0]


def mdl_sum(value):
    bit = 1
    while bit < lax.axis_size("mdl"):
        value = value + swap(value, "mdl", bit)
        bit *= 2
    return value


def unit_rows(values):
    norm_sq = jnp.sum(values * values, axis=1)
    return (values * lax.rsqrt(norm_sq + eps)[:, None]).astype(bf16)


def exp_total(rows_full, texts):
    scores = lax.dot_general(
        rows_full, texts, (((1,), (1,)), ((), ())), preferred_element_type=f32
    )
    return jnp.sum(jnp.exp(logit_scale * scores), axis=1)


def own_product(rows, texts):
    return jnp.sum(rows.astype(f32) * texts.astype(f32), axis=1)


def per_device(patches, text, ref_proj, w_up, w_down, kept_index, dest, cotan):
    n_sel = lax.axis_size("sel")
    n_mdl = lax.axis_size("mdl")
    ex_dev = text.shape[0]
    d_part = patches.shape[1]
    n_patch = patches.shape[0] // ex_dev
    k_dev = kept_index.shape[0]
    n_rows = k_dev * n_patch
    ff_dev = w_up.shape[1]
    n_high = n_sel // 2
    rotations = n_high <= 4
    sel_me, mdl_me = lax.axis_index("sel"), lax.axis_index("mdl")
    pair_me, high_me = sel_me % 2, sel_me // 2

    patches_t = patches.T
    row_of = (kept_index[:, None] * n_patch + jnp.arange(n_patch)[None, :]).reshape(-1)
    pick = (jnp.arange(ex_dev * n_patch)[:, None] == row_of[None, :]).astype(bf16)
    tok_t = jnp.dot(patches_t, pick, preferred_element_type=f32).astype(bf16)
    cot_t = cotan.T
    blk = d_part * n_mdl // n_sel
    halves = tok_t.reshape(d_part // (2 * blk), 2, blk, n_rows)
    send_half = lax.dynamic_index_in_dim(halves, 1 - pair_me, 1, keepdims=False)
    recv_half = swap(send_half.reshape(d_part // 2, n_rows), "sel", 1)

    tok_full = in_order(mdl_pieces(tok_t), 0)
    cot_full = in_order(mdl_pieces(cot_t), 0)
    recv_half_full = in_order(mdl_pieces(recv_half), 0)
    n_blk = d_part * n_mdl // (2 * blk)
    own_half_full = lax.dynamic_index_in_dim(
        tok_full.reshape(n_blk, 2, blk, n_rows), pair_me, 1, keepdims=False
    ).reshape(n_blk * blk, n_rows)
    tok_pair = jnp.concatenate([own_half_full, recv_half_full], axis=1)

    counts = jnp.sum((dest[:, None] == jnp.arange(n_sel)[None, :]).astype(f32), axis=0)
    if rotations:
        pair_counts = counts + swap(counts, "sel", 1)
        counts = pair_counts
        for step in range(1, n_high):
            counts = counts + rotate_pairs(pair_counts, step)
    else:
        counts = lax.psum(counts, "sel")
    row_weight = 1.0 / jnp.repeat(counts[dest], n_patch)

    text_full = in_order(mdl_pieces(text), 1).astype(f32)
    text_hat = unit_rows(text_full)
    share = ex_dev // n_mdl
    text_share = lax.dynamic_slice_in_dim(text_hat, mdl_me * share, share, 0)
    if rotations:
        pair_share = jnp.concatenate([text_share, swap(text_share, "sel", 1)], axis=0)
        text_split = jnp.concatenate(
            [pair_share] + [rotate_pairs(pair_share, s) for s in range(1, n_high)], axis=0
        )
    else:
        text_split = lax.all_gather(text_share, "sel", axis=0, tiled=True)

    pooled_t = (
        jnp.sum(patches_t.reshape(d_part, ex_dev, n_patch).astype(f32), axis=2) * (1.0 / n_patch)
    ).astype(bf16)
    pooled_full = in_order(mdl_pieces(pooled_t), 0)
    img_emb = lax.dot_general(
        pooled_full, ref_proj, (((0,), (0,)), ((), ())), preferred_element_type=f32
    )
    img_hat = unit_rows(in_order(mdl_pieces(img_emb), 1))
    ref_own = own_product(img_hat, text_hat)
    ref_part = exp_total(img_hat, text_split)

    pre_act = lax.dot_general(
        tok_full, w_up, (((0,), (0,)), ((), ())), preferred_element_type=f32
    )
    activated, gelu_slope = gelu_parts(pre_act)
    hidden = activated.astype(bf16)
    mixed = jnp.dot(hidden, w_down, preferred_element_type=f32)
    mixed_pool = mdl_sum(jnp.sum(mixed.reshape(k_dev, n_patch, -1), axis=1))
    tok_pool = jnp.sum(tok_full.reshape(-1, k_dev, n_patch).astype(f32), axis=2).T
    learn_pool = ((mixed_pool + tok_pool) * (1.0 / n_patch)).astype(bf16)
    learn_emb = jnp.dot(learn_pool, ref_proj, preferred_element_type=f32)
    learn_hat = unit_rows(in_order(mdl_pieces(learn_emb), 1))
    kept_text = text_hat[kept_index]
    learn_own = own_product(learn_hat, kept_text)
    learn_part = exp_total(learn_hat, text_split)
    totals = mdl_sum(jnp.concatenate([ref_part, learn_part]))
    ref_loss = jnp.log(totals[:ex_dev]) - logit_scale * ref_own
    learner_loss = jnp.log(totals[ex_dev:]) - logit_scale * learn_own
    learnability = learner_loss - ref_loss[kept_index]

    n_chunks = 4
    width = ff_dev // n_chunks
    outs = []
    for c in range(n_chunks):
        cols = slice(c * width, (c + 1) * width)
        grad_act = lax.dot_general(
            cot_full, w_down[cols], (((0,), (1,)), ((), ())), preferred_element_type=f32
        )
        grad_pre = (grad_act * row_weight[:, None] * gelu_slope[:, cols]).astype(bf16)
        pair_pre = jnp.concatenate([grad_pre, swap(grad_pre, "sel", 1)], axis=0)
        part = jnp.dot(tok_pair, pair_pre, preferred_element_type=f32)
        part = part.reshape(n_high, blk, width)
        if rotations:
            total = lax.dynamic_index_in_dim(part, high_me, 0, keepdims=False)
            for step in range(1, n_high):
                block = lax.dynamic_index_in_dim(
                    part, (high_me + step) % n_high, 0, keepdims=False
                )
                total = total + rotate_pairs(block.astype(bf16), step).astype(f32)
        else:
            total = lax.psum_scatter(
                part,
                "sel",
                scatter_dimension=0,
                axis_index_groups=[list(range(p, n_sel, 2)) for p in range(2)],
                tiled=False,
            )
        outs.append(total)
    grad_up = jnp.concatenate(outs, axis=1)
    return (ref_loss, learnability, grad_up)


def dot_f32(a, b):
    return jnp.dot(a, b, preferred_element_type=f32)


def dot_rows(a, b):
    return lax.dot_general(a, b, (((1,), (1,)), ((), ())), preferred_element_type=f32)


def dot_cols(a, b):
    return lax.dot_general(a, b, (((0,), (0,)), ((), ())), preferred_element_type=f32)


def group_mask(n_items, n_patch):
    shape = (n_items, n_items * n_patch)
    row = lax.broadcasted_iota(jnp.int32, shape, 1)
    first = n_patch * lax.broadcasted_iota(jnp.int32, shape, 0)
    return (row >= first) & (row < first + n_patch), row - first


def as_row(column):
    n = column.shape[0]
    return jnp.broadcast_to(column, (n, n)).T[0:1]


def place(index, length):
    return pl.ds(pl.multiple_of(index * length, length), length)


def call(body, out_shape, cost, grid=(), vmem=24 * 2**20, **kwargs):
    flops, moved = cost
    return pl.pallas_call(
        body,
        out_shape=out_shape,
        grid=grid,
        cost_estimate=pl.CostEstimate(flops=1, bytes_accessed=1, transcendentals=0),
        compiler_params=pltpu.CompilerParams(vmem_limit_bytes=vmem),
        **kwargs,
    )


def struct(shape, dtype):
    return jax.ShapeDtypeStruct(shape, dtype)


def pick_body(
    n_patch, patches_hbm, cot_hbm, kept, dest, text_hbm, both, half, pool, texts, patches, sems
):
    d_part, n_all = patches.shape
    ex_dev = n_all // n_patch
    copies = [
        pltpu.make_async_copy(patches_hbm, patches, sems.at[0]),
        pltpu.make_async_copy(cot_hbm, both.at[pl.ds(d_part, d_part), :], sems.at[1]),
        pltpu.make_async_copy(text_hbm, texts.at[pl.ds(0, ex_dev), :], sems.at[2]),
    ]
    for copy in copies:
        copy.start()
    k_dev = kept.shape[1]
    member, offset = group_mask(k_dev, n_patch)
    expand = member.astype(bf16)
    index = jnp.broadcast_to(kept[...].astype(f32), (8, k_dev)).astype(bf16)
    base = dot_f32(index, expand)[0:1].astype(jnp.int32)
    row = base * n_patch + jnp.sum(jnp.where(member, offset, 0), axis=0, keepdims=True)
    pick = (lax.broadcasted_iota(jnp.int32, (n_all, row.shape[1]), 0) == row).astype(bf16)
    for copy in copies:
        copy.wait()
    values = patches[...]
    both[0:d_part, :] = dot_f32(values, pick).astype(bf16)
    other = 1 - lax.rem(lax.axis_index("sel"), 2)
    half[...] = both[place(other, d_part // 2), :]
    texts[ex_dev:, :] = jnp.zeros((16, texts.shape[1]), bf16)
    texts[ex_dev:, 0:k_dev] = jnp.broadcast_to(dest[...].astype(f32), (16, k_dev)).astype(bf16)
    groups, _ = group_mask(ex_dev, n_patch)
    pool[...] = (dot_rows(values, groups.astype(bf16)) * (1.0 / n_patch)).astype(bf16)


def extras_body(half, pool, t0, t1, t2, t3, extras, texts):
    n_half, n_rows = half.shape
    n_ex = pool.shape[1]
    extras[:, 0:n_rows] = half[...]
    extras[:, n_rows : n_rows + n_ex] = pool[0:n_half, :]
    extras[:, n_rows + n_ex :] = pool[n_half:, :]
    n_text = t0.shape[0]
    for r, piece in enumerate((t0, t1, t2, t3)):
        texts[r * n_text : (r + 1) * n_text, :] = piece[...]


def text_body(k_dev, n_patch, mine, theirs, whole, send, weights):
    n_high = 4
    n_text = mine.shape[0] // n_high
    ex_dev = n_text - 16
    me = lax.axis_index("mdl")
    sel = lax.axis_index("sel")
    parity, high = lax.rem(sel, 2), lax.div(sel, 2)
    shard = lax.broadcasted_iota(jnp.int32, (128, k_dev), 0).astype(f32)
    ones = jnp.ones((8, k_dev), bf16)
    counts = jnp.zeros((8, 128), f32)
    named = []
    for which, place_in_pair in ((mine, parity), (theirs, 1 - parity)):
        for r in range(n_high):
            source = lax.rem(high + n_high - r, n_high)
            rows = place(source * 2 + place_in_pair, ex_dev)
            whole[rows, :] = which[r * n_text : r * n_text + ex_dev, :]
            dest = which[r * n_text + ex_dev : (r + 1) * n_text, 0:k_dev].astype(f32)[0:1]
            is_dest = (shard == dest).astype(bf16)
            counts = counts + dot_rows(ones, is_dest)
            if r == 0:
                named.append(is_dest)
    member = group_mask(k_dev, n_patch)[0].astype(bf16)
    n_rows = k_dev * n_patch
    for i, is_dest in enumerate(named):
        count = dot_f32(counts.astype(bf16), is_dest).astype(bf16)
        weights[:, i * n_rows : (i + 1) * n_rows] = 1.0 / dot_f32(count, member)
    for i in range(2):
        send[i * 2 * ex_dev : (i + 1) * 2 * ex_dev, :] = whole[place(me ^ (2 + i), 2 * ex_dev), :]


def text_relay_body(whole, received, send):
    n_share = received.shape[0] // 2
    send[0:n_share, :] = whole[place(lax.axis_index("mdl") ^ 1, n_share), :]
    send[n_share:, :] = received[n_share:, :]


def share_body(whole, from_x, from_core, share, values):
    n_share, width = share.shape[0], whole.shape[1]
    me = lax.axis_index("mdl")
    pieces = (
        whole[place(me, n_share), :],
        from_core[0:n_share, :],
        from_x[0:n_share, :],
        from_core[n_share:, :],
    )
    for j, piece in enumerate(pieces):
        values[:, place(me ^ j, width)] = piece.astype(f32)
    rows = values[...]
    norm_sq = jnp.sum(rows * rows, axis=1, keepdims=True)
    share[...] = (rows * lax.rsqrt(norm_sq + eps)).astype(bf16)


def stage_body(up, down, up_held, down_held, sems):
    copies = [
        pltpu.make_async_copy(up, up_held, sems.at[0]),
        pltpu.make_async_copy(down, down_held, sems.at[1]),
    ]
    for copy in copies:
        copy.start()
    for copy in copies:
        copy.wait()


def chunk_work(n_patch, tok, cot, w_up, w_down, pre, mixed):
    k_dev = tok.shape[0] // n_patch
    groups = group_mask(k_dev, n_patch)[0].astype(bf16)
    pre_act = dot_f32(tok[...], w_up[...])
    activated, gelu_slope = gelu_parts(pre_act)
    pre[...] = (dot_rows(cot[...], w_down[...]) * gelu_slope).astype(bf16)
    pooled = dot_f32(groups, activated.astype(bf16))
    high = pooled.astype(bf16)
    low = (pooled - high.astype(f32)).astype(bf16)
    both = dot_f32(jnp.concatenate([high, low], axis=0), w_down[...])
    return mixed + (both[:k_dev] + both[k_dev:])


def first_chunk_body(
    n_patch, n_mdl, b0, b1, b2, b3, w_up, w_down, pre, mixed, tok_full, tok, cot, cot_full
):
    d_part, n_rows = b0.shape[0] // 2, b0.shape[1]
    groups = group_mask(n_rows // n_patch, n_patch)[0].astype(bf16)
    me = lax.axis_index("mdl")
    for j, piece in enumerate((b0, b1, b2, b3)):
        tok_full[place(me ^ j, d_part), :] = piece[0:d_part, :]
        cot_full[place(me ^ j, d_part), :] = piece[d_part:, :]
    tok[...] = tok_full[...].T
    cot[...] = cot_full[...].T
    start = dot_f32(groups, tok[...]) * (1.0 / n_mdl)
    mixed[...] = chunk_work(n_patch, tok, cot, w_up, w_down, pre, start)


def next_chunk_body(n_patch, tok, cot, w_up, w_down, mixed_in, pre, mixed):
    mixed[...] = chunk_work(n_patch, tok, cot, w_up, w_down, pre, mixed_in[...])


def split_part(part, keep, send):
    n_keep = keep.shape[0]
    keep[...] = part[:n_keep]
    send[...] = part[n_keep:].astype(bf16)


def first_grad_body(tok_full, h0, h1, h2, h3, weights, pre, pre_pair, pair, keep, send):
    n_rows = tok_full.shape[1]
    blk = h0.shape[0]
    me = lax.axis_index("mdl")
    sel = lax.axis_index("sel")
    parity, high = lax.rem(sel, 2), lax.div(sel, 2)
    for j, piece in enumerate((h0, h1, h2, h3)):
        block = me ^ j
        apart = block ^ high
        rows = place(2 * lax.rem(apart, 2) + lax.div(apart, 2), blk)
        own_tok = tok_full[place(2 * block + parity, blk), :].astype(f32)
        pair[rows, 0:n_rows] = (own_tok * weights[0:1, 0:n_rows]).astype(bf16)
        pair_tok = piece[:, 0:n_rows].astype(f32)
        pair[rows, n_rows:] = (pair_tok * weights[0:1, n_rows:]).astype(bf16)
    grad_body(pair, pre, pre_pair, keep, send)


def grad_body(pair, pre, pre_pair, keep, send):
    n_rows = pre.shape[0]
    part = dot_f32(pair[:, 0:n_rows], pre[...]) + dot_f32(pair[:, n_rows:], pre_pair[...])
    split_part(part, keep, send)


def add_body(held, received, keep, send):
    split_part(held[...] + received[...].astype(f32), keep, send)


def mix_body(a, b, total):
    total[...] = (a[...] + b[...]).astype(total.dtype)


def heads_body(n_patch, h0, h1, h2, h3, a, b, ref_proj, emb, pooled):
    me = lax.axis_index("mdl")
    n_rows = h0.shape[0]
    n_ex = pooled.shape[1]
    first = h0.shape[1] - 2 * n_ex
    for j, piece in enumerate((h0, h1, h2, h3)):
        for part in range(2):
            pooled[place((me ^ j) * 2 + part, n_rows), :] = piece[
                :, first + part * n_ex : first + (part + 1) * n_ex
            ]
    learn_pool = ((a[...].astype(f32) + b[...].astype(f32)) * (1.0 / n_patch)).astype(bf16)
    emb[0:n_ex, :] = dot_cols(pooled[...], ref_proj[...])
    emb[n_ex:, :] = dot_f32(learn_pool, ref_proj[...])


def own_score(hat, texts):
    return jnp.sum(hat.astype(f32) * texts.astype(f32), axis=1, keepdims=True)


def scores_body(e0, e1, e2, e3, share, kept, out, whole):
    me = lax.axis_index("mdl")
    sel = lax.axis_index("sel")
    width = e0.shape[1]
    for j, piece in enumerate((e0, e1, e2, e3)):
        whole[:, place(me ^ j, width)] = piece[...]
    values = whole[...]
    norm_sq = jnp.sum(values * values, axis=1, keepdims=True)
    hat = (values * lax.rsqrt(norm_sq + eps)).astype(bf16)
    k_dev = kept.shape[1]
    n_all = hat.shape[0]
    ex_dev = n_all - k_dev
    scores = dot_rows(share[...], hat)
    out[:, 0:n_all] = jnp.sum(jnp.exp(logit_scale * scores), axis=0, keepdims=True)
    own_text = share[place(lax.rem(sel, 2), ex_dev), :]
    holds = me == lax.div(sel, 2)
    pick = (lax.broadcasted_iota(jnp.int32, (ex_dev, k_dev), 0) == kept[...]).astype(bf16)
    kept_text = dot_cols(pick, own_text)
    learn_own = as_row(own_score(hat[ex_dev:], kept_text))
    image_own = as_row(own_score(hat[:ex_dev], own_text))
    out[:, n_all : n_all + k_dev] = jnp.where(holds, learn_own, 0.0)
    out[:, n_all + k_dev :] = jnp.where(holds, image_own, 0.0)


def losses_body(a, b, kept, ref_loss, learnability):
    sums = a[...] + b[...]
    k_dev, ex_dev = kept.shape[1], ref_loss.shape[1]
    n_all = ex_dev + k_dev
    losses = jnp.log(sums[:, 0:ex_dev]) - logit_scale * sums[:, n_all + k_dev :]
    ref_loss[...] = losses
    learner = jnp.log(sums[:, ex_dev:n_all]) - logit_scale * sums[:, n_all : n_all + k_dev]
    pick = lax.broadcasted_iota(jnp.int32, (ex_dev, k_dev), 0) == kept[...]
    picked = jnp.sum(jnp.where(pick, as_row_t(losses), 0.0), axis=0, keepdims=True)
    learnability[...] = learner - picked


def as_row_t(row):
    n = row.shape[1]
    return jnp.broadcast_to(row, (n, n)).T[:, 0:1]


def after(value, *others):
    return lax.optimization_barrier((value,) + others)[0] if others else value


def quarter_sel(patches, text, ref_proj, w_up, w_down, kept_index, dest, cotan):
    n_mdl, n_sel = lax.axis_size("mdl"), lax.axis_size("sel")
    n_high = n_sel // 2
    ex_dev, emb_part = text.shape
    emb_full = emb_part * n_mdl
    d_part = patches.shape[1]
    d_full = d_part * n_mdl
    n_patch = patches.shape[0] // ex_dev
    k_dev = kept_index.shape[0]
    n_rows = k_dev * n_patch
    ff_dev = w_up.shape[1]
    blk = d_full // n_sel
    n_share = ex_dev * n_sel // n_mdl
    n_emb = ex_dev + k_dev
    kept_row = kept_index.reshape(1, k_dev)
    dest_row = dest.reshape(1, k_dev)
    size = ff_dev // 4
    whole = lambda shape: pl.BlockSpec(shape, lambda i: (0,) * len(shape))
    row_struct = struct((n_rows, d_full), bf16)
    row_spec = whole((n_rows, d_full))
    mixed_struct = struct((k_dev, d_full), f32)
    mixed_spec = whole((k_dev, d_full))
    pre_struct = struct((n_rows, size), bf16)
    pre_spec = whole((n_rows, size))
    halves = (struct((2 * blk, size), f32), struct((2 * blk, size), bf16))

    def run(ties, body, out_shape, *operands, **kwargs):
        first = after(operands[0], *ties)
        return call(body, out_shape, (2**20, 2**20), **kwargs)(first, *operands[1:])

    def pick(ties):
        return run(
            ties,
            functools.partial(pick_body, n_patch),
            (
                struct((2 * d_part, n_rows), bf16),
                struct((d_part // 2, n_rows), bf16),
                struct((d_part, ex_dev), bf16),
                struct((ex_dev + 16, emb_part), bf16),
            ),
            patches.T,
            cotan.T,
            kept_row,
            dest_row,
            text,
            in_specs=[
                pl.BlockSpec(memory_space=space)
                for space in (pltpu.HBM, pltpu.HBM, pltpu.VMEM, pltpu.VMEM, pltpu.HBM)
            ],
            scratch_shapes=[
                pltpu.VMEM((d_part, ex_dev * n_patch), bf16),
                pltpu.SemaphoreType.DMA((3,)),
            ],
            vmem=60 * 2**20,
        )


    def stage(ties):
        return run(
            ties,
            stage_body,
            (struct(w_up.shape, bf16), struct(w_down.shape, bf16)),
            w_up,
            w_down,
            in_specs=[pl.BlockSpec(memory_space=pltpu.HBM)] * 2,
            scratch_shapes=[pltpu.SemaphoreType.DMA((2,))],
            vmem=40 * 2**20,
        )


    def make_extras(ties, half_pair, pool, texts):
        rotated = [rotate_pairs(texts, s) for s in range(1, n_high)]
        return run(
            ties,
            extras_body,
            (
                struct((d_part // 2, n_rows + 2 * ex_dev), bf16),
                struct((n_high * (ex_dev + 16), emb_part), bf16),
            ),
            half_pair,
            pool,
            texts,
            *rotated,
        )


    def weight_specs(c):
        return [
            pl.BlockSpec((d_full, size), lambda i: (0, c)),
            pl.BlockSpec((size, d_full), lambda i: (c, 0)),
        ]


    def forward_first(ties, *operands):
        return run(
            ties,
            functools.partial(first_chunk_body, n_patch, n_mdl),
            (pre_struct, mixed_struct, struct((d_full, n_rows), bf16), row_struct, row_struct),
            *operands,
            grid=(1,),
            in_specs=[whole((2 * d_part, n_rows))] * 4 + weight_specs(0),
            out_specs=[pre_spec, mixed_spec, whole((d_full, n_rows)), row_spec, row_spec],
            scratch_shapes=[pltpu.VMEM((d_full, n_rows), bf16)],
        )

    def forward(ties, c, tok, cot, held_up, held_down, mixed):
        return run(
            ties,
            functools.partial(next_chunk_body, n_patch),
            (pre_struct, mixed_struct),
            tok,
            cot,
            held_up,
            held_down,
            mixed,
            grid=(1,),
            in_specs=[row_spec, row_spec] + weight_specs(c) + [mixed_spec],
            out_specs=[pre_spec, mixed_spec],
        )


    def all_shards(ties, my_texts, pair_texts):
        return run(
            ties,
            functools.partial(text_body, k_dev, n_patch),
            (
                struct((ex_dev * n_sel, emb_part), bf16),
                struct((2 * n_share, emb_part), bf16),
                struct((8, 2 * n_rows), f32),
            ),
            my_texts,
            pair_texts,
        )

    def grad_first(ties, *operands):
        pair_struct = struct((blk * n_high, 2 * n_rows), bf16)
        return run(ties, first_grad_body, (pair_struct,) + halves, *operands)

    def grad(ties, *operands):
        return run(ties, grad_body, halves, *operands)

    def add(ties, keep, received):
        structs = (struct((blk, size), f32), struct((blk, size), bf16))
        return run(ties, add_body, structs, keep, received)

    def relay_text(ties, all_texts, text_x):
        send = struct((2 * n_share, emb_part), bf16)
        return run(ties, text_relay_body, send, all_texts, text_x)

    def share_text(ties, *operands):
        return run(
            ties,
            share_body,
            struct((n_share, emb_full), bf16),
            *operands,
            scratch_shapes=[pltpu.VMEM((n_share, emb_full), f32)],
        )

    def heads(ties, *operands):
        return run(
            ties,
            functools.partial(heads_body, n_patch),
            struct((n_emb, emb_part), f32),
            *operands,
            ref_proj,
            scratch_shapes=[pltpu.VMEM((d_full, ex_dev), bf16)],
        )

    def scores(ties, *operands):
        return run(
            ties,
            scores_body,
            struct((1, 2 * n_emb), f32),
            *operands,
            kept_row,
            scratch_shapes=[pltpu.VMEM((n_emb, emb_full), f32)],
        )

    def losses(ties, total, total_x):
        structs = (struct((1, ex_dev), f32), struct((1, k_dev), f32))
        return run(ties, losses_body, structs, total, total_x, kept_row)


    both, half, pool, texts = pick(())
    both_x = swap(both, "mdl", 2)
    both_core = swap(both, "mdl", 1)
    half_pair = swap(half, "sel", 1)
    held_up, held_down = stage((texts,))
    extras, my_texts = make_extras((held_down,), half_pair, pool, texts)
    both_diag = swap(after(both_x, extras), "mdl", 1)
    extras_x = swap(extras, "mdl", 2)
    extras_core = swap(extras, "mdl", 1)
    extras_diag = swap(extras_x, "mdl", 1)
    pair_texts = swap(my_texts, "sel", 1)
    pre0, mixed0, tok_full, tok, cot = forward_first(
        (my_texts, extras_core),
        both,
        both_core,
        both_x,
        both_diag,
        held_up,
        held_down,
    )
    pair_pre0 = swap(pre0, "sel", 1)
    all_texts, text_send, weights = all_shards((cot,), my_texts, pair_texts)
    text_x = swap(text_send, "mdl", 2)
    pre1, mixed1 = forward((weights,), 1, tok, cot, held_up, held_down, mixed0)
    pair_pre1 = swap(pre1, "sel", 1)
    pre2, mixed2 = forward((mixed1,), 2, tok, cot, held_up, held_down, mixed1)
    pair_pre2 = swap(pre2, "sel", 1)
    pre3, mixed = forward((mixed2, extras_x), 3, tok, cot, held_up, held_down, mixed2)
    mixed_core = swap(mixed, "mdl", 1)
    pair, keep0, send0 = grad_first(
        (mixed,),
        tok_full,
        extras,
        extras_core,
        extras_x,
        extras_diag,
        weights,
        pre0,
        pair_pre0,
    )
    first0 = swap(send0, "sel", 2)
    keep1, send1 = grad((send0,), pair, pre1, pair_pre1)
    first1 = swap(send1, "sel", 2)
    mixsum = run((send1,), mix_body, struct((k_dev, d_full), bf16), mixed, mixed_core)
    mixsum_x = swap(mixsum, "mdl", 2)
    own0, rest0 = add((mixsum,), keep0, first0)
    pair_pre3 = swap(after(pre3, own0), "sel", 1)
    second0 = swap(rest0, "sel", 4)
    relay = relay_text((rest0,), all_texts, text_x)
    text_core = swap(relay, "mdl", 1)
    emb = heads((relay,), extras, extras_core, extras_x, extras_diag, mixsum, mixsum_x)
    emb_x = swap(emb, "mdl", 2)
    emb_core = swap(emb, "mdl", 1)
    emb_diag = swap(emb_x, "mdl", 1)
    keep2, send2 = grad((emb,), pair, pre2, pair_pre2)
    first2 = swap(send2, "sel", 2)
    own1, rest1 = add((send2,), keep1, first1)
    second1 = swap(rest1, "sel", 4)
    share = share_text((rest1,), all_texts, text_x, text_core)
    keep3, send3 = grad((share,), pair, pre3, pair_pre3)
    first3 = swap(send3, "sel", 2)
    sums = scores((send3,), emb, emb_core, emb_x, emb_diag, share)
    sums_core = swap(sums, "mdl", 1)
    own2, rest2 = add((sums, second0), keep2, first2)
    second2 = swap(rest2, "sel", 4)
    total = run((rest2,), mix_body, struct((1, 2 * n_emb), f32), sums, sums_core)
    total_x = swap(total, "mdl", 2)
    own3, rest3 = add((total, second1), keep3, first3)
    second3 = swap(rest3, "sel", 4)
    ref_loss, learnability = losses((rest3,), total, total_x)

    own3, ref_loss, learnability = lax.optimization_barrier((own3, ref_loss, learnability))
    sums = [
        (own0, second0),
        (own1, second1),
        (own2, second2),
        (own3, second3),
    ]
    grad_up = jnp.concatenate([own + other.astype(f32) for own, other in sums], axis=1)
    return (ref_loss.reshape(ex_dev), learnability.reshape(k_dev), grad_up)


def solution(mesh):
    in_specs = (
        P("sel", "mdl"),
        P("sel", "mdl"),
        P(None, "mdl"),
        P(None, "mdl"),
        P("mdl", None),
        P("sel"),
        P("sel"),
        P("sel", "mdl"),
    )
    out_specs = (P("sel"), P("sel"), P("sel", "mdl"))
    body = quarter_sel if (mesh.shape["sel"], mesh.shape["mdl"]) == (8, 4) else per_device
    return jax.shard_map(
        body, mesh=mesh, in_specs=in_specs, out_specs=out_specs, check_vma=False
    )
```

```python
import functools

import jax
import jax.numpy as jnp
from jax import lax
from jax.experimental import pallas as pl
from jax.experimental.pallas import tpu as pltpu
from jax.sharding import PartitionSpec as P

logit_scale = 64.0
eps = 1e-06
f32 = jnp.float32
bf16 = jnp.bfloat16


def gelu_parts(pre_act):
    cumul = 0.5 * (1.0 + lax.erf(pre_act * 0.7071067811865476))
    density = jnp.exp(-0.5 * pre_act * pre_act) * 0.3989422804014327
    return (pre_act * cumul, cumul + pre_act * density)


def swap(value, axis, bit):
    size = lax.axis_size(axis)
    return lax.ppermute(value, axis, [(i, i ^ bit) for i in range(size)])


def rotate_pairs(value, step):
    size = lax.axis_size("sel")
    return lax.ppermute(value, "sel", [(i, (i + 2 * step) % size) for i in range(size)])


def mdl_pieces(value):
    n = lax.axis_size("mdl")
    out = [value] + [None] * (n - 1)
    top = n // 2
    if n == 1:
        return out
    out[top] = swap(value, "mdl", top)
    low = top // 2
    have = [0, top]
    while low:
        for j in list(have):
            out[j | low] = swap(out[j], "mdl", low)
            have.append(j | low)
        low //= 2
    return out


def in_order(pieces, axis):
    me = lax.axis_index("mdl")
    bit = 1
    while bit < lax.axis_size("mdl"):
        set_bit = (me & bit) != 0
        merged = []
        for j in range(0, len(pieces), 2):
            first, second = pieces[j], pieces[j + 1]
            merged.append(
                jnp.where(
                    set_bit,
                    jnp.concatenate([second, first], axis),
                    jnp.concatenate([first, second], axis),
                )
            )
        pieces = merged
        bit *= 2
    return pieces[0]


def mdl_sum(value):
    bit = 1
    while bit < lax.axis_size("mdl"):
        value = value + swap(value, "mdl", bit)
        bit *= 2
    return value


def unit_rows(values):
    norm_sq = jnp.sum(values * values, axis=1)
    return (values * lax.rsqrt(norm_sq + eps)[:, None]).astype(bf16)


def exp_total(rows_full, texts):
    scores = lax.dot_general(
        rows_full, texts, (((1,), (1,)), ((), ())), preferred_element_type=f32
    )
    return jnp.sum(jnp.exp(logit_scale * scores), axis=1)


def own_product(rows, texts):
    return jnp.sum(rows.astype(f32) * texts.astype(f32), axis=1)


def per_device(patches, text, ref_proj, w_up, w_down, kept_index, dest, cotan):
    n_sel = lax.axis_size("sel")
    n_mdl = lax.axis_size("mdl")
    ex_dev = text.shape[0]
    d_part = patches.shape[1]
    n_patch = patches.shape[0] // ex_dev
    k_dev = kept_index.shape[0]
    n_rows = k_dev * n_patch
    ff_dev = w_up.shape[1]
    n_high = n_sel // 2
    rotations = n_high <= 4
    sel_me, mdl_me = lax.axis_index("sel"), lax.axis_index("mdl")
    pair_me, high_me = sel_me % 2, sel_me // 2

    patches_t = patches.T
    row_of = (kept_index[:, None] * n_patch + jnp.arange(n_patch)[None, :]).reshape(-1)
    pick = (jnp.arange(ex_dev * n_patch)[:, None] == row_of[None, :]).astype(bf16)
    tok_t = jnp.dot(patches_t, pick, preferred_element_type=f32).astype(bf16)
    cot_t = cotan.T
    blk = d_part * n_mdl // n_sel
    halves = tok_t.reshape(d_part // (2 * blk), 2, blk, n_rows)
    send_half = lax.dynamic_index_in_dim(halves, 1 - pair_me, 1, keepdims=False)
    recv_half = swap(send_half.reshape(d_part // 2, n_rows), "sel", 1)

    tok_full = in_order(mdl_pieces(tok_t), 0)
    cot_full = in_order(mdl_pieces(cot_t), 0)
    recv_half_full = in_order(mdl_pieces(recv_half), 0)
    n_blk = d_part * n_mdl // (2 * blk)
    own_half_full = lax.dynamic_index_in_dim(
        tok_full.reshape(n_blk, 2, blk, n_rows), pair_me, 1, keepdims=False
    ).reshape(n_blk * blk, n_rows)
    tok_pair = jnp.concatenate([own_half_full, recv_half_full], axis=1)

    counts = jnp.sum((dest[:, None] == jnp.arange(n_sel)[None, :]).astype(f32), axis=0)
    if rotations:
        pair_counts = counts + swap(counts, "sel", 1)
        counts = pair_counts
        for step in range(1, n_high):
            counts = counts + rotate_pairs(pair_counts, step)
    else:
        counts = lax.psum(counts, "sel")
    row_weight = 1.0 / jnp.repeat(counts[dest], n_patch)

    text_full = in_order(mdl_pieces(text), 1).astype(f32)
    text_hat = unit_rows(text_full)
    share = ex_dev // n_mdl
    text_share = lax.dynamic_slice_in_dim(text_hat, mdl_me * share, share, 0)
    if rotations:
        pair_share = jnp.concatenate([text_share, swap(text_share, "sel", 1)], axis=0)
        text_split = jnp.concatenate(
            [pair_share] + [rotate_pairs(pair_share, s) for s in range(1, n_high)], axis=0
        )
    else:
        text_split = lax.all_gather(text_share, "sel", axis=0, tiled=True)

    pooled_t = (
        jnp.sum(patches_t.reshape(d_part, ex_dev, n_patch).astype(f32), axis=2) * (1.0 / n_patch)
    ).astype(bf16)
    pooled_full = in_order(mdl_pieces(pooled_t), 0)
    img_emb = lax.dot_general(
        pooled_full, ref_proj, (((0,), (0,)), ((), ())), preferred_element_type=f32
    )
    img_hat = unit_rows(in_order(mdl_pieces(img_emb), 1))
    ref_own = own_product(img_hat, text_hat)
    ref_part = exp_total(img_hat, text_split)

    pre_act = lax.dot_general(
        tok_full, w_up, (((0,), (0,)), ((), ())), preferred_element_type=f32
    )
    activated, gelu_slope = gelu_parts(pre_act)
    hidden = activated.astype(bf16)
    mixed = jnp.dot(hidden, w_down, preferred_element_type=f32)
    mixed_pool = mdl_sum(jnp.sum(mixed.reshape(k_dev, n_patch, -1), axis=1))
    tok_pool = jnp.sum(tok_full.reshape(-1, k_dev, n_patch).astype(f32), axis=2).T
    learn_pool = ((mixed_pool + tok_pool) * (1.0 / n_patch)).astype(bf16)
    learn_emb = jnp.dot(learn_pool, ref_proj, preferred_element_type=f32)
    learn_hat = unit_rows(in_order(mdl_pieces(learn_emb), 1))
    kept_text = text_hat[kept_index]
    learn_own = own_product(learn_hat, kept_text)
    learn_part = exp_total(learn_hat, text_split)
    totals = mdl_sum(jnp.concatenate([ref_part, learn_part]))
    ref_loss = jnp.log(totals[:ex_dev]) - logit_scale * ref_own
    learner_loss = jnp.log(totals[ex_dev:]) - logit_scale * learn_own
    learnability = learner_loss - ref_loss[kept_index]

    n_chunks = 4
    width = ff_dev // n_chunks
    outs = []
    for c in range(n_chunks):
        cols = slice(c * width, (c + 1) * width)
        grad_act = lax.dot_general(
            cot_full, w_down[cols], (((0,), (1,)), ((), ())), preferred_element_type=f32
        )
        grad_pre = (grad_act * row_weight[:, None] * gelu_slope[:, cols]).astype(bf16)
        pair_pre = jnp.concatenate([grad_pre, swap(grad_pre, "sel", 1)], axis=0)
        part = jnp.dot(tok_pair, pair_pre, preferred_element_type=f32)
        part = part.reshape(n_high, blk, width)
        if rotations:
            total = lax.dynamic_index_in_dim(part, high_me, 0, keepdims=False)
            for step in range(1, n_high):
                block = lax.dynamic_index_in_dim(
                    part, (high_me + step) % n_high, 0, keepdims=False
                )
                total = total + rotate_pairs(block.astype(bf16), step).astype(f32)
        else:
            total = lax.psum_scatter(
                part,
                "sel",
                scatter_dimension=0,
                axis_index_groups=[list(range(p, n_sel, 2)) for p in range(2)],
                tiled=False,
            )
        outs.append(total)
    grad_up = jnp.concatenate(outs, axis=1)
    return (ref_loss, learnability, grad_up)


def dot_f32(a, b):
    return jnp.dot(a, b, preferred_element_type=f32)


def dot_rows(a, b):
    return lax.dot_general(a, b, (((1,), (1,)), ((), ())), preferred_element_type=f32)


def dot_cols(a, b):
    return lax.dot_general(a, b, (((0,), (0,)), ((), ())), preferred_element_type=f32)


def group_mask(n_items, n_patch):
    shape = (n_items, n_items * n_patch)
    row = lax.broadcasted_iota(jnp.int32, shape, 1)
    first = n_patch * lax.broadcasted_iota(jnp.int32, shape, 0)
    return (row >= first) & (row < first + n_patch), row - first


def as_row(column):
    n = column.shape[0]
    return jnp.broadcast_to(column, (n, n)).T[0:1]


def place(index, length):
    return pl.ds(pl.multiple_of(index * length, length), length)


def call(body, out_shape, cost, grid=(), vmem=24 * 2**20, **kwargs):
    flops, moved = cost
    return pl.pallas_call(
        body,
        out_shape=out_shape,
        grid=grid,
        cost_estimate=pl.CostEstimate(flops=1, bytes_accessed=1, transcendentals=0),
        compiler_params=pltpu.CompilerParams(vmem_limit_bytes=vmem),
        **kwargs,
    )


def struct(shape, dtype):
    return jax.ShapeDtypeStruct(shape, dtype)


def pick_body(
    n_patch, patches_hbm, cot_hbm, kept, dest, text_hbm, both, half, pool, texts, patches, sems
):
    d_part, n_all = patches.shape
    ex_dev = n_all // n_patch
    copies = [
        pltpu.make_async_copy(patches_hbm, patches, sems.at[0]),
        pltpu.make_async_copy(cot_hbm, both.at[pl.ds(d_part, d_part), :], sems.at[1]),
        pltpu.make_async_copy(text_hbm, texts.at[pl.ds(0, ex_dev), :], sems.at[2]),
    ]
    for copy in copies:
        copy.start()
    k_dev = kept.shape[1]
    member, offset = group_mask(k_dev, n_patch)
    expand = member.astype(bf16)
    index = jnp.broadcast_to(kept[...].astype(f32), (8, k_dev)).astype(bf16)
    base = dot_f32(index, expand)[0:1].astype(jnp.int32)
    row = base * n_patch + jnp.sum(jnp.where(member, offset, 0), axis=0, keepdims=True)
    pick = (lax.broadcasted_iota(jnp.int32, (n_all, row.shape[1]), 0) == row).astype(bf16)
    for copy in copies:
        copy.wait()
    values = patches[...]
    both[0:d_part, :] = dot_f32(values, pick).astype(bf16)
    other = 1 - lax.rem(lax.axis_index("sel"), 2)
    half[...] = both[place(other, d_part // 2), :]
    texts[ex_dev:, :] = jnp.zeros((16, texts.shape[1]), bf16)
    texts[ex_dev:, 0:k_dev] = jnp.broadcast_to(dest[...].astype(f32), (16, k_dev)).astype(bf16)
    groups, _ = group_mask(ex_dev, n_patch)
    pool[...] = (dot_rows(values, groups.astype(bf16)) * (1.0 / n_patch)).astype(bf16)


def extras_body(half, pool, t0, t1, t2, t3, extras, texts, dests):
    n_half, n_rows = half.shape
    n_ex = pool.shape[1]
    extras[:, 0:n_rows] = half[...]
    extras[:, n_rows : n_rows + n_ex] = pool[0:n_half, :]
    extras[:, n_rows + n_ex :] = pool[n_half:, :]
    n_text = t0.shape[0]
    for r, piece in enumerate((t0, t1, t2, t3)):
        texts[r * n_text : (r + 1) * n_text, :] = piece[...]
        k_dev = dests.shape[1] // 4
        dests[:, r * k_dev : (r + 1) * k_dev] = piece[n_text - 16 :, 0:k_dev]


def text_body(mine, theirs, whole, send):
    n_high = 4
    n_text = mine.shape[0] // n_high
    ex_dev = n_text - 16
    me = lax.axis_index("mdl")
    sel = lax.axis_index("sel")
    parity, high = lax.rem(sel, 2), lax.div(sel, 2)
    for which, place_in_pair in ((mine, parity), (theirs, 1 - parity)):
        for r in range(n_high):
            source = lax.rem(high + n_high - r, n_high)
            rows = place(source * 2 + place_in_pair, ex_dev)
            whole[rows, :] = which[r * n_text : r * n_text + ex_dev, :]
    for i in range(2):
        send[i * 2 * ex_dev : (i + 1) * 2 * ex_dev, :] = whole[place(me ^ (2 + i), 2 * ex_dev), :]


def row_weights(n_patch, n_rows, pre, pre_pair):
    k_dev = n_rows // n_patch
    shard = lax.broadcasted_iota(jnp.int32, (128, k_dev), 0).astype(f32)
    ones = jnp.ones((8, k_dev), bf16)
    counts = jnp.zeros((8, 128), f32)
    named = []
    for which in (pre, pre_pair):
        dests = which[n_rows:, :].astype(f32)
        for r in range(4):
            is_dest = (shard == dests[0:1, r * k_dev : (r + 1) * k_dev]).astype(bf16)
            counts = counts + dot_rows(ones, is_dest)
            if r == 0:
                named.append(is_dest)
    member = group_mask(k_dev, n_patch)[0].astype(bf16)
    weights = []
    for is_dest in named:
        count = dot_f32(counts.astype(bf16), is_dest).astype(bf16)
        weights.append(1.0 / dot_f32(count, member)[0:1])
    return weights


def text_relay_body(whole, received, send):
    n_share = received.shape[0] // 2
    send[0:n_share, :] = whole[place(lax.axis_index("mdl") ^ 1, n_share), :]
    send[n_share:, :] = received[n_share:, :]


def share_body(whole, from_x, from_core, share, values):
    n_share, width = share.shape[0], whole.shape[1]
    me = lax.axis_index("mdl")
    pieces = (
        whole[place(me, n_share), :],
        from_core[0:n_share, :],
        from_x[0:n_share, :],
        from_core[n_share:, :],
    )
    for j, piece in enumerate(pieces):
        values[:, place(me ^ j, width)] = piece.astype(f32)
    rows = values[...]
    norm_sq = jnp.sum(rows * rows, axis=1, keepdims=True)
    share[...] = (rows * lax.rsqrt(norm_sq + eps)).astype(bf16)


def stage_body(up, down, up_held, down_held, sems):
    copies = [
        pltpu.make_async_copy(up, up_held, sems.at[0]),
        pltpu.make_async_copy(down, down_held, sems.at[1]),
    ]
    for copy in copies:
        copy.start()
    for copy in copies:
        copy.wait()


def chunk_work(n_patch, tok, cot, w_up, w_down, pre, mixed):
    k_dev = tok.shape[0] // n_patch
    groups = group_mask(k_dev, n_patch)[0].astype(bf16)
    pre_act = dot_f32(tok[...], w_up[...])
    activated, gelu_slope = gelu_parts(pre_act)
    pre[0 : tok.shape[0], :] = (dot_rows(cot[...], w_down[...]) * gelu_slope).astype(bf16)
    pooled = dot_f32(groups, activated.astype(bf16))
    high = pooled.astype(bf16)
    low = (pooled - high.astype(f32)).astype(bf16)
    both = dot_f32(jnp.concatenate([high, low], axis=0), w_down[...])
    return mixed + (both[:k_dev] + both[k_dev:])


def first_chunk_body(
    n_patch, n_mdl, dests, b0, b1, b2, b3, w_up, w_down, pre, mixed, tok_full, tok, cot, cot_full
):
    d_part, n_rows = b0.shape[0] // 2, b0.shape[1]
    groups = group_mask(n_rows // n_patch, n_patch)[0].astype(bf16)
    me = lax.axis_index("mdl")
    for j, piece in enumerate((b0, b1, b2, b3)):
        tok_full[place(me ^ j, d_part), :] = piece[0:d_part, :]
        cot_full[place(me ^ j, d_part), :] = piece[d_part:, :]
    tok[...] = tok_full[...].T
    cot[...] = cot_full[...].T
    start = dot_f32(groups, tok[...]) * (1.0 / n_mdl)
    mixed[...] = chunk_work(n_patch, tok, cot, w_up, w_down, pre, start)
    pre[n_rows:, :] = jnp.zeros((16, pre.shape[1]), bf16)
    pre[n_rows:, 0 : dests.shape[1]] = dests[...]


def next_chunk_body(n_patch, tok, cot, w_up, w_down, mixed_in, pre, mixed):
    total = chunk_work(n_patch, tok, cot, w_up, w_down, pre, mixed_in[...])
    mixed[...] = total.astype(mixed.dtype)


def split_part(part, keep, send):
    n_keep = keep.shape[0]
    keep[...] = part[:n_keep]
    send[...] = part[n_keep:].astype(bf16)


def first_grad_body(n_patch, tok_full, h0, h1, h2, h3, pre, pre_pair, pair, keep, send):
    n_rows = tok_full.shape[1]
    blk = h0.shape[0]
    weights = row_weights(n_patch, n_rows, pre, pre_pair)
    me = lax.axis_index("mdl")
    sel = lax.axis_index("sel")
    parity, high = lax.rem(sel, 2), lax.div(sel, 2)
    for j, piece in enumerate((h0, h1, h2, h3)):
        block = me ^ j
        apart = block ^ high
        rows = place(2 * lax.rem(apart, 2) + lax.div(apart, 2), blk)
        own_tok = tok_full[place(2 * block + parity, blk), :].astype(f32)
        pair[rows, 0:n_rows] = (own_tok * weights[0]).astype(bf16)
        pair_tok = piece[:, 0:n_rows].astype(f32)
        pair[rows, n_rows:] = (pair_tok * weights[1]).astype(bf16)
    grad_body(pair, pre, pre_pair, keep, send)


def grad_body(pair, pre, pre_pair, keep, send):
    n_rows = pair.shape[1] // 2
    part = dot_f32(pair[:, 0:n_rows], pre[0:n_rows, :])
    part = part + dot_f32(pair[:, n_rows:], pre_pair[0:n_rows, :])
    split_part(part, keep, send)


def add_body(held, received, keep, send):
    split_part(held[...] + received[...].astype(f32), keep, send)


def mix_body(a, b, total):
    total[...] = (a[...].astype(f32) + b[...].astype(f32)).astype(total.dtype)


def heads_body(n_patch, h0, h1, h2, h3, a, b, ref_proj, emb, pooled):
    me = lax.axis_index("mdl")
    n_rows = h0.shape[0]
    n_ex = pooled.shape[1]
    first = h0.shape[1] - 2 * n_ex
    for j, piece in enumerate((h0, h1, h2, h3)):
        for part in range(2):
            pooled[place((me ^ j) * 2 + part, n_rows), :] = piece[
                :, first + part * n_ex : first + (part + 1) * n_ex
            ]
    learn_pool = ((a[...].astype(f32) + b[...].astype(f32)) * (1.0 / n_patch)).astype(bf16)
    emb[0:n_ex, :] = dot_cols(pooled[...], ref_proj[...])
    emb[n_ex:, :] = dot_f32(learn_pool, ref_proj[...])


def own_score(hat, texts):
    return jnp.sum(hat.astype(f32) * texts.astype(f32), axis=1, keepdims=True)


def scores_body(e0, e1, e2, e3, share, kept, out, whole):
    me = lax.axis_index("mdl")
    sel = lax.axis_index("sel")
    width = e0.shape[1]
    for j, piece in enumerate((e0, e1, e2, e3)):
        whole[:, place(me ^ j, width)] = piece[...]
    values = whole[...]
    norm_sq = jnp.sum(values * values, axis=1, keepdims=True)
    hat = (values * lax.rsqrt(norm_sq + eps)).astype(bf16)
    k_dev = kept.shape[1]
    n_all = hat.shape[0]
    ex_dev = n_all - k_dev
    scores = dot_rows(share[...], hat)
    out[:, 0:n_all] = jnp.sum(jnp.exp(logit_scale * scores), axis=0, keepdims=True)
    own_text = share[place(lax.rem(sel, 2), ex_dev), :]
    holds = me == lax.div(sel, 2)
    pick = (lax.broadcasted_iota(jnp.int32, (ex_dev, k_dev), 0) == kept[...]).astype(bf16)
    kept_text = dot_cols(pick, own_text)
    learn_own = as_row(own_score(hat[ex_dev:], kept_text))
    image_own = as_row(own_score(hat[:ex_dev], own_text))
    out[:, n_all : n_all + k_dev] = jnp.where(holds, learn_own, 0.0)
    out[:, n_all + k_dev :] = jnp.where(holds, image_own, 0.0)


def losses_body(a, b, kept, ref_loss, learnability):
    sums = a[...] + b[...]
    k_dev, ex_dev = kept.shape[1], ref_loss.shape[1]
    n_all = ex_dev + k_dev
    losses = jnp.log(sums[:, 0:ex_dev]) - logit_scale * sums[:, n_all + k_dev :]
    ref_loss[...] = losses
    learner = jnp.log(sums[:, ex_dev:n_all]) - logit_scale * sums[:, n_all : n_all + k_dev]
    pick = lax.broadcasted_iota(jnp.int32, (ex_dev, k_dev), 0) == kept[...]
    picked = jnp.sum(jnp.where(pick, as_row_t(losses), 0.0), axis=0, keepdims=True)
    learnability[...] = learner - picked


def as_row_t(row):
    n = row.shape[1]
    return jnp.broadcast_to(row, (n, n)).T[:, 0:1]


def after(value, *others):
    return lax.optimization_barrier((value,) + others)[0] if others else value


def quarter_sel(patches, text, ref_proj, w_up, w_down, kept_index, dest, cotan):
    n_mdl, n_sel = lax.axis_size("mdl"), lax.axis_size("sel")
    n_high = n_sel // 2
    ex_dev, emb_part = text.shape
    emb_full = emb_part * n_mdl
    d_part = patches.shape[1]
    d_full = d_part * n_mdl
    n_patch = patches.shape[0] // ex_dev
    k_dev = kept_index.shape[0]
    n_rows = k_dev * n_patch
    ff_dev = w_up.shape[1]
    blk = d_full // n_sel
    n_share = ex_dev * n_sel // n_mdl
    n_emb = ex_dev + k_dev
    kept_row = kept_index.reshape(1, k_dev)
    dest_row = dest.reshape(1, k_dev)
    size = ff_dev // 4
    whole = lambda shape: pl.BlockSpec(shape, lambda i: (0,) * len(shape))
    row_struct = struct((n_rows, d_full), bf16)
    row_spec = whole((n_rows, d_full))
    mixed_struct = struct((k_dev, d_full), f32)
    mixed_spec = whole((k_dev, d_full))
    pre_struct = struct((n_rows, size), bf16)
    pre_spec = whole((n_rows, size))
    halves = (struct((2 * blk, size), f32), struct((2 * blk, size), bf16))

    def run(ties, body, out_shape, *operands, **kwargs):
        first = after(operands[0], *ties)
        return call(body, out_shape, (2**20, 2**20), **kwargs)(first, *operands[1:])

    def pick(ties):
        return run(
            ties,
            functools.partial(pick_body, n_patch),
            (
                struct((2 * d_part, n_rows), bf16),
                struct((d_part // 2, n_rows), bf16),
                struct((d_part, ex_dev), bf16),
                struct((ex_dev + 16, emb_part), bf16),
            ),
            patches.T,
            cotan.T,
            kept_row,
            dest_row,
            text,
            in_specs=[
                pl.BlockSpec(memory_space=space)
                for space in (pltpu.HBM, pltpu.HBM, pltpu.VMEM, pltpu.VMEM, pltpu.HBM)
            ],
            scratch_shapes=[
                pltpu.VMEM((d_part, ex_dev * n_patch), bf16),
                pltpu.SemaphoreType.DMA((3,)),
            ],
            vmem=60 * 2**20,
        )


    def stage(ties):
        return run(
            ties,
            stage_body,
            (struct(w_up.shape, bf16), struct(w_down.shape, bf16)),
            w_up,
            w_down,
            in_specs=[pl.BlockSpec(memory_space=pltpu.HBM)] * 2,
            scratch_shapes=[pltpu.SemaphoreType.DMA((2,))],
            vmem=32 * 2**20,
        )


    def make_extras(ties, half_pair, pool, texts):
        rotated = [rotate_pairs(texts, s) for s in range(1, n_high)]
        return run(
            ties,
            extras_body,
            (
                struct((d_part // 2, n_rows + 2 * ex_dev), bf16),
                struct((n_high * (ex_dev + 16), emb_part), bf16),
                struct((16, n_high * k_dev), bf16),
            ),
            half_pair,
            pool,
            texts,
            *rotated,
        )


    def weight_specs(c):
        return [
            pl.BlockSpec((d_full, size), lambda i: (0, c)),
            pl.BlockSpec((size, d_full), lambda i: (c, 0)),
        ]


    def forward_first(ties, *operands):
        return run(
            ties,
            functools.partial(first_chunk_body, n_patch, n_mdl),
            (
                struct((n_rows + 16, size), bf16),
                mixed_struct,
                struct((d_full, n_rows), bf16),
                row_struct,
                row_struct,
            ),
            *operands,
            grid=(1,),
            in_specs=[whole((16, n_high * k_dev))]
            + [whole((2 * d_part, n_rows))] * 4 + weight_specs(0),
            out_specs=[
                whole((n_rows + 16, size)),
                mixed_spec,
                whole((d_full, n_rows)),
                row_spec,
                row_spec,
            ],
            scratch_shapes=[pltpu.VMEM((d_full, n_rows), bf16)],
        )

    def forward(ties, c, tok, cot, held_up, held_down, mixed):
        last = c == ff_dev // size - 1
        return run(
            ties,
            functools.partial(next_chunk_body, n_patch),
            (pre_struct, struct((k_dev, d_full), bf16 if last else f32)),
            tok,
            cot,
            held_up,
            held_down,
            mixed,
            grid=(1,),
            in_specs=[row_spec, row_spec] + weight_specs(c) + [mixed_spec],
            out_specs=[pre_spec, mixed_spec],
        )


    def all_shards(ties, my_texts, pair_texts):
        return run(
            ties,
            text_body,
            (
                struct((ex_dev * n_sel, emb_part), bf16),
                struct((2 * n_share, emb_part), bf16),
            ),
            my_texts,
            pair_texts,
        )

    def grad_first(ties, *operands):
        pair_struct = struct((blk * n_high, 2 * n_rows), bf16)
        return run(ties, functools.partial(first_grad_body, n_patch), (pair_struct,) + halves, *operands)

    def grad(ties, *operands):
        return run(ties, grad_body, halves, *operands)

    def add(ties, keep, received):
        structs = (struct((blk, size), f32), struct((blk, size), bf16))
        return run(ties, add_body, structs, keep, received)

    def relay_text(ties, all_texts, text_x):
        send = struct((2 * n_share, emb_part), bf16)
        return run(ties, text_relay_body, send, all_texts, text_x)

    def share_text(ties, *operands):
        return run(
            ties,
            share_body,
            struct((n_share, emb_full), bf16),
            *operands,
            scratch_shapes=[pltpu.VMEM((n_share, emb_full), f32)],
        )

    def heads(ties, *operands):
        return run(
            ties,
            functools.partial(heads_body, n_patch),
            struct((n_emb, emb_part), f32),
            *operands,
            ref_proj,
            scratch_shapes=[pltpu.VMEM((d_full, ex_dev), bf16)],
        )

    def scores(ties, *operands):
        return run(
            ties,
            scores_body,
            struct((1, 2 * n_emb), f32),
            *operands,
            kept_row,
            scratch_shapes=[pltpu.VMEM((n_emb, emb_full), f32)],
        )

    def losses(ties, total, total_x):
        structs = (struct((1, ex_dev), f32), struct((1, k_dev), f32))
        return run(ties, losses_body, structs, total, total_x, kept_row)


    both, half, pool, texts = pick(())
    both_x = swap(both, "mdl", 2)
    both_core = swap(both, "mdl", 1)
    half_pair = swap(half, "sel", 1)
    held_up, held_down = stage((texts,))
    extras, my_texts, dests = make_extras((held_down,), half_pair, pool, texts)
    both_diag = swap(after(both_x, extras), "mdl", 1)
    extras_x = swap(extras, "mdl", 2)
    extras_core = swap(extras, "mdl", 1)
    extras_diag = swap(extras_x, "mdl", 1)
    pair_texts = swap(my_texts, "sel", 1)
    pre0, mixed0, tok_full, tok, cot = forward_first(
        (dests, extras_core),
        dests,
        both,
        both_core,
        both_x,
        both_diag,
        held_up,
        held_down,
    )
    pair_pre0 = swap(pre0, "sel", 1)
    pre1, mixed1 = forward((cot,), 1, tok, cot, held_up, held_down, mixed0)
    pair_pre1 = swap(pre1, "sel", 1)
    all_texts, text_send = all_shards((mixed1,), my_texts, pair_texts)
    text_x = swap(text_send, "mdl", 2)
    pre2, mixed2 = forward((text_send,), 2, tok, cot, held_up, held_down, mixed1)
    pair_pre2 = swap(pre2, "sel", 1)
    pre3, mixed = forward((mixed2,), 3, tok, cot, held_up, held_down, mixed2)
    mixed_core = swap(mixed, "mdl", 1)
    mixsum = run((mixed, extras_diag), mix_body, struct((k_dev, d_full), bf16), mixed, mixed_core)
    mixsum_x = swap(mixsum, "mdl", 2)
    relay = relay_text((mixsum,), all_texts, text_x)
    text_core = swap(relay, "mdl", 1)
    pair, keep0, send0 = grad_first(
        (relay,),
        tok_full,
        extras,
        extras_core,
        extras_x,
        extras_diag,
        pre0,
        pair_pre0,
    )
    first0 = swap(send0, "sel", 2)
    keep1, send1 = grad((send0, text_x), pair, pre1, pair_pre1)
    first1 = swap(send1, "sel", 2)
    emb = heads((send1, first0), extras, extras_core, extras_x, extras_diag, mixsum, mixsum_x)
    emb_x = swap(emb, "mdl", 2)
    emb_core = swap(emb, "mdl", 1)
    emb_diag = swap(emb_x, "mdl", 1)
    own0, rest0 = add((emb,), keep0, first0)
    pair_pre3 = swap(after(pre3, own0), "sel", 1)
    second0 = swap(rest0, "sel", 4)
    keep2, send2 = grad((rest0,), pair, pre2, pair_pre2)
    first2 = swap(send2, "sel", 2)
    own1, rest1 = add((send2,), keep1, first1)
    second1 = swap(rest1, "sel", 4)
    share = share_text((rest1,), all_texts, text_x, text_core)
    keep3, send3 = grad((share,), pair, pre3, pair_pre3)
    first3 = swap(send3, "sel", 2)
    own2, rest2 = add((send3,), keep2, first2)
    second2 = swap(rest2, "sel", 4)
    sums = scores((rest2,), emb, emb_core, emb_x, emb_diag, share)
    sums_core = swap(sums, "mdl", 1)
    total = run((sums,), mix_body, struct((1, 2 * n_emb), f32), sums, sums_core)
    own3, rest3 = add((total,), keep3, first3)
    total_x = swap(after(total, own3), "mdl", 2)
    second3 = swap(rest3, "sel", 4)
    ref_loss, learnability = losses((rest3,), total, total_x)

    own3, ref_loss, learnability = lax.optimization_barrier((own3, ref_loss, learnability))
    sums = [
        (own0, second0),
        (own1, second1),
        (own2, second2),
        (own3, second3),
    ]
    grad_up = jnp.concatenate([own + other.astype(f32) for own, other in sums], axis=1)
    return (ref_loss.reshape(ex_dev), learnability.reshape(k_dev), grad_up)


def solution(mesh):
    in_specs = (
        P("sel", "mdl"),
        P("sel", "mdl"),
        P(None, "mdl"),
        P(None, "mdl"),
        P("mdl", None),
        P("sel"),
        P("sel"),
        P("sel", "mdl"),
    )
    out_specs = (P("sel"), P("sel"), P("sel", "mdl"))
    body = quarter_sel if (mesh.shape["sel"], mesh.shape["mdl"]) == (8, 4) else per_device
    return jax.shard_map(
        body, mesh=mesh, in_specs=in_specs, out_specs=out_specs, check_vma=False
    )
```

```python
import functools

import jax
import jax.numpy as jnp
from jax import lax
from jax.experimental import pallas as pl
from jax.experimental.pallas import tpu as pltpu
from jax.sharding import PartitionSpec as P

logit_scale = 64.0
eps = 1e-06
f32 = jnp.float32
bf16 = jnp.bfloat16


def gelu_parts(pre_act):
    cumul = 0.5 * (1.0 + lax.erf(pre_act * 0.7071067811865476))
    density = jnp.exp(-0.5 * pre_act * pre_act) * 0.3989422804014327
    return (pre_act * cumul, cumul + pre_act * density)


def swap(value, axis, bit):
    size = lax.axis_size(axis)
    return lax.ppermute(value, axis, [(i, i ^ bit) for i in range(size)])


def rotate_pairs(value, step):
    size = lax.axis_size("sel")
    return lax.ppermute(value, "sel", [(i, (i + 2 * step) % size) for i in range(size)])


def mdl_pieces(value):
    n = lax.axis_size("mdl")
    out = [value] + [None] * (n - 1)
    top = n // 2
    if n == 1:
        return out
    out[top] = swap(value, "mdl", top)
    low = top // 2
    have = [0, top]
    while low:
        for j in list(have):
            out[j | low] = swap(out[j], "mdl", low)
            have.append(j | low)
        low //= 2
    return out


def in_order(pieces, axis):
    me = lax.axis_index("mdl")
    bit = 1
    while bit < lax.axis_size("mdl"):
        set_bit = (me & bit) != 0
        merged = []
        for j in range(0, len(pieces), 2):
            first, second = pieces[j], pieces[j + 1]
            merged.append(
                jnp.where(
                    set_bit,
                    jnp.concatenate([second, first], axis),
                    jnp.concatenate([first, second], axis),
                )
            )
        pieces = merged
        bit *= 2
    return pieces[0]


def mdl_sum(value):
    bit = 1
    while bit < lax.axis_size("mdl"):
        value = value + swap(value, "mdl", bit)
        bit *= 2
    return value


def unit_rows(values):
    norm_sq = jnp.sum(values * values, axis=1)
    return (values * lax.rsqrt(norm_sq + eps)[:, None]).astype(bf16)


def exp_total(rows_full, texts):
    scores = lax.dot_general(
        rows_full, texts, (((1,), (1,)), ((), ())), preferred_element_type=f32
    )
    return jnp.sum(jnp.exp(logit_scale * scores), axis=1)


def own_product(rows, texts):
    return jnp.sum(rows.astype(f32) * texts.astype(f32), axis=1)


def per_device(patches, text, ref_proj, w_up, w_down, kept_index, dest, cotan):
    n_sel = lax.axis_size("sel")
    n_mdl = lax.axis_size("mdl")
    ex_dev = text.shape[0]
    d_part = patches.shape[1]
    n_patch = patches.shape[0] // ex_dev
    k_dev = kept_index.shape[0]
    n_rows = k_dev * n_patch
    ff_dev = w_up.shape[1]
    n_high = n_sel // 2
    rotations = n_high <= 4
    sel_me, mdl_me = lax.axis_index("sel"), lax.axis_index("mdl")
    pair_me, high_me = sel_me % 2, sel_me // 2

    patches_t = patches.T
    row_of = (kept_index[:, None] * n_patch + jnp.arange(n_patch)[None, :]).reshape(-1)
    pick = (jnp.arange(ex_dev * n_patch)[:, None] == row_of[None, :]).astype(bf16)
    tok_t = jnp.dot(patches_t, pick, preferred_element_type=f32).astype(bf16)
    cot_t = cotan.T
    blk = d_part * n_mdl // n_sel
    halves = tok_t.reshape(d_part // (2 * blk), 2, blk, n_rows)
    send_half = lax.dynamic_index_in_dim(halves, 1 - pair_me, 1, keepdims=False)
    recv_half = swap(send_half.reshape(d_part // 2, n_rows), "sel", 1)

    tok_full = in_order(mdl_pieces(tok_t), 0)
    cot_full = in_order(mdl_pieces(cot_t), 0)
    recv_half_full = in_order(mdl_pieces(recv_half), 0)
    n_blk = d_part * n_mdl // (2 * blk)
    own_half_full = lax.dynamic_index_in_dim(
        tok_full.reshape(n_blk, 2, blk, n_rows), pair_me, 1, keepdims=False
    ).reshape(n_blk * blk, n_rows)
    tok_pair = jnp.concatenate([own_half_full, recv_half_full], axis=1)

    counts = jnp.sum((dest[:, None] == jnp.arange(n_sel)[None, :]).astype(f32), axis=0)
    if rotations:
        pair_counts = counts + swap(counts, "sel", 1)
        counts = pair_counts
        for step in range(1, n_high):
            counts = counts + rotate_pairs(pair_counts, step)
    else:
        counts = lax.psum(counts, "sel")
    row_weight = 1.0 / jnp.repeat(counts[dest], n_patch)

    text_full = in_order(mdl_pieces(text), 1).astype(f32)
    text_hat = unit_rows(text_full)
    share = ex_dev // n_mdl
    text_share = lax.dynamic_slice_in_dim(text_hat, mdl_me * share, share, 0)
    if rotations:
        pair_share = jnp.concatenate([text_share, swap(text_share, "sel", 1)], axis=0)
        text_split = jnp.concatenate(
            [pair_share] + [rotate_pairs(pair_share, s) for s in range(1, n_high)], axis=0
        )
    else:
        text_split = lax.all_gather(text_share, "sel", axis=0, tiled=True)

    pooled_t = (
        jnp.sum(patches_t.reshape(d_part, ex_dev, n_patch).astype(f32), axis=2) * (1.0 / n_patch)
    ).astype(bf16)
    pooled_full = in_order(mdl_pieces(pooled_t), 0)
    img_emb = lax.dot_general(
        pooled_full, ref_proj, (((0,), (0,)), ((), ())), preferred_element_type=f32
    )
    img_hat = unit_rows(in_order(mdl_pieces(img_emb), 1))
    ref_own = own_product(img_hat, text_hat)
    ref_part = exp_total(img_hat, text_split)

    pre_act = lax.dot_general(
        tok_full, w_up, (((0,), (0,)), ((), ())), preferred_element_type=f32
    )
    activated, gelu_slope = gelu_parts(pre_act)
    hidden = activated.astype(bf16)
    mixed = jnp.dot(hidden, w_down, preferred_element_type=f32)
    mixed_pool = mdl_sum(jnp.sum(mixed.reshape(k_dev, n_patch, -1), axis=1))
    tok_pool = jnp.sum(tok_full.reshape(-1, k_dev, n_patch).astype(f32), axis=2).T
    learn_pool = ((mixed_pool + tok_pool) * (1.0 / n_patch)).astype(bf16)
    learn_emb = jnp.dot(learn_pool, ref_proj, preferred_element_type=f32)
    learn_hat = unit_rows(in_order(mdl_pieces(learn_emb), 1))
    kept_text = text_hat[kept_index]
    learn_own = own_product(learn_hat, kept_text)
    learn_part = exp_total(learn_hat, text_split)
    totals = mdl_sum(jnp.concatenate([ref_part, learn_part]))
    ref_loss = jnp.log(totals[:ex_dev]) - logit_scale * ref_own
    learner_loss = jnp.log(totals[ex_dev:]) - logit_scale * learn_own
    learnability = learner_loss - ref_loss[kept_index]

    n_chunks = 4
    width = ff_dev // n_chunks
    outs = []
    for c in range(n_chunks):
        cols = slice(c * width, (c + 1) * width)
        grad_act = lax.dot_general(
            cot_full, w_down[cols], (((0,), (1,)), ((), ())), preferred_element_type=f32
        )
        grad_pre = (grad_act * row_weight[:, None] * gelu_slope[:, cols]).astype(bf16)
        pair_pre = jnp.concatenate([grad_pre, swap(grad_pre, "sel", 1)], axis=0)
        part = jnp.dot(tok_pair, pair_pre, preferred_element_type=f32)
        part = part.reshape(n_high, blk, width)
        if rotations:
            total = lax.dynamic_index_in_dim(part, high_me, 0, keepdims=False)
            for step in range(1, n_high):
                block = lax.dynamic_index_in_dim(
                    part, (high_me + step) % n_high, 0, keepdims=False
                )
                total = total + rotate_pairs(block.astype(bf16), step).astype(f32)
        else:
            total = lax.psum_scatter(
                part,
                "sel",
                scatter_dimension=0,
                axis_index_groups=[list(range(p, n_sel, 2)) for p in range(2)],
                tiled=False,
            )
        outs.append(total)
    grad_up = jnp.concatenate(outs, axis=1)
    return (ref_loss, learnability, grad_up)


def dot_f32(a, b):
    return jnp.dot(a, b, preferred_element_type=f32)


def dot_rows(a, b):
    return lax.dot_general(a, b, (((1,), (1,)), ((), ())), preferred_element_type=f32)


def dot_cols(a, b):
    return lax.dot_general(a, b, (((0,), (0,)), ((), ())), preferred_element_type=f32)


def group_mask(n_items, n_patch):
    shape = (n_items, n_items * n_patch)
    row = lax.broadcasted_iota(jnp.int32, shape, 1)
    first = n_patch * lax.broadcasted_iota(jnp.int32, shape, 0)
    return (row >= first) & (row < first + n_patch), row - first


def as_row(column):
    n = column.shape[0]
    return jnp.broadcast_to(column, (n, n)).T[0:1]


def place(index, length):
    return pl.ds(pl.multiple_of(index * length, length), length)


def call(body, out_shape, cost, grid=(), vmem=24 * 2**20, **kwargs):
    flops, moved = cost
    return pl.pallas_call(
        body,
        out_shape=out_shape,
        grid=grid,
        cost_estimate=pl.CostEstimate(flops=1, bytes_accessed=1, transcendentals=0),
        compiler_params=pltpu.CompilerParams(vmem_limit_bytes=vmem),
        **kwargs,
    )


def struct(shape, dtype):
    return jax.ShapeDtypeStruct(shape, dtype)


def pick_body(
    n_patch, patches_hbm, cot_hbm, kept, dest, text_hbm, both, half, pool, texts, patches, sems
):
    d_part, n_all = patches.shape
    ex_dev = n_all // n_patch
    copies = [
        pltpu.make_async_copy(patches_hbm, patches, sems.at[0]),
        pltpu.make_async_copy(cot_hbm, both.at[pl.ds(d_part, d_part), :], sems.at[1]),
        pltpu.make_async_copy(text_hbm, texts.at[pl.ds(0, ex_dev), :], sems.at[2]),
    ]
    for copy in copies:
        copy.start()
    k_dev = kept.shape[1]
    member, offset = group_mask(k_dev, n_patch)
    expand = member.astype(bf16)
    index = jnp.broadcast_to(kept[...].astype(f32), (8, k_dev)).astype(bf16)
    base = dot_f32(index, expand)[0:1].astype(jnp.int32)
    row = base * n_patch + jnp.sum(jnp.where(member, offset, 0), axis=0, keepdims=True)
    pick = (lax.broadcasted_iota(jnp.int32, (n_all, row.shape[1]), 0) == row).astype(bf16)
    for copy in copies:
        copy.wait()
    values = patches[...]
    both[0:d_part, :] = dot_f32(values, pick).astype(bf16)
    other = 1 - lax.rem(lax.axis_index("sel"), 2)
    half[...] = both[place(other, d_part // 2), :]
    texts[ex_dev:, :] = jnp.zeros((16, texts.shape[1]), bf16)
    texts[ex_dev:, 0:k_dev] = jnp.broadcast_to(dest[...].astype(f32), (16, k_dev)).astype(bf16)
    groups, _ = group_mask(ex_dev, n_patch)
    pool[...] = (dot_rows(values, groups.astype(bf16)) * (1.0 / n_patch)).astype(bf16)


def extras_body(half, pool, t0, t1, t2, t3, extras, texts, dests):
    n_half, n_rows = half.shape
    n_ex = pool.shape[1]
    extras[:, 0:n_rows] = half[...]
    extras[:, n_rows : n_rows + n_ex] = pool[0:n_half, :]
    extras[:, n_rows + n_ex :] = pool[n_half:, :]
    n_text = t0.shape[0]
    for r, piece in enumerate((t0, t1, t2, t3)):
        texts[r * n_text : (r + 1) * n_text, :] = piece[...]
        k_dev = dests.shape[1] // 4
        dests[:, r * k_dev : (r + 1) * k_dev] = piece[n_text - 16 :, 0:k_dev]


def text_body(mine, theirs, whole, send):
    n_high = 4
    n_text = mine.shape[0] // n_high
    ex_dev = n_text - 16
    me = lax.axis_index("mdl")
    sel = lax.axis_index("sel")
    parity, high = lax.rem(sel, 2), lax.div(sel, 2)
    for which, place_in_pair in ((mine, parity), (theirs, 1 - parity)):
        for r in range(n_high):
            source = lax.rem(high + n_high - r, n_high)
            rows = place(source * 2 + place_in_pair, ex_dev)
            whole[rows, :] = which[r * n_text : r * n_text + ex_dev, :]
    for i in range(2):
        send[i * 2 * ex_dev : (i + 1) * 2 * ex_dev, :] = whole[place(me ^ (2 + i), 2 * ex_dev), :]


def row_weights(n_patch, n_rows, pre, pre_pair):
    k_dev = n_rows // n_patch
    shard = lax.broadcasted_iota(jnp.int32, (128, k_dev), 0).astype(f32)
    ones = jnp.ones((8, k_dev), bf16)
    counts = jnp.zeros((8, 128), f32)
    named = []
    for which in (pre, pre_pair):
        dests = which[n_rows:, :].astype(f32)
        for r in range(4):
            is_dest = (shard == dests[0:1, r * k_dev : (r + 1) * k_dev]).astype(bf16)
            counts = counts + dot_rows(ones, is_dest)
            if r == 0:
                named.append(is_dest)
    member = group_mask(k_dev, n_patch)[0].astype(bf16)
    weights = []
    for is_dest in named:
        count = dot_f32(counts.astype(bf16), is_dest).astype(bf16)
        weights.append(1.0 / dot_f32(count, member)[0:1])
    return weights


def text_relay_body(whole, received, send):
    n_share = received.shape[0] // 2
    send[0:n_share, :] = whole[place(lax.axis_index("mdl") ^ 1, n_share), :]
    send[n_share:, :] = received[n_share:, :]


def share_body(whole, from_x, from_core, share, values):
    n_share, width = share.shape[0], whole.shape[1]
    me = lax.axis_index("mdl")
    pieces = (
        whole[place(me, n_share), :],
        from_core[0:n_share, :],
        from_x[0:n_share, :],
        from_core[n_share:, :],
    )
    for j, piece in enumerate(pieces):
        values[:, place(me ^ j, width)] = piece.astype(f32)
    rows = values[...]
    norm_sq = jnp.sum(rows * rows, axis=1, keepdims=True)
    share[...] = (rows * lax.rsqrt(norm_sq + eps)).astype(bf16)


def stage_body(up, down, up_held, down_held, sems):
    copies = [
        pltpu.make_async_copy(up, up_held, sems.at[0]),
        pltpu.make_async_copy(down, down_held, sems.at[1]),
    ]
    for copy in copies:
        copy.start()
    for copy in copies:
        copy.wait()


def chunk_work(n_patch, tok, cot, w_up, w_down, pre, mixed):
    k_dev = tok.shape[0] // n_patch
    groups = group_mask(k_dev, n_patch)[0].astype(bf16)
    pre_act = dot_f32(tok[...], w_up[...])
    activated, gelu_slope = gelu_parts(pre_act)
    pre[0 : tok.shape[0], :] = (dot_rows(cot[...], w_down[...]) * gelu_slope).astype(bf16)
    pooled = dot_f32(groups, activated.astype(bf16))
    high = pooled.astype(bf16)
    low = (pooled - high.astype(f32)).astype(bf16)
    both = dot_f32(jnp.concatenate([high, low], axis=0), w_down[...])
    return mixed + (both[:k_dev] + both[k_dev:])


def first_chunk_body(
    n_patch, n_mdl, dests, b0, b1, b2, b3, w_up, w_down, pre, mixed, tok_full, tok, cot, cot_full
):
    d_part, n_rows = b0.shape[0] // 2, b0.shape[1]
    groups = group_mask(n_rows // n_patch, n_patch)[0].astype(bf16)
    me = lax.axis_index("mdl")
    for j, piece in enumerate((b0, b1, b2, b3)):
        tok_full[place(me ^ j, d_part), :] = piece[0:d_part, :]
        cot_full[place(me ^ j, d_part), :] = piece[d_part:, :]
    tok[...] = tok_full[...].T
    cot[...] = cot_full[...].T
    start = dot_f32(groups, tok[...]) * (1.0 / n_mdl)
    mixed[...] = chunk_work(n_patch, tok, cot, w_up, w_down, pre, start)
    pre[n_rows:, :] = jnp.zeros((16, pre.shape[1]), bf16)
    pre[n_rows:, 0 : dests.shape[1]] = dests[...]


def next_chunk_body(n_patch, tok, cot, w_up, w_down, mixed_in, pre, mixed):
    total = chunk_work(n_patch, tok, cot, w_up, w_down, pre, mixed_in[...])
    mixed[...] = total.astype(mixed.dtype)


def split_part(part, keep, send):
    n_keep = keep.shape[0]
    keep[...] = part[:n_keep]
    send[...] = part[n_keep:].astype(bf16)


def first_grad_body(n_patch, tok_full, h0, h1, h2, h3, pre, pre_pair, pair, keep, send):
    n_rows = tok_full.shape[1]
    blk = h0.shape[0]
    weights = row_weights(n_patch, n_rows, pre, pre_pair)
    me = lax.axis_index("mdl")
    sel = lax.axis_index("sel")
    parity, high = lax.rem(sel, 2), lax.div(sel, 2)
    for j, piece in enumerate((h0, h1, h2, h3)):
        block = me ^ j
        apart = block ^ high
        rows = place(2 * lax.rem(apart, 2) + lax.div(apart, 2), blk)
        own_tok = tok_full[place(2 * block + parity, blk), :].astype(f32)
        pair[rows, 0:n_rows] = (own_tok * weights[0]).astype(bf16)
        pair_tok = piece[:, 0:n_rows].astype(f32)
        pair[rows, n_rows:] = (pair_tok * weights[1]).astype(bf16)
    grad_body(pair, pre, pre_pair, keep, send)


def grad_body(pair, pre, pre_pair, keep, send):
    n_rows = pair.shape[1] // 2
    part = dot_f32(pair[:, 0:n_rows], pre[0:n_rows, :])
    part = part + dot_f32(pair[:, n_rows:], pre_pair[0:n_rows, :])
    split_part(part, keep, send)


def add_body(held, received, keep, send):
    split_part(held[...] + received[...].astype(f32), keep, send)


def mix_body(a, b, total):
    total[...] = (a[...].astype(f32) + b[...].astype(f32)).astype(total.dtype)


def heads_body(n_patch, h0, h1, h2, h3, a, b, ref_proj, emb, pooled):
    me = lax.axis_index("mdl")
    n_rows = h0.shape[0]
    n_ex = pooled.shape[1]
    first = h0.shape[1] - 2 * n_ex
    for j, piece in enumerate((h0, h1, h2, h3)):
        for part in range(2):
            pooled[place((me ^ j) * 2 + part, n_rows), :] = piece[
                :, first + part * n_ex : first + (part + 1) * n_ex
            ]
    learn_pool = ((a[...].astype(f32) + b[...].astype(f32)) * (1.0 / n_patch)).astype(bf16)
    emb[0:n_ex, :] = dot_cols(pooled[...], ref_proj[...])
    emb[n_ex:, :] = dot_f32(learn_pool, ref_proj[...])


def own_score(hat, texts):
    return jnp.sum(hat.astype(f32) * texts.astype(f32), axis=1, keepdims=True)


def scores_body(e0, e1, e2, e3, share, kept, out, whole):
    me = lax.axis_index("mdl")
    sel = lax.axis_index("sel")
    width = e0.shape[1]
    for j, piece in enumerate((e0, e1, e2, e3)):
        whole[:, place(me ^ j, width)] = piece[...]
    values = whole[...]
    norm_sq = jnp.sum(values * values, axis=1, keepdims=True)
    hat = (values * lax.rsqrt(norm_sq + eps)).astype(bf16)
    k_dev = kept.shape[1]
    n_all = hat.shape[0]
    ex_dev = n_all - k_dev
    scores = dot_rows(share[...], hat)
    out[:, 0:n_all] = jnp.sum(jnp.exp(logit_scale * scores), axis=0, keepdims=True)
    own_text = share[place(lax.rem(sel, 2), ex_dev), :]
    holds = me == lax.div(sel, 2)
    pick = (lax.broadcasted_iota(jnp.int32, (ex_dev, k_dev), 0) == kept[...]).astype(bf16)
    kept_text = dot_cols(pick, own_text)
    learn_own = as_row(own_score(hat[ex_dev:], kept_text))
    image_own = as_row(own_score(hat[:ex_dev], own_text))
    out[:, n_all : n_all + k_dev] = jnp.where(holds, learn_own, 0.0)
    out[:, n_all + k_dev :] = jnp.where(holds, image_own, 0.0)


def losses_body(a, b, kept, ref_loss, learnability):
    sums = a[...] + b[...]
    k_dev, ex_dev = kept.shape[1], ref_loss.shape[1]
    n_all = ex_dev + k_dev
    losses = jnp.log(sums[:, 0:ex_dev]) - logit_scale * sums[:, n_all + k_dev :]
    ref_loss[...] = losses
    learner = jnp.log(sums[:, ex_dev:n_all]) - logit_scale * sums[:, n_all : n_all + k_dev]
    pick = lax.broadcasted_iota(jnp.int32, (ex_dev, k_dev), 0) == kept[...]
    picked = jnp.sum(jnp.where(pick, as_row_t(losses), 0.0), axis=0, keepdims=True)
    learnability[...] = learner - picked


def as_row_t(row):
    n = row.shape[1]
    return jnp.broadcast_to(row, (n, n)).T[:, 0:1]


def after(value, *others):
    return lax.optimization_barrier((value,) + others)[0] if others else value


def quarter_sel(patches, text, ref_proj, w_up, w_down, kept_index, dest, cotan):
    n_mdl, n_sel = lax.axis_size("mdl"), lax.axis_size("sel")
    n_high = n_sel // 2
    ex_dev, emb_part = text.shape
    emb_full = emb_part * n_mdl
    d_part = patches.shape[1]
    d_full = d_part * n_mdl
    n_patch = patches.shape[0] // ex_dev
    k_dev = kept_index.shape[0]
    n_rows = k_dev * n_patch
    ff_dev = w_up.shape[1]
    blk = d_full // n_sel
    n_share = ex_dev * n_sel // n_mdl
    n_emb = ex_dev + k_dev
    kept_row = kept_index.reshape(1, k_dev)
    dest_row = dest.reshape(1, k_dev)
    size = ff_dev // 4
    whole = lambda shape: pl.BlockSpec(shape, lambda i: (0,) * len(shape))
    row_struct = struct((n_rows, d_full), bf16)
    row_spec = whole((n_rows, d_full))
    mixed_struct = struct((k_dev, d_full), f32)
    mixed_spec = whole((k_dev, d_full))
    pre_struct = struct((n_rows, size), bf16)
    pre_spec = whole((n_rows, size))
    halves = (struct((2 * blk, size), f32), struct((2 * blk, size), bf16))

    def run(ties, body, out_shape, *operands, **kwargs):
        first = after(operands[0], *ties)
        return call(body, out_shape, (2**20, 2**20), **kwargs)(first, *operands[1:])

    def pick(ties):
        return run(
            ties,
            functools.partial(pick_body, n_patch),
            (
                struct((2 * d_part, n_rows), bf16),
                struct((d_part // 2, n_rows), bf16),
                struct((d_part, ex_dev), bf16),
                struct((ex_dev + 16, emb_part), bf16),
            ),
            patches.T,
            cotan.T,
            kept_row,
            dest_row,
            text,
            in_specs=[
                pl.BlockSpec(memory_space=space)
                for space in (pltpu.HBM, pltpu.HBM, pltpu.VMEM, pltpu.VMEM, pltpu.HBM)
            ],
            scratch_shapes=[
                pltpu.VMEM((d_part, ex_dev * n_patch), bf16),
                pltpu.SemaphoreType.DMA((3,)),
            ],
            vmem=60 * 2**20,
        )


    def stage(ties):
        return run(
            ties,
            stage_body,
            (struct(w_up.shape, bf16), struct(w_down.shape, bf16)),
            w_up,
            w_down,
            in_specs=[pl.BlockSpec(memory_space=pltpu.HBM)] * 2,
            scratch_shapes=[pltpu.SemaphoreType.DMA((2,))],
            vmem=40 * 2**20,
        )


    def make_extras(ties, half_pair, pool, texts):
        rotated = [rotate_pairs(texts, s) for s in range(1, n_high)]
        return run(
            ties,
            extras_body,
            (
                struct((d_part // 2, n_rows + 2 * ex_dev), bf16),
                struct((n_high * (ex_dev + 16), emb_part), bf16),
                struct((16, n_high * k_dev), bf16),
            ),
            half_pair,
            pool,
            texts,
            *rotated,
        )


    def weight_specs(c):
        return [
            pl.BlockSpec((d_full, size), lambda i: (0, c)),
            pl.BlockSpec((size, d_full), lambda i: (c, 0)),
        ]


    def forward_first(ties, *operands):
        return run(
            ties,
            functools.partial(first_chunk_body, n_patch, n_mdl),
            (
                struct((n_rows + 16, size), bf16),
                mixed_struct,
                struct((d_full, n_rows), bf16),
                row_struct,
                row_struct,
            ),
            *operands,
            grid=(1,),
            in_specs=[whole((16, n_high * k_dev))]
            + [whole((2 * d_part, n_rows))] * 4 + weight_specs(0),
            out_specs=[
                whole((n_rows + 16, size)),
                mixed_spec,
                whole((d_full, n_rows)),
                row_spec,
                row_spec,
            ],
            scratch_shapes=[pltpu.VMEM((d_full, n_rows), bf16)],
        )

    def forward(ties, c, tok, cot, held_up, held_down, mixed):
        last = c == ff_dev // size - 1
        return run(
            ties,
            functools.partial(next_chunk_body, n_patch),
            (pre_struct, struct((k_dev, d_full), bf16 if last else f32)),
            tok,
            cot,
            held_up,
            held_down,
            mixed,
            grid=(1,),
            in_specs=[row_spec, row_spec] + weight_specs(c) + [mixed_spec],
            out_specs=[pre_spec, mixed_spec],
        )


    def all_shards(ties, my_texts, pair_texts):
        return run(
            ties,
            text_body,
            (
                struct((ex_dev * n_sel, emb_part), bf16),
                struct((2 * n_share, emb_part), bf16),
            ),
            my_texts,
            pair_texts,
        )

    def grad_first(ties, *operands):
        pair_struct = struct((blk * n_high, 2 * n_rows), bf16)
        return run(ties, functools.partial(first_grad_body, n_patch), (pair_struct,) + halves, *operands)

    def grad(ties, *operands):
        return run(ties, grad_body, halves, *operands)

    def add(ties, keep, received):
        structs = (struct((blk, size), f32), struct((blk, size), bf16))
        return run(ties, add_body, structs, keep, received)

    def relay_text(ties, all_texts, text_x):
        send = struct((2 * n_share, emb_part), bf16)
        return run(ties, text_relay_body, send, all_texts, text_x)

    def share_text(ties, *operands):
        return run(
            ties,
            share_body,
            struct((n_share, emb_full), bf16),
            *operands,
            scratch_shapes=[pltpu.VMEM((n_share, emb_full), f32)],
        )

    def heads(ties, *operands):
        return run(
            ties,
            functools.partial(heads_body, n_patch),
            struct((n_emb, emb_part), f32),
            *operands,
            ref_proj,
            scratch_shapes=[pltpu.VMEM((d_full, ex_dev), bf16)],
        )

    def scores(ties, *operands):
        return run(
            ties,
            scores_body,
            struct((1, 2 * n_emb), f32),
            *operands,
            kept_row,
            scratch_shapes=[pltpu.VMEM((n_emb, emb_full), f32)],
        )

    def losses(ties, total, total_x):
        structs = (struct((1, ex_dev), f32), struct((1, k_dev), f32))
        return run(ties, losses_body, structs, total, total_x, kept_row)


    both, half, pool, texts = pick(())
    both_x = swap(both, "mdl", 2)
    both_core = swap(both, "mdl", 1)
    half_pair = swap(half, "sel", 1)
    held_up, held_down = stage((texts,))
    extras, my_texts, dests = make_extras((held_down,), half_pair, pool, texts)
    both_diag = swap(after(both_x, extras), "mdl", 1)
    extras_x = swap(extras, "mdl", 2)
    extras_core = swap(extras, "mdl", 1)
    extras_diag = swap(extras_x, "mdl", 1)
    pair_texts = swap(my_texts, "sel", 1)
    pre0, mixed0, tok_full, tok, cot = forward_first(
        (dests, extras_core),
        dests,
        both,
        both_core,
        both_x,
        both_diag,
        held_up,
        held_down,
    )
    pair_pre0 = swap(pre0, "sel", 1)
    pre1, mixed1 = forward((cot,), 1, tok, cot, held_up, held_down, mixed0)
    pair_pre1 = swap(pre1, "sel", 1)
    all_texts, text_send = all_shards((mixed1,), my_texts, pair_texts)
    text_x = swap(text_send, "mdl", 2)
    pre2, mixed2 = forward((text_send,), 2, tok, cot, held_up, held_down, mixed1)
    pair_pre2 = swap(pre2, "sel", 1)
    pre3, mixed = forward((mixed2,), 3, tok, cot, held_up, held_down, mixed2)
    pair_pre3 = swap(pre3, "sel", 1)
    mixed_core = swap(mixed, "mdl", 1)
    mixsum = run((mixed, extras_diag), mix_body, struct((k_dev, d_full), bf16), mixed, mixed_core)
    mixsum_x = swap(mixsum, "mdl", 2)
    relay = relay_text((mixsum,), all_texts, text_x)
    text_core = swap(relay, "mdl", 1)
    pair, keep0, send0 = grad_first(
        (relay,),
        tok_full,
        extras,
        extras_core,
        extras_x,
        extras_diag,
        pre0,
        pair_pre0,
    )
    first0 = swap(send0, "sel", 2)
    emb = heads((send0,), extras, extras_core, extras_x, extras_diag, mixsum, mixsum_x)
    emb_x = swap(emb, "mdl", 2)
    emb_core = swap(emb, "mdl", 1)
    emb_diag = swap(emb_x, "mdl", 1)
    keep1, send1 = grad((emb, text_x), pair, pre1, pair_pre1)
    first1 = swap(send1, "sel", 2)
    own0, rest0 = add((send1,), keep0, first0)
    second0 = swap(rest0, "sel", 4)
    keep2, send2 = grad((rest0,), pair, pre2, pair_pre2)
    first2 = swap(send2, "sel", 2)
    own1, rest1 = add((send2,), keep1, first1)
    second1 = swap(rest1, "sel", 4)
    share = share_text((rest1,), all_texts, text_x, text_core)
    keep3, send3 = grad((share, emb_diag), pair, pre3, pair_pre3)
    first3 = swap(send3, "sel", 2)
    own2, rest2 = add((send3,), keep2, first2)
    second2 = swap(rest2, "sel", 4)
    sums = scores((rest2,), emb, emb_core, emb_x, emb_diag, share)
    sums_core = swap(sums, "mdl", 1)
    total = run((sums,), mix_body, struct((1, 2 * n_emb), f32), sums, sums_core)
    total_x = swap(after(total, pair_texts), "mdl", 2)
    ref_loss, learnability = losses((total,), total, total_x)
    own3, rest3 = add((learnability,), keep3, first3)
    second3 = swap(rest3, "sel", 4)

    own3, ref_loss, learnability = lax.optimization_barrier((own3, ref_loss, learnability))
    sums = [
        (own0, second0),
        (own1, second1),
        (own2, second2),
        (own3, second3),
    ]
    grad_up = jnp.concatenate([own + other.astype(f32) for own, other in sums], axis=1)
    return (ref_loss.reshape(ex_dev), learnability.reshape(k_dev), grad_up)


def solution(mesh):
    in_specs = (
        P("sel", "mdl"),
        P("sel", "mdl"),
        P(None, "mdl"),
        P(None, "mdl"),
        P("mdl", None),
        P("sel"),
        P("sel"),
        P("sel", "mdl"),
    )
    out_specs = (P("sel"), P("sel"), P("sel", "mdl"))
    body = quarter_sel if (mesh.shape["sel"], mesh.shape["mdl"]) == (8, 4) else per_device
    return jax.shard_map(
        body, mesh=mesh, in_specs=in_specs, out_specs=out_specs, check_vma=False
    )
```

```python
import functools

import jax
import jax.numpy as jnp
from jax import lax
from jax.experimental import pallas as pl
from jax.experimental.pallas import tpu as pltpu
from jax.sharding import PartitionSpec as P

logit_scale = 64.0
eps = 1e-06
f32 = jnp.float32
bf16 = jnp.bfloat16


def gelu_parts(pre_act):
    cumul = 0.5 * (1.0 + lax.erf(pre_act * 0.7071067811865476))
    density = jnp.exp(-0.5 * pre_act * pre_act) * 0.3989422804014327
    return (pre_act * cumul, cumul + pre_act * density)


def swap(value, axis, bit):
    size = lax.axis_size(axis)
    return lax.ppermute(value, axis, [(i, i ^ bit) for i in range(size)])


def rotate_pairs(value, step):
    size = lax.axis_size("sel")
    return lax.ppermute(value, "sel", [(i, (i + 2 * step) % size) for i in range(size)])


def mdl_pieces(value):
    n = lax.axis_size("mdl")
    out = [value] + [None] * (n - 1)
    top = n // 2
    if n == 1:
        return out
    out[top] = swap(value, "mdl", top)
    low = top // 2
    have = [0, top]
    while low:
        for j in list(have):
            out[j | low] = swap(out[j], "mdl", low)
            have.append(j | low)
        low //= 2
    return out


def in_order(pieces, axis):
    me = lax.axis_index("mdl")
    bit = 1
    while bit < lax.axis_size("mdl"):
        set_bit = (me & bit) != 0
        merged = []
        for j in range(0, len(pieces), 2):
            first, second = pieces[j], pieces[j + 1]
            merged.append(
                jnp.where(
                    set_bit,
                    jnp.concatenate([second, first], axis),
                    jnp.concatenate([first, second], axis),
                )
            )
        pieces = merged
        bit *= 2
    return pieces[0]


def mdl_sum(value):
    bit = 1
    while bit < lax.axis_size("mdl"):
        value = value + swap(value, "mdl", bit)
        bit *= 2
    return value


def unit_rows(values):
    norm_sq = jnp.sum(values * values, axis=1)
    return (values * lax.rsqrt(norm_sq + eps)[:, None]).astype(bf16)


def exp_total(rows_full, texts):
    scores = lax.dot_general(
        rows_full, texts, (((1,), (1,)), ((), ())), preferred_element_type=f32
    )
    return jnp.sum(jnp.exp(logit_scale * scores), axis=1)


def own_product(rows, texts):
    return jnp.sum(rows.astype(f32) * texts.astype(f32), axis=1)


def per_device(patches, text, ref_proj, w_up, w_down, kept_index, dest, cotan):
    n_sel = lax.axis_size("sel")
    n_mdl = lax.axis_size("mdl")
    ex_dev = text.shape[0]
    d_part = patches.shape[1]
    n_patch = patches.shape[0] // ex_dev
    k_dev = kept_index.shape[0]
    n_rows = k_dev * n_patch
    ff_dev = w_up.shape[1]
    n_high = n_sel // 2
    rotations = n_high <= 4
    sel_me, mdl_me = lax.axis_index("sel"), lax.axis_index("mdl")
    pair_me, high_me = sel_me % 2, sel_me // 2

    patches_t = patches.T
    row_of = (kept_index[:, None] * n_patch + jnp.arange(n_patch)[None, :]).reshape(-1)
    pick = (jnp.arange(ex_dev * n_patch)[:, None] == row_of[None, :]).astype(bf16)
    tok_t = jnp.dot(patches_t, pick, preferred_element_type=f32).astype(bf16)
    cot_t = cotan.T
    blk = d_part * n_mdl // n_sel
    halves = tok_t.reshape(d_part // (2 * blk), 2, blk, n_rows)
    send_half = lax.dynamic_index_in_dim(halves, 1 - pair_me, 1, keepdims=False)
    recv_half = swap(send_half.reshape(d_part // 2, n_rows), "sel", 1)

    tok_full = in_order(mdl_pieces(tok_t), 0)
    cot_full = in_order(mdl_pieces(cot_t), 0)
    recv_half_full = in_order(mdl_pieces(recv_half), 0)
    n_blk = d_part * n_mdl // (2 * blk)
    own_half_full = lax.dynamic_index_in_dim(
        tok_full.reshape(n_blk, 2, blk, n_rows), pair_me, 1, keepdims=False
    ).reshape(n_blk * blk, n_rows)
    tok_pair = jnp.concatenate([own_half_full, recv_half_full], axis=1)

    counts = jnp.sum((dest[:, None] == jnp.arange(n_sel)[None, :]).astype(f32), axis=0)
    if rotations:
        pair_counts = counts + swap(counts, "sel", 1)
        counts = pair_counts
        for step in range(1, n_high):
            counts = counts + rotate_pairs(pair_counts, step)
    else:
        counts = lax.psum(counts, "sel")
    row_weight = 1.0 / jnp.repeat(counts[dest], n_patch)

    text_full = in_order(mdl_pieces(text), 1).astype(f32)
    text_hat = unit_rows(text_full)
    share = ex_dev // n_mdl
    text_share = lax.dynamic_slice_in_dim(text_hat, mdl_me * share, share, 0)
    if rotations:
        pair_share = jnp.concatenate([text_share, swap(text_share, "sel", 1)], axis=0)
        text_split = jnp.concatenate(
            [pair_share] + [rotate_pairs(pair_share, s) for s in range(1, n_high)], axis=0
        )
    else:
        text_split = lax.all_gather(text_share, "sel", axis=0, tiled=True)

    pooled_t = (
        jnp.sum(patches_t.reshape(d_part, ex_dev, n_patch).astype(f32), axis=2) * (1.0 / n_patch)
    ).astype(bf16)
    pooled_full = in_order(mdl_pieces(pooled_t), 0)
    img_emb = lax.dot_general(
        pooled_full, ref_proj, (((0,), (0,)), ((), ())), preferred_element_type=f32
    )
    img_hat = unit_rows(in_order(mdl_pieces(img_emb), 1))
    ref_own = own_product(img_hat, text_hat)
    ref_part = exp_total(img_hat, text_split)

    pre_act = lax.dot_general(
        tok_full, w_up, (((0,), (0,)), ((), ())), preferred_element_type=f32
    )
    activated, gelu_slope = gelu_parts(pre_act)
    hidden = activated.astype(bf16)
    mixed = jnp.dot(hidden, w_down, preferred_element_type=f32)
    mixed_pool = mdl_sum(jnp.sum(mixed.reshape(k_dev, n_patch, -1), axis=1))
    tok_pool = jnp.sum(tok_full.reshape(-1, k_dev, n_patch).astype(f32), axis=2).T
    learn_pool = ((mixed_pool + tok_pool) * (1.0 / n_patch)).astype(bf16)
    learn_emb = jnp.dot(learn_pool, ref_proj, preferred_element_type=f32)
    learn_hat = unit_rows(in_order(mdl_pieces(learn_emb), 1))
    kept_text = text_hat[kept_index]
    learn_own = own_product(learn_hat, kept_text)
    learn_part = exp_total(learn_hat, text_split)
    totals = mdl_sum(jnp.concatenate([ref_part, learn_part]))
    ref_loss = jnp.log(totals[:ex_dev]) - logit_scale * ref_own
    learner_loss = jnp.log(totals[ex_dev:]) - logit_scale * learn_own
    learnability = learner_loss - ref_loss[kept_index]

    n_chunks = 4
    width = ff_dev // n_chunks
    outs = []
    for c in range(n_chunks):
        cols = slice(c * width, (c + 1) * width)
        grad_act = lax.dot_general(
            cot_full, w_down[cols], (((0,), (1,)), ((), ())), preferred_element_type=f32
        )
        grad_pre = (grad_act * row_weight[:, None] * gelu_slope[:, cols]).astype(bf16)
        pair_pre = jnp.concatenate([grad_pre, swap(grad_pre, "sel", 1)], axis=0)
        part = jnp.dot(tok_pair, pair_pre, preferred_element_type=f32)
        part = part.reshape(n_high, blk, width)
        if rotations:
            total = lax.dynamic_index_in_dim(part, high_me, 0, keepdims=False)
            for step in range(1, n_high):
                block = lax.dynamic_index_in_dim(
                    part, (high_me + step) % n_high, 0, keepdims=False
                )
                total = total + rotate_pairs(block.astype(bf16), step).astype(f32)
        else:
            total = lax.psum_scatter(
                part,
                "sel",
                scatter_dimension=0,
                axis_index_groups=[list(range(p, n_sel, 2)) for p in range(2)],
                tiled=False,
            )
        outs.append(total)
    grad_up = jnp.concatenate(outs, axis=1)
    return (ref_loss, learnability, grad_up)


def dot_f32(a, b):
    return jnp.dot(a, b, preferred_element_type=f32)


def dot_rows(a, b):
    return lax.dot_general(a, b, (((1,), (1,)), ((), ())), preferred_element_type=f32)


def dot_cols(a, b):
    return lax.dot_general(a, b, (((0,), (0,)), ((), ())), preferred_element_type=f32)


def group_mask(n_items, n_patch):
    shape = (n_items, n_items * n_patch)
    row = lax.broadcasted_iota(jnp.int32, shape, 1)
    first = n_patch * lax.broadcasted_iota(jnp.int32, shape, 0)
    return (row >= first) & (row < first + n_patch), row - first


def as_row(column):
    n = column.shape[0]
    return jnp.broadcast_to(column, (n, n)).T[0:1]


def place(index, length):
    return pl.ds(pl.multiple_of(index * length, length), length)


def call(body, out_shape, cost, grid=(), vmem=24 * 2**20, **kwargs):
    flops, moved = cost
    return pl.pallas_call(
        body,
        out_shape=out_shape,
        grid=grid,
        cost_estimate=pl.CostEstimate(flops=1, bytes_accessed=1, transcendentals=0),
        compiler_params=pltpu.CompilerParams(vmem_limit_bytes=vmem),
        **kwargs,
    )


def struct(shape, dtype):
    return jax.ShapeDtypeStruct(shape, dtype)


def pick_body(
    n_patch, patches_hbm, cot_hbm, kept, dest, text_hbm, both, half, pool, texts, patches, sems
):
    d_part, n_all = patches.shape
    ex_dev = n_all // n_patch
    copies = [
        pltpu.make_async_copy(patches_hbm, patches, sems.at[0]),
        pltpu.make_async_copy(cot_hbm, both.at[pl.ds(d_part, d_part), :], sems.at[1]),
        pltpu.make_async_copy(text_hbm, texts.at[pl.ds(0, ex_dev), :], sems.at[2]),
    ]
    for copy in copies:
        copy.start()
    k_dev = kept.shape[1]
    member, offset = group_mask(k_dev, n_patch)
    expand = member.astype(bf16)
    index = jnp.broadcast_to(kept[...].astype(f32), (8, k_dev)).astype(bf16)
    base = dot_f32(index, expand)[0:1].astype(jnp.int32)
    row = base * n_patch + jnp.sum(jnp.where(member, offset, 0), axis=0, keepdims=True)
    pick = (lax.broadcasted_iota(jnp.int32, (n_all, row.shape[1]), 0) == row).astype(bf16)
    for copy in copies:
        copy.wait()
    values = patches[...]
    both[0:d_part, :] = dot_f32(values, pick).astype(bf16)
    other = 1 - lax.rem(lax.axis_index("sel"), 2)
    half[...] = both[place(other, d_part // 2), :]
    texts[ex_dev:, :] = jnp.zeros((16, texts.shape[1]), bf16)
    texts[ex_dev:, 0:k_dev] = jnp.broadcast_to(dest[...].astype(f32), (16, k_dev)).astype(bf16)
    groups, _ = group_mask(ex_dev, n_patch)
    pool[...] = (dot_rows(values, groups.astype(bf16)) * (1.0 / n_patch)).astype(bf16)


def extras_body(half, pool, t0, t1, t2, t3, extras, texts, dests):
    n_half, n_rows = half.shape
    n_ex = pool.shape[1]
    extras[:, 0:n_rows] = half[...]
    extras[:, n_rows : n_rows + n_ex] = pool[0:n_half, :]
    extras[:, n_rows + n_ex :] = pool[n_half:, :]
    n_text = t0.shape[0]
    for r, piece in enumerate((t0, t1, t2, t3)):
        texts[r * n_text : (r + 1) * n_text, :] = piece[...]
        k_dev = dests.shape[1] // 4
        dests[:, r * k_dev : (r + 1) * k_dev] = piece[n_text - 16 :, 0:k_dev]


def text_body(mine, theirs, whole, send):
    n_high = 4
    n_text = mine.shape[0] // n_high
    ex_dev = n_text - 16
    me = lax.axis_index("mdl")
    sel = lax.axis_index("sel")
    parity, high = lax.rem(sel, 2), lax.div(sel, 2)
    for which, place_in_pair in ((mine, parity), (theirs, 1 - parity)):
        for r in range(n_high):
            source = lax.rem(high + n_high - r, n_high)
            rows = place(source * 2 + place_in_pair, ex_dev)
            whole[rows, :] = which[r * n_text : r * n_text + ex_dev, :]
    for i in range(2):
        send[i * 2 * ex_dev : (i + 1) * 2 * ex_dev, :] = whole[place(me ^ (2 + i), 2 * ex_dev), :]


def row_weights(n_patch, n_rows, pre, pre_pair):
    k_dev = n_rows // n_patch
    shard = lax.broadcasted_iota(jnp.int32, (128, k_dev), 0).astype(f32)
    ones = jnp.ones((8, k_dev), bf16)
    counts = jnp.zeros((8, 128), f32)
    named = []
    for which in (pre, pre_pair):
        dests = which[n_rows:, :].astype(f32)
        for r in range(4):
            is_dest = (shard == dests[0:1, r * k_dev : (r + 1) * k_dev]).astype(bf16)
            counts = counts + dot_rows(ones, is_dest)
            if r == 0:
                named.append(is_dest)
    member = group_mask(k_dev, n_patch)[0].astype(bf16)
    weights = []
    for is_dest in named:
        count = dot_f32(counts.astype(bf16), is_dest).astype(bf16)
        weights.append(1.0 / dot_f32(count, member)[0:1])
    return weights


def text_relay_body(whole, received, send):
    n_share = received.shape[0] // 2
    send[0:n_share, :] = whole[place(lax.axis_index("mdl") ^ 1, n_share), :]
    send[n_share:, :] = received[n_share:, :]


def share_body(whole, from_x, from_core, share, values):
    n_share, width = share.shape[0], whole.shape[1]
    me = lax.axis_index("mdl")
    pieces = (
        whole[place(me, n_share), :],
        from_core[0:n_share, :],
        from_x[0:n_share, :],
        from_core[n_share:, :],
    )
    for j, piece in enumerate(pieces):
        values[:, place(me ^ j, width)] = piece.astype(f32)
    rows = values[...]
    norm_sq = jnp.sum(rows * rows, axis=1, keepdims=True)
    share[...] = (rows * lax.rsqrt(norm_sq + eps)).astype(bf16)


def stage_body(up, down, up_held, down_held, sems):
    copies = [
        pltpu.make_async_copy(up, up_held, sems.at[0]),
        pltpu.make_async_copy(down, down_held, sems.at[1]),
    ]
    for copy in copies:
        copy.start()
    for copy in copies:
        copy.wait()


def chunk_work(n_patch, first, tok, cot, w_up, w_down, pre, mixed):
    k_dev = tok.shape[0] // n_patch
    groups = group_mask(k_dev, n_patch)[0].astype(bf16)
    size = pre.shape[1]
    pre_act = dot_f32(tok[...], w_up[:, first : first + size])
    activated, gelu_slope = gelu_parts(pre_act)
    pre[0 : tok.shape[0], :] = (dot_rows(cot[...], w_down[first : first + size, :]) * gelu_slope).astype(bf16)
    pooled = dot_f32(groups, activated.astype(bf16))
    high = pooled.astype(bf16)
    low = (pooled - high.astype(f32)).astype(bf16)
    both = dot_f32(jnp.concatenate([high, low], axis=0), w_down[first : first + size, :])
    return mixed + (both[:k_dev] + both[k_dev:])


def first_chunk_body(
    n_patch, n_mdl, dests, b0, b1, b2, b3, w_up, w_down, pre, mixed, tok_full, tok, cot, cot_full
):
    d_part, n_rows = b0.shape[0] // 2, b0.shape[1]
    groups = group_mask(n_rows // n_patch, n_patch)[0].astype(bf16)
    me = lax.axis_index("mdl")
    for j, piece in enumerate((b0, b1, b2, b3)):
        tok_full[place(me ^ j, d_part), :] = piece[0:d_part, :]
        cot_full[place(me ^ j, d_part), :] = piece[d_part:, :]
    tok[...] = tok_full[...].T
    cot[...] = cot_full[...].T
    start = dot_f32(groups, tok[...]) * (1.0 / n_mdl)
    mixed[...] = chunk_work(n_patch, 0, tok, cot, w_up, w_down, pre, start)
    pre[n_rows:, :] = jnp.zeros((16, pre.shape[1]), bf16)
    pre[n_rows:, 0 : dests.shape[1]] = dests[...]


def next_chunk_body(n_patch, first, tok, cot, w_up, w_down, mixed_in, pre, mixed):
    total = chunk_work(n_patch, first, tok, cot, w_up, w_down, pre, mixed_in[...])
    mixed[...] = total.astype(mixed.dtype)


def split_part(part, keep, send):
    n_keep = keep.shape[0]
    keep[...] = part[:n_keep]
    send[...] = part[n_keep:].astype(bf16)


def first_grad_body(n_patch, tok_full, h0, h1, h2, h3, pre, pre_pair, pair, keep, send):
    n_rows = tok_full.shape[1]
    blk = h0.shape[0]
    weights = row_weights(n_patch, n_rows, pre, pre_pair)
    me = lax.axis_index("mdl")
    sel = lax.axis_index("sel")
    parity, high = lax.rem(sel, 2), lax.div(sel, 2)
    for j, piece in enumerate((h0, h1, h2, h3)):
        block = me ^ j
        apart = block ^ high
        rows = place(2 * lax.rem(apart, 2) + lax.div(apart, 2), blk)
        own_tok = tok_full[place(2 * block + parity, blk), :].astype(f32)
        pair[rows, 0:n_rows] = (own_tok * weights[0]).astype(bf16)
        pair_tok = piece[:, 0:n_rows].astype(f32)
        pair[rows, n_rows:] = (pair_tok * weights[1]).astype(bf16)
    grad_body(pair, pre, pre_pair, keep, send)


def grad_body(pair, pre, pre_pair, keep, send):
    n_rows = pair.shape[1] // 2
    part = dot_f32(pair[:, 0:n_rows], pre[0:n_rows, :])
    part = part + dot_f32(pair[:, n_rows:], pre_pair[0:n_rows, :])
    split_part(part, keep, send)


def add_body(held, received, keep, send):
    split_part(held[...] + received[...].astype(f32), keep, send)


def mix_body(a, b, total):
    total[...] = (a[...].astype(f32) + b[...].astype(f32)).astype(total.dtype)


def heads_body(n_patch, h0, h1, h2, h3, a, b, ref_proj, emb, pooled):
    me = lax.axis_index("mdl")
    n_rows = h0.shape[0]
    n_ex = pooled.shape[1]
    first = h0.shape[1] - 2 * n_ex
    for j, piece in enumerate((h0, h1, h2, h3)):
        for part in range(2):
            pooled[place((me ^ j) * 2 + part, n_rows), :] = piece[
                :, first + part * n_ex : first + (part + 1) * n_ex
            ]
    learn_pool = ((a[...].astype(f32) + b[...].astype(f32)) * (1.0 / n_patch)).astype(bf16)
    emb[0:n_ex, :] = dot_cols(pooled[...], ref_proj[...])
    emb[n_ex:, :] = dot_f32(learn_pool, ref_proj[...])


def own_score(hat, texts):
    return jnp.sum(hat.astype(f32) * texts.astype(f32), axis=1, keepdims=True)


def scores_body(e0, e1, e2, e3, share, kept, out, whole):
    me = lax.axis_index("mdl")
    sel = lax.axis_index("sel")
    width = e0.shape[1]
    for j, piece in enumerate((e0, e1, e2, e3)):
        whole[:, place(me ^ j, width)] = piece[...]
    values = whole[...]
    norm_sq = jnp.sum(values * values, axis=1, keepdims=True)
    hat = (values * lax.rsqrt(norm_sq + eps)).astype(bf16)
    k_dev = kept.shape[1]
    n_all = hat.shape[0]
    ex_dev = n_all - k_dev
    scores = dot_rows(share[...], hat)
    out[:, 0:n_all] = jnp.sum(jnp.exp(logit_scale * scores), axis=0, keepdims=True)
    own_text = share[place(lax.rem(sel, 2), ex_dev), :]
    holds = me == lax.div(sel, 2)
    pick = (lax.broadcasted_iota(jnp.int32, (ex_dev, k_dev), 0) == kept[...]).astype(bf16)
    kept_text = dot_cols(pick, own_text)
    learn_own = as_row(own_score(hat[ex_dev:], kept_text))
    image_own = as_row(own_score(hat[:ex_dev], own_text))
    out[:, n_all : n_all + k_dev] = jnp.where(holds, learn_own, 0.0)
    out[:, n_all + k_dev :] = jnp.where(holds, image_own, 0.0)


def losses_body(a, b, kept, ref_loss, learnability):
    sums = a[...] + b[...]
    k_dev, ex_dev = kept.shape[1], ref_loss.shape[1]
    n_all = ex_dev + k_dev
    losses = jnp.log(sums[:, 0:ex_dev]) - logit_scale * sums[:, n_all + k_dev :]
    ref_loss[...] = losses
    learner = jnp.log(sums[:, ex_dev:n_all]) - logit_scale * sums[:, n_all : n_all + k_dev]
    pick = lax.broadcasted_iota(jnp.int32, (ex_dev, k_dev), 0) == kept[...]
    picked = jnp.sum(jnp.where(pick, as_row_t(losses), 0.0), axis=0, keepdims=True)
    learnability[...] = learner - picked


def as_row_t(row):
    n = row.shape[1]
    return jnp.broadcast_to(row, (n, n)).T[:, 0:1]


def after(value, *others):
    return lax.optimization_barrier((value,) + others)[0] if others else value


def quarter_sel(patches, text, ref_proj, w_up, w_down, kept_index, dest, cotan):
    n_mdl, n_sel = lax.axis_size("mdl"), lax.axis_size("sel")
    n_high = n_sel // 2
    ex_dev, emb_part = text.shape
    emb_full = emb_part * n_mdl
    d_part = patches.shape[1]
    d_full = d_part * n_mdl
    n_patch = patches.shape[0] // ex_dev
    k_dev = kept_index.shape[0]
    n_rows = k_dev * n_patch
    ff_dev = w_up.shape[1]
    blk = d_full // n_sel
    n_share = ex_dev * n_sel // n_mdl
    n_emb = ex_dev + k_dev
    kept_row = kept_index.reshape(1, k_dev)
    dest_row = dest.reshape(1, k_dev)
    widths = (384, 384, 384, 384)
    starts = [sum(widths[:c]) for c in range(len(widths))]
    row_struct = struct((n_rows, d_full), bf16)
    mixed_struct = struct((k_dev, d_full), f32)

    def run(ties, body, out_shape, *operands, **kwargs):
        first = after(operands[0], *ties)
        return call(body, out_shape, (2**20, 2**20), **kwargs)(first, *operands[1:])

    def pick(ties):
        return run(
            ties,
            functools.partial(pick_body, n_patch),
            (
                struct((2 * d_part, n_rows), bf16),
                struct((d_part // 2, n_rows), bf16),
                struct((d_part, ex_dev), bf16),
                struct((ex_dev + 16, emb_part), bf16),
            ),
            patches.T,
            cotan.T,
            kept_row,
            dest_row,
            text,
            in_specs=[
                pl.BlockSpec(memory_space=space)
                for space in (pltpu.HBM, pltpu.HBM, pltpu.VMEM, pltpu.VMEM, pltpu.HBM)
            ],
            scratch_shapes=[
                pltpu.VMEM((d_part, ex_dev * n_patch), bf16),
                pltpu.SemaphoreType.DMA((3,)),
            ],
            vmem=60 * 2**20,
        )


    def stage(ties):
        return run(
            ties,
            stage_body,
            (struct(w_up.shape, bf16), struct(w_down.shape, bf16)),
            w_up,
            w_down,
            in_specs=[pl.BlockSpec(memory_space=pltpu.HBM)] * 2,
            scratch_shapes=[pltpu.SemaphoreType.DMA((2,))],
            vmem=40 * 2**20,
        )


    def make_extras(ties, half_pair, pool, texts):
        rotated = [rotate_pairs(texts, s) for s in range(1, n_high)]
        return run(
            ties,
            extras_body,
            (
                struct((d_part // 2, n_rows + 2 * ex_dev), bf16),
                struct((n_high * (ex_dev + 16), emb_part), bf16),
                struct((16, n_high * k_dev), bf16),
            ),
            half_pair,
            pool,
            texts,
            *rotated,
        )


    def forward_first(ties, *operands):
        return run(
            ties,
            functools.partial(first_chunk_body, n_patch, n_mdl),
            (
                struct((n_rows + 16, widths[0]), bf16),
                mixed_struct,
                struct((d_full, n_rows), bf16),
                row_struct,
                row_struct,
            ),
            *operands,
            scratch_shapes=[pltpu.VMEM((d_full, n_rows), bf16)],
        )

    def forward(ties, c, tok, cot, held_up, held_down, mixed):
        last = c == len(widths) - 1
        return run(
            ties,
            functools.partial(next_chunk_body, n_patch, starts[c]),
            (
                struct((n_rows, widths[c]), bf16),
                struct((k_dev, d_full), bf16 if last else f32),
            ),
            tok,
            cot,
            held_up,
            held_down,
            mixed,
        )


    def all_shards(ties, my_texts, pair_texts):
        return run(
            ties,
            text_body,
            (
                struct((ex_dev * n_sel, emb_part), bf16),
                struct((2 * n_share, emb_part), bf16),
            ),
            my_texts,
            pair_texts,
        )

    def halves(width):
        return (struct((2 * blk, width), f32), struct((2 * blk, width), bf16))

    def grad_first(ties, *operands):
        pair_struct = struct((blk * n_high, 2 * n_rows), bf16)
        return run(ties, functools.partial(first_grad_body, n_patch), (pair_struct,) + halves(widths[0]), *operands)

    def grad(ties, pair, pre, pair_pre):
        return run(ties, grad_body, halves(pre.shape[1]), pair, pre, pair_pre)

    def add(ties, keep, received):
        width = keep.shape[1]
        structs = (struct((blk, width), f32), struct((blk, width), bf16))
        return run(ties, add_body, structs, keep, received)

    def relay_text(ties, all_texts, text_x):
        send = struct((2 * n_share, emb_part), bf16)
        return run(ties, text_relay_body, send, all_texts, text_x)

    def share_text(ties, *operands):
        return run(
            ties,
            share_body,
            struct((n_share, emb_full), bf16),
            *operands,
            scratch_shapes=[pltpu.VMEM((n_share, emb_full), f32)],
        )

    def heads(ties, *operands):
        return run(
            ties,
            functools.partial(heads_body, n_patch),
            struct((n_emb, emb_part), f32),
            *operands,
            ref_proj,
            scratch_shapes=[pltpu.VMEM((d_full, ex_dev), bf16)],
        )

    def scores(ties, *operands):
        return run(
            ties,
            scores_body,
            struct((1, 2 * n_emb), f32),
            *operands,
            kept_row,
            scratch_shapes=[pltpu.VMEM((n_emb, emb_full), f32)],
        )

    def losses(ties, total, total_x):
        structs = (struct((1, ex_dev), f32), struct((1, k_dev), f32))
        return run(ties, losses_body, structs, total, total_x, kept_row)


    both, half, pool, texts = pick(())
    both_x = swap(both, "mdl", 2)
    both_core = swap(both, "mdl", 1)
    half_pair = swap(half, "sel", 1)
    held_up, held_down = stage((texts,))
    extras, my_texts, dests = make_extras((held_down,), half_pair, pool, texts)
    both_diag = swap(after(both_x, extras), "mdl", 1)
    extras_x = swap(extras, "mdl", 2)
    extras_core = swap(extras, "mdl", 1)
    extras_diag = swap(extras_x, "mdl", 1)
    pair_texts = swap(my_texts, "sel", 1)
    pre0, mixed0, tok_full, tok, cot = forward_first(
        (dests, extras_core),
        dests,
        both,
        both_core,
        both_x,
        both_diag,
        held_up,
        held_down,
    )
    pair_pre0 = swap(pre0, "sel", 1)
    pre1, mixed1 = forward((cot,), 1, tok, cot, held_up, held_down, mixed0)
    pair_pre1 = swap(pre1, "sel", 1)
    all_texts, text_send = all_shards((mixed1,), my_texts, pair_texts)
    text_x = swap(text_send, "mdl", 2)
    pre2, mixed2 = forward((text_send,), 2, tok, cot, held_up, held_down, mixed1)
    pair_pre2 = swap(pre2, "sel", 1)
    pre3, mixed = forward((mixed2,), 3, tok, cot, held_up, held_down, mixed2)
    pair_pre3 = swap(pre3, "sel", 1)
    mixed_core = swap(mixed, "mdl", 1)
    mixsum = run((mixed, extras_diag), mix_body, struct((k_dev, d_full), bf16), mixed, mixed_core)
    mixsum_x = swap(mixsum, "mdl", 2)
    relay = relay_text((mixsum,), all_texts, text_x)
    text_core = swap(relay, "mdl", 1)
    pair, keep0, send0 = grad_first(
        (relay,),
        tok_full,
        extras,
        extras_core,
        extras_x,
        extras_diag,
        pre0,
        pair_pre0,
    )
    first0 = swap(send0, "sel", 2)
    emb = heads((send0,), extras, extras_core, extras_x, extras_diag, mixsum, mixsum_x)
    emb_x = swap(emb, "mdl", 2)
    emb_core = swap(emb, "mdl", 1)
    emb_diag = swap(emb_x, "mdl", 1)
    keep1, send1 = grad((emb, text_x), pair, pre1, pair_pre1)
    first1 = swap(send1, "sel", 2)
    own0, rest0 = add((send1,), keep0, first0)
    second0 = swap(rest0, "sel", 4)
    keep2, send2 = grad((rest0,), pair, pre2, pair_pre2)
    first2 = swap(send2, "sel", 2)
    own1, rest1 = add((send2,), keep1, first1)
    second1 = swap(rest1, "sel", 4)
    share = share_text((rest1,), all_texts, text_x, text_core)
    keep3, send3 = grad((share, emb_diag), pair, pre3, pair_pre3)
    first3 = swap(send3, "sel", 2)
    own2, rest2 = add((send3,), keep2, first2)
    second2 = swap(rest2, "sel", 4)
    sums = scores((rest2,), emb, emb_core, emb_x, emb_diag, share)
    sums_core = swap(sums, "mdl", 1)
    total = run((sums,), mix_body, struct((1, 2 * n_emb), f32), sums, sums_core)
    total_x = swap(after(total, pair_texts), "mdl", 2)
    ref_loss, learnability = losses((total,), total, total_x)
    own3, rest3 = add((learnability,), keep3, first3)
    second3 = swap(rest3, "sel", 4)

    own3, ref_loss, learnability = lax.optimization_barrier((own3, ref_loss, learnability))
    sums = [
        (own0, second0),
        (own1, second1),
        (own2, second2),
        (own3, second3),
    ]
    grad_up = jnp.concatenate([own + other.astype(f32) for own, other in sums], axis=1)
    return (ref_loss.reshape(ex_dev), learnability.reshape(k_dev), grad_up)


def solution(mesh):
    in_specs = (
        P("sel", "mdl"),
        P("sel", "mdl"),
        P(None, "mdl"),
        P(None, "mdl"),
        P("mdl", None),
        P("sel"),
        P("sel"),
        P("sel", "mdl"),
    )
    out_specs = (P("sel"), P("sel"), P("sel", "mdl"))
    body = quarter_sel if (mesh.shape["sel"], mesh.shape["mdl"]) == (8, 4) else per_device
    return jax.shard_map(
        body, mesh=mesh, in_specs=in_specs, out_specs=out_specs, check_vma=False
    )
```
